32 devices in a mesh: vec: 8 (over y, x, core), cent: 4 (over z).
Axes of the slice: x: 2, y: 2, z: 4, core: 2. Of those that a mesh axis runs over, the one named last changes fastest.
Arguments:
- weights: bfloat16 [16384, 256], P('vec'), may hold values from -44 to 44
- centroids: bfloat16 [8192, 256], P('cent'), may hold values from -4 to 4
- cotangent: bfloat16 [16384, 256], P('vec'), may hold values from -6 to 6
Outputs:
- grad_weights: bfloat16 [16384, 256], P('vec')
- grad_centroids: float32 [8192, 256], P('cent')
The draws below stay inside these ranges and needn't reach their ends.
All inputs are finite; a program needn't handle non-finite values.
Results may differ from the reference program's by a relative error of at most 0.02.
The reference program's roundings to bfloat16 on the way count: a program that leaves them out, or rounds other values in their place, can miss the bound.
Values may be sent and summed in bfloat16 or wider, within the bound.
No kernel may reach another device: no remote copies, remote signals or barrier semaphores. Data moves between devices by JAX's collectives and lax.ppermute only.
A program may use at most 128 MiB of HBM per device.

```python
import jax
import jax.numpy as jnp
from jax import lax

D = 256
K = 8192
V_DEV = 2048
VECTORS = 16384


def draw_pair(key):
    keys = jax.random.split(jax.random.fold_in(key, 7), 2)
    cent = jnp.clip(jax.random.normal(keys[0], (K, D), jnp.float32), -4.0, 4.0)
    vecs = jnp.clip(jax.random.normal(keys[1], (VECTORS, D), jnp.float32), -4.0, 4.0)
    return (vecs, cent)


def draw_weights(key, part):
    vecs, cent = draw_pair(key)
    return vecs.astype(jnp.bfloat16)


def draw_centroids(key, part):
    vecs, cent = draw_pair(key)
    return cent.astype(jnp.bfloat16)


def steps_of(stream_key, shape, shards, smallest, high):
    def one(position, shards_of):
        steps = jax.random.uniform(jax.random.fold_in(jax.random.fold_in(stream_key, 6), position), (shards_of,), jnp.float32, smallest / len(shards), high / len(shards))
        return jnp.repeat(jnp.exp(steps), shape[position] // shards_of).reshape((-1,) + (1,) * (len(shape) - position - 1))

    gain = one(*shards[0])
    for cut in shards[1:]:
        gain = gain * one(*cut)
    return gain


def scatter_about(rng, dims, scale, limit, shards=(), dtype=jnp.bfloat16):
    values = scale * jax.random.normal(rng, dims, jnp.float32)
    if shards:
        values = values * steps_of(rng, dims, shards, -0.22, 0.18)
    return jnp.clip(values, -limit, limit).astype(dtype)


def setup_inputs(seed: int = 0) -> dict:
    key_list = jax.random.split(jax.random.key(seed), 4)
    return {
        "weights": draw_weights(jax.random.fold_in(key_list[3], 71), 0),
        "centroids": draw_centroids(jax.random.fold_in(key_list[3], 71), 0),
        "cotangent": scatter_about(key_list[2], (VECTORS, D), 1.0, 6.0, ((0, 8),)),
    }


def logits(rows, cent):
    cross = jnp.dot(rows, cent.T, preferred_element_type=jnp.float32)
    square = jnp.sum(jnp.square(cent.astype(jnp.float32)), axis=1)
    return (2.0 * cross - square[None, :]) * (D ** -0.5)


def soften(score):
    top = jnp.max(score, axis=1, keepdims=True)
    expo = jnp.exp(score - top)
    return expo / jnp.sum(expo, axis=1, keepdims=True)


def reference(weights, centroids, cotangent):
    blocks = weights.shape[0] // V_DEV
    wblock = weights.reshape(blocks, V_DEV, D)
    gblock = cotangent.reshape(blocks, V_DEV, D)
    scale = 2.0 * D ** -0.5

    def first_pass(carry, rows):
        mass, count = carry
        resp = soften(logits(rows, centroids))
        mass = mass + jnp.dot(resp.astype(jnp.bfloat16).T, rows, preferred_element_type=jnp.float32)
        count = count + jnp.sum(resp, axis=0)
        return (mass, count), None

    init = (jnp.zeros((K, D), jnp.float32), jnp.zeros((K,), jnp.float32))
    (mass, count), _ = lax.scan(first_pass, init, wblock)
    denom = count + 1e-6
    moved = (mass / denom[:, None]).astype(jnp.bfloat16)
    moved_f = moved.astype(jnp.float32)

    def second_pass(carry, pair):
        rows, cot = pair
        resp = soften(logits(rows, moved))
        dresp = jnp.dot(cot, moved.T, preferred_element_type=jnp.float32)
        dots = jnp.sum(resp * dresp, axis=1, keepdims=True)
        edge = resp * (dresp - dots) * scale
        edge_b = edge.astype(jnp.bfloat16)
        part = jnp.dot(edge_b, moved, preferred_element_type=jnp.float32)
        carry = carry + jnp.dot(resp.astype(jnp.bfloat16).T, cot, preferred_element_type=jnp.float32)
        carry = carry + jnp.dot(edge_b.T, rows, preferred_element_type=jnp.float32)
        carry = carry - jnp.sum(edge, axis=0)[:, None] * moved_f
        return carry, part

    moved_cot, part_two = lax.scan(second_pass, jnp.zeros((K, D), jnp.float32), (wblock, gblock))
    mean_cot = (moved_cot / denom[:, None]).astype(jnp.bfloat16)
    count_cot = -jnp.sum(mean_cot.astype(jnp.float32) * moved_f, axis=1)
    cent_f = centroids.astype(jnp.float32)

    def third_pass(carry, pair):
        rows, part = pair
        resp = soften(logits(rows, centroids))
        dresp = jnp.dot(rows, mean_cot.T, preferred_element_type=jnp.float32) + count_cot[None, :]
        dots = jnp.sum(resp * dresp, axis=1, keepdims=True)
        edge = resp * (dresp - dots) * scale
        edge_b = edge.astype(jnp.bfloat16)
        total = part + jnp.dot(resp.astype(jnp.bfloat16), mean_cot, preferred_element_type=jnp.float32)
        total = total + jnp.dot(edge_b, centroids, preferred_element_type=jnp.float32)
        carry = carry + jnp.dot(edge_b.T, rows, preferred_element_type=jnp.float32)
        carry = carry - jnp.sum(edge, axis=0)[:, None] * cent_f
        return carry, total.astype(jnp.bfloat16)

    start_cot, grad_rows = lax.scan(third_pass, jnp.zeros((K, D), jnp.float32), (wblock, part_two))
    return grad_rows.reshape(blocks * V_DEV, D), start_cot
```

```python
import jax
import jax.numpy as jnp
from jax import lax
from jax.experimental import pallas as pl
from jax.experimental.pallas import tpu as pltpu
from jax.sharding import PartitionSpec as P

F32 = jnp.float32
BF16 = jnp.bfloat16
STEP = 512


def vmem():
    return pl.BlockSpec(memory_space=pltpu.VMEM)


def smem():
    return pl.BlockSpec(memory_space=pltpu.SMEM)


def call(kernel, outs, args, scratch=(), flops=0, specs=None):
    return pl.pallas_call(
        kernel,
        in_specs=specs or [vmem()] * len(args),
        out_specs=jax.tree.map(lambda _: vmem(), outs),
        out_shape=outs,
        scratch_shapes=list(scratch),
        cost_estimate=pl.CostEstimate(flops=flops, bytes_accessed=2**22, transcendentals=0),
        compiler_params=pltpu.CompilerParams(vmem_limit_bytes=56 * 2**20),
    )(*args)


def shape(*dims, dtype=F32):
    return jax.ShapeDtypeStruct(dims, dtype)


def dot_nt(a, b):
    return lax.dot_general(a, b, (((1,), (1,)), ((), ())), preferred_element_type=F32)


def dot(a, b):
    return jnp.dot(a, b, preferred_element_type=F32)


def cut(total, step=STEP):
    step = min(step, total)
    return [slice(at, at + step) for at in range(0, total, step)]


def tiles(refs):
    start = 0
    for ref in refs:
        for rows in cut(ref.shape[0]):
            yield ref, rows, slice(start + rows.start, start + rows.stop)
        start += ref.shape[0]


def factor(block):
    scale = block.shape[1] ** (-0.5)
    block_f = block.astype(F32)
    square = jnp.sum(jnp.square(block_f), axis=1, keepdims=True) * scale
    return (block_f * (2.0 * scale)).astype(BF16), square


def put_rows(x, out, at):
    out[at : at + 1, 0 : x.shape[0]] = jnp.sum(x.T, axis=0, keepdims=True)


def lanes(x):
    total = x[:, 0:128]
    for at in range(128, x.shape[1], 128):
        total = total + x[:, at : at + 128]
    return total


def merge(stats):
    top = stats[0][0:1, :]
    for part in stats[1:]:
        top = jnp.maximum(top, part[0:1, :])
    weights = [jnp.exp(part[0:1, :] - top) for part in stats]
    total = sum(w * part[1:2, :] for w, part in zip(weights, stats))
    return top, total, weights


def online(out, top, sums, load):
    top[...] = jnp.full(top.shape, -jnp.inf, F32)
    sums[...] = jnp.zeros(sums.shape, F32)
    for score, cols, weight in load:
        score = score.reshape(score.shape[0] // 8, 8, score.shape[1])
        old = top[:, cols]
        new = jnp.maximum(old, jnp.max(score, axis=0))
        drop = jnp.exp(old - new)
        expo = jnp.exp(score - new[None])
        sums[0, :, cols] = sums[0, :, cols] * drop + jnp.sum(expo, axis=0)
        if weight is not None:
            expo = expo * weight.reshape(expo.shape)
            sums[1, :, cols] = sums[1, :, cols] * drop + jnp.sum(expo, axis=0)
        top[:, cols] = new
    peak = jnp.max(top[...], axis=0, keepdims=True)
    scale = jnp.exp(top[...] - peak)
    out[0:1, :] = peak
    for at in range(sums.shape[0]):
        out[at + 1 : at + 2, :] = jnp.sum(sums[at] * scale, axis=0, keepdims=True)


def first_stats(order, block, ids, cent, rows, out, cent_rel, top, sums):
    for at, mask in enumerate(order):
        owner = jnp.bitwise_xor(ids[0], mask)
        cent_rel[at * block : (at + 1) * block, :] = cent[pl.ds(pl.multiple_of(owner * block, block), block), :]

    def load():
        for rows_k in cut(cent_rel.shape[0]):
            lhs, square = factor(cent_rel[rows_k, :])
            for cols in cut(rows.shape[0]):
                yield dot_nt(lhs, rows[cols, :]) - square, cols, None

    online(out, top, sums, load())


def first_sums(half, block, parts, stats, cent, rows, out, lse, expo_b):
    peak, total, _ = merge(stats)
    lse[...] = peak + jnp.log(total)
    size = out.shape[0] * block
    per = max(1, min(STEP, size) // block)
    for at in range(0, out.shape[0], per):
        start = half * size + at * block
        lhs, square = factor(cent[start : start + per * block, :])
        count = jnp.zeros((per * block, 128), F32)
        for cols in cut(rows.shape[0]):
            expo = jnp.exp(dot_nt(lhs, rows[cols, :]) - square - lse[:, cols])
            count = count + lanes(expo)
            expo_b[:, cols] = expo.astype(BF16)
        mass = dot(expo_b[...], rows[...])
        for r in range(per):
            part = slice(r * block, (r + 1) * block)
            out[at + r, 0:block, :] = mass[part, :]
            out[at + r, block:, :] = jnp.zeros((out.shape[1] - block, out.shape[2]), F32)
            out[at + r, block : block + 1, 0:block] = jnp.sum(count[part, :].T, axis=0, keepdims=True)


def second_stats(moved, rows, cot, out, top, sums):
    def load():
        for ref, rows_k, _ in tiles(moved):
            block = ref[rows_k, :]
            lhs, square = factor(block)
            for cols in cut(rows.shape[0]):
                yield dot_nt(lhs, rows[cols, :]) - square, cols, dot_nt(block, cot[cols, :])

    online(out, top, sums, load())


def second_rows(stats, lse, dots):
    peak, total, weights = merge(stats)
    lse[...] = peak + jnp.log(total)
    dots[...] = sum(w * part[2:3, :] for w, part in zip(weights, stats)) / total


def second_sums(stats, moved, rows, cot, out, lse, dots, expo_b, edge_b):
    second_rows(stats, lse, dots)
    scale = 2.0 * rows.shape[1] ** (-0.5)
    for ref, rows_k, whole in tiles(moved):
        block = ref[rows_k, :]
        lhs, square = factor(block)
        edges = jnp.zeros((block.shape[0], 128), F32)
        for cols in cut(rows.shape[0]):
            expo = jnp.exp(dot_nt(lhs, rows[cols, :]) - square - lse[:, cols])
            expo_b[:, cols] = expo.astype(BF16)
            edge = expo * (dot_nt(block, cot[cols, :]) - dots[:, cols]) * scale
            edges = edges + lanes(edge)
            edge_b[:, cols] = edge.astype(BF16)
        total = dot(expo_b[...], cot[...]) + dot(edge_b[...], rows[...])
        total = total - jnp.sum(edges, axis=1, keepdims=True) * block.astype(F32)
        out[whole, :] = total.astype(out.dtype)


def second_part(stats, moved, rows, cot, out, lse, dots, edge_b):
    second_rows(stats, lse, dots)
    scale = 2.0 * rows.shape[1] ** (-0.5)
    for ref, rows_k, whole in tiles(moved):
        block = ref[rows_k, :]
        lhs, square = factor(block)
        for cols in cut(rows.shape[0]):
            expo = jnp.exp(dot_nt(lhs, rows[cols, :]) - square - lse[:, cols])
            edge = expo * (dot_nt(block, cot[cols, :]) - dots[:, cols]) * scale
            edge_b[whole, cols] = edge.astype(BF16)
    for cols in cut(rows.shape[0]):
        out[:, cols] = sum(
            dot(ref[...].T, edge_b[at : at + ref.shape[0], cols])
            for ref, at in zip(moved, (0, moved[0].shape[0]))
        )


def third_terms(cent, moved, mean_cot, rows, lse, moved_at, whole, mean):
    lhs, square = factor(cent[whole, :])
    ref, rows_k = moved_at
    count_cot = -jnp.sum(mean.astype(F32) * ref[rows_k, :].astype(F32), axis=1, keepdims=True)
    for cols in cut(rows.shape[0]):
        expo = jnp.exp(dot_nt(lhs, rows[cols, :]) - square - lse[:, cols])
        yield cols, expo, dot_nt(mean, rows[cols, :]) + count_cot


def third_stats(cent, moved, mean_cot, rows, lse, out, sums):
    sums[...] = jnp.zeros(sums.shape, F32)
    for (mean_ref, rows_k, whole), (moved_ref, _, _) in zip(tiles(mean_cot), tiles(moved)):
        mean = mean_ref[rows_k, :]
        for cols, expo, dfirst in third_terms(cent, moved, mean_cot, rows, lse, (moved_ref, rows_k), whole, mean):
            term = (expo * dfirst).reshape(expo.shape[0] // 8, 8, expo.shape[1])
            sums[:, cols] = sums[:, cols] + jnp.sum(term, axis=0)
    out[...] = jnp.sum(sums[...], axis=0, keepdims=True)


def third_rows(ids, dots_parts, cent, moved, mean_cot, rows, lse, part, outs, dots, expo_b, edge_b, total):
    dots[...] = sum(ref[...] for ref in dots_parts)
    scale = 2.0 * rows.shape[1] ** (-0.5)
    for (mean_ref, rows_k, whole), (moved_ref, _, _) in zip(tiles(mean_cot), tiles(moved)):
        mean = mean_ref[rows_k, :]
        for cols, expo, dfirst in third_terms(cent, moved, mean_cot, rows, lse, (moved_ref, rows_k), whole, mean):
            expo_b[whole, cols] = expo.astype(BF16)
            edge_b[whole, cols] = (expo * (dfirst - dots[:, cols]) * scale).astype(BF16)
    cent_t = cent[...].T
    halves = [(ref[...].T, at) for ref, at in zip(mean_cot, (0, mean_cot[0].shape[0]))]
    for cols in cut(rows.shape[0]):
        value = part[:, cols] + dot(cent_t, edge_b[:, cols])
        for mean_t, at in halves:
            value = value + dot(mean_t, expo_b[at : at + mean_t.shape[1], cols])
        total[cols, :] = value.T
    size = rows.shape[0] // len(outs)
    for r, out in enumerate(outs):
        at = jnp.bitwise_xor(ids[1], r) * size
        out[...] = total[pl.ds(pl.multiple_of(at, size), size), :].astype(out.dtype)


def third_sums(dots_parts, cent, moved, mean_cot, rows, lse, out, dots, edge_b):
    dots[...] = sum(ref[...] for ref in dots_parts)
    scale = 2.0 * rows.shape[1] ** (-0.5)
    for (mean_ref, rows_k, whole), (moved_ref, _, _) in zip(tiles(mean_cot), tiles(moved)):
        mean = mean_ref[rows_k, :]
        edges = jnp.zeros((mean.shape[0], 128), F32)
        for cols, expo, dfirst in third_terms(cent, moved, mean_cot, rows, lse, (moved_ref, rows_k), whole, mean):
            edge = expo * (dfirst - dots[:, cols]) * scale
            edges = edges + lanes(edge)
            edge_b[:, cols] = edge.astype(BF16)
        value = dot(edge_b[...], rows[...])
        value = value - jnp.sum(edges, axis=1, keepdims=True) * cent[whole, :].astype(F32)
        out[whole, :] = value.astype(out.dtype)


def place_blocks(order, axis, ids, parts, out):
    at = 0
    for part in parts:
        block = out.shape[0] // len(order)
        for start in range(0, part.shape[0], block):
            owner = jnp.bitwise_xor(ids[axis], order[at])
            out[pl.ds(pl.multiple_of(owner * block, block), block), :] = part[start : start + block, :].astype(out.dtype)
            at += 1


def swap(x, axis, n, mask):
    return lax.ppermute(x, axis, [(i, i ^ mask) for i in range(n)])


def make_local(nv, nc):
    nq = nv // 2
    order = [2 * r + a for a in range(2) for r in range(nq)]

    def local(weights, centroids, cotangent):
        V, D = weights.shape
        K = centroids.shape[0]
        block, half = K // nv, K // 2
        step = min(STEP, half)
        ids = jnp.stack([lax.axis_index("vec"), lax.axis_index("cent")]).astype(jnp.int32)
        unit = 2 * K * V * D
        row = pltpu.VMEM((1, V), F32)
        strip = pltpu.VMEM((step, V), BF16)
        sheet = pltpu.VMEM((K, V), BF16)

        def spread(x):
            return [x] + [swap(x, "cent", nc, r) for r in range(1, nc)]

        def collect(keep, send):
            chunks = keep.astype(F32) + swap(send, "vec", nv, 1).astype(F32)
            kind = keep.dtype
            parts = [chunks[0]]
            for r in range(1, nq):
                parts.append(swap(chunks[r].astype(kind), "vec", nv, 2 * r).astype(F32))
            return sum(parts)

        def share(x):
            mine = jnp.concatenate([x] + [swap(x, "vec", nv, 2 * r) for r in range(1, nq)])
            return [mine, swap(mine, "vec", nv, 1)]

        def split(fn, *counts):
            def kernel(*refs):
                groups, at = [], 0
                for count in counts:
                    groups.append(refs[at] if count == 0 else list(refs[at : at + count]))
                    at += max(count, 1)
                fn(*groups, *refs[at:])
            return kernel

        stats, cent = call(
            lambda *refs: first_stats(order, block, *refs),
            (shape(2, V), shape(K, D, dtype=BF16)),
            (ids, centroids, weights),
            [pltpu.VMEM((8, V), F32), pltpu.VMEM((1, 8, V), F32)],
            unit,
            [smem(), vmem(), vmem()],
        )
        stats = spread(stats)

        def sums(at):
            return call(
                split(lambda *refs: first_sums(at, block, nc, *refs), nc, 0, 0, 0, 0),
                (shape(nq, block + 8, D), shape(1, V)),
                (*stats, cent, weights),
                [strip],
                unit,
            )

        send, _ = sums(1)
        keep, lse = sums(0)
        chunk = collect(keep, send)
        denom = chunk[block, :block] + 1e-6
        moved = share((chunk[:block] / denom[:, None]).astype(BF16))

        stats = spread(call(
            split(second_stats, 2),
            shape(3, V),
            (*moved, weights, cotangent),
            [pltpu.VMEM((8, V), F32), pltpu.VMEM((2, 8, V), F32)],
            2 * unit,
        ))
        moved_cot = call(
            split(second_sums, nc, 2),
            shape(K, D, dtype=BF16),
            (*stats, *moved, weights, cotangent),
            [row, row, strip, strip],
            4 * unit,
        ).reshape(2, nq, block, D)
        part = call(
            split(second_part, nc, 2),
            shape(D, V),
            (*stats, *moved, weights, cotangent),
            [row, row, sheet],
            3 * unit,
        )
        mean_cot = share((collect(moved_cot[0], moved_cot[1]) / denom[:, None]).astype(BF16))

        dots = spread(call(
            split(third_stats, 0, 2, 2),
            shape(1, V),
            (cent, *moved, *mean_cot, weights, lse),
            [pltpu.VMEM((8, V), F32)],
            2 * unit,
        ))
        grad_rows = call(
            split(third_rows, 0, nc, 0, 2, 2, 0, 0, 0, nc),
            [shape(V // nc, D, dtype=BF16)] * nc,
            (ids, *dots, cent, *moved, *mean_cot, weights, lse, part),
            [row, sheet, sheet, pltpu.VMEM((V, D), F32)],
            4 * unit,
            [smem()] + [vmem()] * (nc + 8),
        )
        start_cot = call(
            split(third_sums, nc, 0, 2, 2),
            shape(K, D, dtype=BF16),
            (*dots, cent, *moved, *mean_cot, weights, lse),
            [row, strip],
            3 * unit,
        ).reshape(2, nq, block, D)

        rows = sum(x.astype(F32) for x in [grad_rows[0]] + [swap(grad_rows[r], "cent", nc, r) for r in range(1, nc)])
        rows = spread(rows.astype(BF16))
        start_cot = share(collect(start_cot[0], start_cot[1]).astype(BF16))
        grad_rows = call(
            split(lambda *refs: place_blocks(list(range(nc)), 1, *refs), 0, nc),
            shape(V, D, dtype=BF16),
            (ids, *rows),
            specs=[smem()] + [vmem()] * nc,
        )
        start_cot = call(
            split(lambda *refs: place_blocks(order, 0, *refs), 0, 2),
            shape(K, D),
            (ids, *start_cot),
            specs=[smem()] + [vmem()] * 2,
        )
        return grad_rows, start_cot

    return local


def solution(mesh):
    return jax.shard_map(
        make_local(mesh.shape["vec"], mesh.shape["cent"]),
        mesh=mesh,
        in_specs=(P("vec", None), P("cent", None), P("vec", None)),
        out_specs=(P("vec", None), P("cent", None)),
        check_vma=False,
    )
```

```python
import jax
import jax.numpy as jnp
from jax import lax
from jax.experimental import pallas as pl
from jax.experimental.pallas import tpu as pltpu
from jax.sharding import PartitionSpec as P

F32 = jnp.float32
BF16 = jnp.bfloat16
STEP = 512


def vmem():
    return pl.BlockSpec(memory_space=pltpu.VMEM)


def smem():
    return pl.BlockSpec(memory_space=pltpu.SMEM)


def call(kernel, outs, args, scratch=(), flops=0, specs=None):
    return pl.pallas_call(
        kernel,
        in_specs=specs or [vmem()] * len(args),
        out_specs=jax.tree.map(lambda _: vmem(), outs),
        out_shape=outs,
        scratch_shapes=list(scratch),
        cost_estimate=pl.CostEstimate(flops=flops, bytes_accessed=2**22, transcendentals=0),
        compiler_params=pltpu.CompilerParams(vmem_limit_bytes=56 * 2**20),
    )(*args)


def shape(*dims, dtype=F32):
    return jax.ShapeDtypeStruct(dims, dtype)


def dot_nt(a, b):
    return lax.dot_general(a, b, (((1,), (1,)), ((), ())), preferred_element_type=F32)


def dot(a, b):
    return jnp.dot(a, b, preferred_element_type=F32)


def cut(total, step=STEP):
    step = min(step, total)
    return [slice(at, at + step) for at in range(0, total, step)]


def tiles(refs):
    start = 0
    for ref in refs:
        for rows in cut(ref.shape[0]):
            yield ref, rows, slice(start + rows.start, start + rows.stop)
        start += ref.shape[0]


def factor(block):
    scale = block.shape[1] ** (-0.5)
    block_f = block.astype(F32)
    square = jnp.sum(jnp.square(block_f), axis=1, keepdims=True) * scale
    return (block_f * (2.0 * scale)).astype(BF16), square


def lanes(x):
    total = x[:, 0:128]
    for at in range(128, x.shape[1], 128):
        total = total + x[:, at : at + 128]
    return total


def merge(stats):
    top = stats[0][0:1, :]
    for part in stats[1:]:
        top = jnp.maximum(top, part[0:1, :])
    weights = [jnp.exp(part[0:1, :] - top) for part in stats]
    total = sum(w * part[1:2, :] for w, part in zip(weights, stats))
    return top, total, weights


def online(out, top, sums, load):
    top[...] = jnp.full(top.shape, -jnp.inf, F32)
    sums[...] = jnp.zeros(sums.shape, F32)
    for score, cols, weight in load:
        score = score.reshape(score.shape[0] // 8, 8, score.shape[1])
        old = top[:, cols]
        new = jnp.maximum(old, jnp.max(score, axis=0))
        drop = jnp.exp(old - new)
        expo = jnp.exp(score - new[None])
        sums[0, :, cols] = sums[0, :, cols] * drop + jnp.sum(expo, axis=0)
        if weight is not None:
            expo = expo * weight.reshape(expo.shape)
            sums[1, :, cols] = sums[1, :, cols] * drop + jnp.sum(expo, axis=0)
        top[:, cols] = new
    peak = jnp.max(top[...], axis=0, keepdims=True)
    scale = jnp.exp(top[...] - peak)
    out[0:1, :] = peak
    for at in range(sums.shape[0]):
        out[at + 1 : at + 2, :] = jnp.sum(sums[at] * scale, axis=0, keepdims=True)


def first_stats(order, block, ids, cent, rows, out, cent_rel, top, sums):
    for at, mask in enumerate(order):
        owner = jnp.bitwise_xor(ids[0], mask)
        cent_rel[at * block : (at + 1) * block, :] = cent[pl.ds(pl.multiple_of(owner * block, block), block), :]

    def load():
        for rows_k in cut(cent_rel.shape[0]):
            lhs, square = factor(cent_rel[rows_k, :])
            for cols in cut(rows.shape[0]):
                yield dot_nt(lhs, rows[cols, :]) - square, cols, None

    online(out, top, sums, load())


def first_sums(half, block, parts, stats, cent, rows, out, lse, expo_b):
    peak, total, _ = merge(stats)
    lse[...] = peak + jnp.log(total)
    size = out.shape[0] * block
    per = max(1, min(STEP, size) // block)
    for at in range(0, out.shape[0], per):
        start = half * size + at * block
        lhs, square = factor(cent[start : start + per * block, :])
        count = jnp.zeros((per * block, 128), F32)
        for cols in cut(rows.shape[0]):
            expo = jnp.exp(dot_nt(lhs, rows[cols, :]) - square - lse[:, cols])
            count = count + lanes(expo)
            expo_b[:, cols] = expo.astype(BF16)
        mass = dot(expo_b[...], rows[...])
        for r in range(per):
            part = slice(r * block, (r + 1) * block)
            out[at + r, 0:block, :] = mass[part, :]
            out[at + r, block:, :] = jnp.zeros((out.shape[1] - block, out.shape[2]), F32)
            out[at + r, block : block + 1, 0:block] = jnp.sum(count[part, :].T, axis=0, keepdims=True)


def second_stats(moved, rows, cot, out, top, sums):
    def load():
        for ref, rows_k, _ in tiles(moved):
            block = ref[rows_k, :]
            lhs, square = factor(block)
            for cols in cut(rows.shape[0]):
                yield dot_nt(lhs, rows[cols, :]) - square, cols, dot_nt(block, cot[cols, :])

    online(out, top, sums, load())


def second_rows(stats, lse, dots, scale):
    peak, total, weights = merge(stats)
    lse[...] = peak + jnp.log(total)
    dots[...] = sum(w * part[2:3, :] for w, part in zip(weights, stats)) / total * scale


def put_owners(out, start, value):
    block = out.shape[1]
    per = value.shape[0] // block
    out[start // block : start // block + per] = value.reshape(per, block, value.shape[1]).astype(out.dtype)


def second_sums(stats, moved, rows, cot, outs, lse, dots, expo_b, edge_b):
    second_rows(stats, lse, dots, 2.0 * rows.shape[1] ** (-0.5))
    for ref, rows_k, _ in tiles(moved):
        block = ref[rows_k, :]
        lhs, square = factor(block)
        edges = jnp.zeros((block.shape[0], 128), F32)
        for cols in cut(rows.shape[0]):
            expo = jnp.exp(dot_nt(lhs, rows[cols, :]) - square - lse[:, cols])
            expo_b[:, cols] = expo.astype(BF16)
            edge = expo * (dot_nt(lhs, cot[cols, :]) - dots[:, cols])
            edges = edges + lanes(edge)
            edge_b[:, cols] = edge.astype(BF16)
        total = dot(expo_b[...], cot[...]) + dot(edge_b[...], rows[...])
        total = total - jnp.sum(edges, axis=1, keepdims=True) * block.astype(F32)
        put_owners(outs[0] if ref is moved[0] else outs[1], rows_k.start, total)


def second_part(stats, moved, rows, cot, out, lse, dots, edge_b):
    second_rows(stats, lse, dots, 2.0 * rows.shape[1] ** (-0.5))
    for ref, rows_k, whole in tiles(moved):
        lhs, square = factor(ref[rows_k, :])
        for cols in cut(rows.shape[0]):
            expo = jnp.exp(dot_nt(lhs, rows[cols, :]) - square - lse[:, cols])
            edge = expo * (dot_nt(lhs, cot[cols, :]) - dots[:, cols])
            edge_b[whole, cols] = edge.astype(BF16)
    for cols in cut(rows.shape[0]):
        out[:, cols] = sum(
            dot(ref[...].T, edge_b[at : at + ref.shape[0], cols])
            for ref, at in zip(moved, (0, moved[0].shape[0]))
        )


def put_chunks(index, total, outs):
    size = total.shape[0] // len(outs)
    for r, out in enumerate(outs):
        at = jnp.bitwise_xor(index, r) * size
        out[...] = total[pl.ds(pl.multiple_of(at, size), size), :].astype(out.dtype)


def first_rows(ids, cent, rows, lse, outs, expo_b, total):
    cent_t = cent[...].T
    for whole in cut(cent.shape[0]):
        lhs, square = factor(cent[whole, :])
        for cols in cut(rows.shape[0]):
            expo_b[whole, cols] = jnp.exp(dot_nt(lhs, rows[cols, :]) - square - lse[:, cols]).astype(BF16)
    for cols in cut(rows.shape[0]):
        total[cols, :] = dot(cent_t, expo_b[:, cols]).T
    put_chunks(ids[1], total, outs)


def third_terms(cent, moved, mean_cot, rows, lse, cols_all):
    scale = 2.0 * rows.shape[1] ** (-0.5)
    for (mean_ref, rows_k, whole), (moved_ref, _, _) in zip(tiles(mean_cot), tiles(moved)):
        lhs, square = factor(cent[whole, :])
        mean = mean_ref[rows_k, :].astype(F32) * scale
        count_cot = -jnp.sum(mean * moved_ref[rows_k, :].astype(F32), axis=1, keepdims=True)
        mean = mean.astype(BF16)
        for cols in cols_all:
            expo = jnp.exp(dot_nt(lhs, rows[cols, :]) - square - lse[:, cols])
            yield whole, cols, expo, dot_nt(mean, rows[cols, :]) + count_cot


def third_rows(ids, cent, moved, mean_cot, rows, lse, part, stats, outs, expo_b, edge_b, expo_f, dfirst_f, sums, total):
    cent_t = cent[...].T
    halves = [(ref[...].T, at) for ref, at in zip(mean_cot, (0, mean_cot[0].shape[0]))]
    span = expo_f.shape[1]
    for begin in range(0, rows.shape[0], span):
        cols_all = [slice(begin + c.start, begin + c.stop) for c in cut(span)]
        sums[...] = jnp.zeros(sums.shape, F32)
        for whole, cols, expo, dfirst in third_terms(cent, moved, mean_cot, rows, lse, cols_all):
            local = slice(cols.start - begin, cols.stop - begin)
            expo_f[whole, local] = expo
            dfirst_f[whole, local] = dfirst
            expo_b[whole, local] = expo.astype(BF16)
            group = (expo.shape[0] // 8, 8, expo.shape[1])
            sums[0, :, local] = sums[0, :, local] + jnp.sum((expo * dfirst).reshape(group), axis=0)
            sums[1, :, local] = sums[1, :, local] + jnp.sum(expo.reshape(group), axis=0)
        dots = jnp.sum(sums[0], axis=0, keepdims=True)
        weight = jnp.sum(sums[1], axis=0, keepdims=True)
        mean = jnp.where(weight > 0.0, dots / jnp.where(weight > 0.0, weight, 1.0), 0.0)
        stats[0:1, begin : begin + span] = dots
        stats[1:2, begin : begin + span] = mean
        for local in cut(span):
            cols = slice(begin + local.start, begin + local.stop)
            for whole in cut(cent.shape[0]):
                edge = expo_f[whole, local] * (dfirst_f[whole, local] - mean[:, local])
                edge_b[whole, local] = edge.astype(BF16)
            value = part[:, cols] + dot(cent_t, edge_b[:, local])
            for mean_t, at in halves:
                value = value + dot(mean_t, expo_b[at : at + mean_t.shape[1], local])
            total[cols, :] = value.T
    put_chunks(ids[1], total, outs)


def third_sums(stats, cent, moved, mean_cot, rows, lse, outs, dots, edge_b):
    dots[...] = sum(ref[0:1, :] for ref in stats)
    edges = jnp.zeros((edge_b.shape[0], 128), F32)
    for whole, cols, expo, dfirst in third_terms(cent, moved, mean_cot, rows, lse, cut(rows.shape[0])):
        edge = expo * (dfirst - dots[:, cols])
        edges = edges + lanes(edge)
        edge_b[:, cols] = edge.astype(BF16)
        if cols.stop == rows.shape[0]:
            value = dot(edge_b[...], rows[...])
            value = value - jnp.sum(edges, axis=1, keepdims=True) * cent[whole, :].astype(F32)
            which, start = divmod(whole.start, cent.shape[0] // 2)
            put_owners(outs[which], start, value)
            edges = jnp.zeros(edges.shape, F32)


def place_blocks(order, axis, ids, parts, out):
    at = 0
    for part in parts:
        block = out.shape[0] // len(order)
        for start in range(0, part.shape[0], block):
            owner = jnp.bitwise_xor(ids[axis], order[at])
            out[pl.ds(pl.multiple_of(owner * block, block), block), :] = part[start : start + block, :].astype(out.dtype)
            at += 1


def swap(x, axis, n, mask):
    return lax.ppermute(x, axis, [(i, i ^ mask) for i in range(n)])


def make_local(nv, nc):
    nq = nv // 2
    order = [2 * r + a for a in range(2) for r in range(nq)]

    def local(weights, centroids, cotangent):
        V, D = weights.shape
        K = centroids.shape[0]
        block, half = K // nv, K // 2
        step = min(STEP, half)
        ids = jnp.stack([lax.axis_index("vec"), lax.axis_index("cent")]).astype(jnp.int32)
        unit = 2 * K * V * D
        row = pltpu.VMEM((1, V), F32)
        strip = pltpu.VMEM((step, V), BF16)
        sheet = pltpu.VMEM((K, V), BF16)

        def spread(x):
            return [x] + [swap(x, "cent", nc, r) for r in range(1, nc)]

        def add_core(keep, send):
            return keep.astype(F32) + swap(send, "vec", nv, 1).astype(F32)

        def collect(chunks, beside):
            parts = [swap(chunks[r].astype(BF16), "vec", nv, 2 * r) for r in range(1, nq)]
            parts, beside = lax.optimization_barrier((parts, beside))
            return sum(part.astype(F32) for part in [chunks[0]] + parts), beside

        def share(x):
            mine = jnp.concatenate([x] + [swap(x, "vec", nv, 2 * r) for r in range(1, nq)])
            return [mine, swap(mine, "vec", nv, 1)]

        def split(fn, *counts):
            def kernel(*refs):
                groups, at = [], 0
                for count in counts:
                    groups.append(refs[at] if count == 0 else list(refs[at : at + count]))
                    at += max(count, 1)
                fn(*groups, *refs[at:])
            return kernel

        stats, cent = call(
            lambda *refs: first_stats(order, block, *refs),
            (shape(2, V), shape(K, D, dtype=BF16)),
            (ids, centroids, weights),
            [pltpu.VMEM((8, V), F32), pltpu.VMEM((1, 8, V), F32)],
            unit,
            [smem(), vmem(), vmem()],
        )
        stats = spread(stats)

        def sums(at):
            return call(
                split(lambda *refs: first_sums(at, block, nc, *refs), nc, 0, 0, 0, 0),
                (shape(nq, block + 16, D), shape(1, V)),
                (*stats, cent, weights),
                [strip],
                unit,
            )

        def rows_shape(kind):
            return [shape(V // nc, D, dtype=kind)] * nc

        def scatter(chunks):
            return [chunks[0]] + [swap(chunks[r], "cent", nc, r) for r in range(1, nc)]

        send, _ = sums(1)
        keep, lse = sums(0)
        first_cent = call(
            split(first_rows, 0, 0, 0, 0, nc),
            rows_shape(BF16),
            (ids, cent, weights, lse),
            [sheet, pltpu.VMEM((V, D), F32)],
            2 * unit,
            [smem()] + [vmem()] * 3,
        )
        chunks = add_core(keep, send)
        count = chunks[:, block]
        near = lax.reduce_precision(count, 8, 7)
        pair = jnp.stack([near, count - near], axis=1)
        chunks = jnp.concatenate([chunks[:, :block], pair, chunks[:, block + 2 :]], axis=1)
        chunk, first_cent = collect(chunks, first_cent)
        denom = chunk[block, :block] + chunk[block + 1, :block] + 1e-6
        moved = share((chunk[:block] / denom[:, None]).astype(BF16))
        first_cent = scatter(first_cent)

        stats = spread(call(
            split(second_stats, 2),
            shape(3, V),
            (*moved, weights, cotangent),
            [pltpu.VMEM((8, V), F32), pltpu.VMEM((2, 8, V), F32)],
        ))
        stats, first_cent = lax.optimization_barrier((stats, first_cent))
        moved_cot = call(
            split(second_sums, nc, 2, 0, 0, 2),
            [shape(nq, block, D, dtype=BF16)] * 2,
            (*stats, *moved, weights, cotangent),
            [row, row, strip, strip],
            4 * unit,
        )
        part = call(
            split(second_part, nc, 2),
            shape(D, V),
            (*stats, *moved, weights, cotangent),
            [row, row, sheet],
            3 * unit,
        )
        moved_cot, part = collect(add_core(*moved_cot), part)
        mean_cot = share((moved_cot / denom[:, None]).astype(BF16))

        span = V // 2
        stats, *grad_rows = call(
            split(third_rows, 0, 0, 2, 2, 0, 0, 0, 0, nc),
            [shape(2, V)] + rows_shape(BF16),
            (ids, cent, *moved, *mean_cot, weights, lse, part),
            [pltpu.VMEM((K, span), BF16)] * 2
            + [pltpu.VMEM((K, span), F32)] * 2
            + [pltpu.VMEM((2, 8, span), F32), pltpu.VMEM((V, D), F32)],
            4 * unit,
            [smem()] + [vmem()] * 8,
        )
        stats = spread(stats)
        grad_rows = scatter(grad_rows)
        start_cot = call(
            split(third_sums, nc, 0, 2, 2, 0, 0, 2),
            [shape(nq, block, D, dtype=BF16)] * 2,
            (*stats, cent, *moved, *mean_cot, weights, lse),
            [row, strip],
        )
        start_cot, grad_rows = lax.optimization_barrier((start_cot, grad_rows))
        start_cot, _ = collect(add_core(*start_cot), ())

        size = V // nc
        mine = lax.axis_index("cent") * size
        own = [lax.dynamic_slice(x, (0, mine), (2, size)) for x in stats]
        dots = sum(x[0] for x in own)
        rows = sum(x.astype(F32) for x in grad_rows)
        rows = rows - sum((dots - x[1])[:, None] * f.astype(F32) for x, f in zip(own, first_cent))
        rows = spread(rows.astype(BF16))
        start_cot = call(
            split(lambda *refs: place_blocks(order, 0, *refs), 0, 2),
            shape(K, D),
            (ids, *share(start_cot.astype(BF16))),
            specs=[smem()] + [vmem()] * 2,
        )
        grad_rows = jnp.zeros((V, D), BF16)
        for r in range(nc):
            at = jnp.bitwise_xor(lax.axis_index("cent"), r) * size
            grad_rows = lax.dynamic_update_slice(grad_rows, rows[r], (at, 0))
        return grad_rows, start_cot

    return local


def solution(mesh):
    return jax.shard_map(
        make_local(mesh.shape["vec"], mesh.shape["cent"]),
        mesh=mesh,
        in_specs=(P("vec", None), P("cent", None), P("vec", None)),
        out_specs=(P("vec", None), P("cent", None)),
        check_vma=False,
    )
```

```python
import jax
import jax.numpy as jnp
from jax import lax
from jax.experimental import pallas as pl
from jax.experimental.pallas import tpu as pltpu
from jax.sharding import PartitionSpec as P

F32 = jnp.float32
BF16 = jnp.bfloat16
STEP = 512


def vmem():
    return pl.BlockSpec(memory_space=pltpu.VMEM)


def smem():
    return pl.BlockSpec(memory_space=pltpu.SMEM)


def call(kernel, outs, args, scratch=(), flops=0, specs=None):
    return pl.pallas_call(
        kernel,
        in_specs=specs or [vmem()] * len(args),
        out_specs=jax.tree.map(lambda _: vmem(), outs),
        out_shape=outs,
        scratch_shapes=list(scratch),
        cost_estimate=pl.CostEstimate(flops=flops, bytes_accessed=2**22, transcendentals=0),
        compiler_params=pltpu.CompilerParams(vmem_limit_bytes=56 * 2**20),
    )(*args)


def shape(*dims, dtype=F32):
    return jax.ShapeDtypeStruct(dims, dtype)


def dot_nt(a, b):
    return lax.dot_general(a, b, (((1,), (1,)), ((), ())), preferred_element_type=F32)


def dot(a, b):
    return jnp.dot(a, b, preferred_element_type=F32)


def cut(total, step=STEP):
    step = min(step, total)
    return [slice(at, at + step) for at in range(0, total, step)]


def tiles(refs):
    start = 0
    for ref in refs:
        for rows in cut(ref.shape[0]):
            yield ref, rows, slice(start + rows.start, start + rows.stop)
        start += ref.shape[0]


def factor(block):
    scale = block.shape[1] ** (-0.5)
    block_f = block.astype(F32)
    square = jnp.sum(jnp.square(block_f), axis=1, keepdims=True) * scale
    return (block_f * (2.0 * scale)).astype(BF16), square


def lanes(x):
    total = x[:, 0:128]
    for at in range(128, x.shape[1], 128):
        total = total + x[:, at : at + 128]
    return total


def merge(stats):
    top = stats[0][0:1, :]
    for part in stats[1:]:
        top = jnp.maximum(top, part[0:1, :])
    weights = [jnp.exp(part[0:1, :] - top) for part in stats]
    total = sum(w * part[1:2, :] for w, part in zip(weights, stats))
    return top, total, weights


def online(out, top, sums, load):
    top[...] = jnp.full(top.shape, -jnp.inf, F32)
    sums[...] = jnp.zeros(sums.shape, F32)
    for score, cols, weight in load:
        score = score.reshape(score.shape[0] // 8, 8, score.shape[1])
        old = top[:, cols]
        new = jnp.maximum(old, jnp.max(score, axis=0))
        drop = jnp.exp(old - new)
        expo = jnp.exp(score - new[None])
        sums[0, :, cols] = sums[0, :, cols] * drop + jnp.sum(expo, axis=0)
        if weight is not None:
            expo = expo * weight.reshape(expo.shape)
            sums[1, :, cols] = sums[1, :, cols] * drop + jnp.sum(expo, axis=0)
        top[:, cols] = new
    peak = jnp.max(top[...], axis=0, keepdims=True)
    scale = jnp.exp(top[...] - peak)
    out[0:1, :] = peak
    for at in range(sums.shape[0]):
        out[at + 1 : at + 2, :] = jnp.sum(sums[at] * scale, axis=0, keepdims=True)


def first_stats(order, block, ids, cent, rows, out, cent_rel, top, sums):
    for at, mask in enumerate(order):
        owner = jnp.bitwise_xor(ids[0], mask)
        cent_rel[at * block : (at + 1) * block, :] = cent[pl.ds(pl.multiple_of(owner * block, block), block), :]

    def load():
        for rows_k in cut(cent_rel.shape[0]):
            lhs, square = factor(cent_rel[rows_k, :])
            for cols in cut(rows.shape[0]):
                yield dot_nt(lhs, rows[cols, :]) - square, cols, None

    online(out, top, sums, load())


def first_sums(half, block, parts, stats, cent, rows, out, lse, expo_b):
    peak, total, _ = merge(stats)
    lse[...] = peak + jnp.log(total)
    size = out.shape[0] * block
    per = max(1, min(STEP, size) // block)
    for at in range(0, out.shape[0], per):
        start = half * size + at * block
        lhs, square = factor(cent[start : start + per * block, :])
        count = jnp.zeros((per * block, 128), F32)
        for cols in cut(rows.shape[0]):
            expo = jnp.exp(dot_nt(lhs, rows[cols, :]) - square - lse[:, cols])
            count = count + lanes(expo)
            expo_b[:, cols] = expo.astype(BF16)
        mass = dot(expo_b[...], rows[...])
        for r in range(per):
            part = slice(r * block, (r + 1) * block)
            out[at + r, 0:block, :] = mass[part, :]
            out[at + r, block:, :] = jnp.zeros((out.shape[1] - block, out.shape[2]), F32)
            out[at + r, block : block + 1, 0:block] = jnp.sum(count[part, :].T, axis=0, keepdims=True)


def second_stats(moved, rows, cot, out, top, sums):
    def load():
        for ref, rows_k, _ in tiles(moved):
            block = ref[rows_k, :]
            lhs, square = factor(block)
            for cols in cut(rows.shape[0]):
                yield dot_nt(lhs, rows[cols, :]) - square, cols, dot_nt(block, cot[cols, :])

    online(out, top, sums, load())


def second_rows(stats, lse, dots, scale):
    peak, total, weights = merge(stats)
    lse[...] = peak + jnp.log(total)
    dots[...] = sum(w * part[2:3, :] for w, part in zip(weights, stats)) / total * scale


def put_owners(out, start, value):
    block = out.shape[1]
    per = value.shape[0] // block
    out[start // block : start // block + per] = value.reshape(per, block, value.shape[1]).astype(out.dtype)


def second_sums(stats, moved, rows, cot, outs, lse, dots, expo_b, edge_b):
    second_rows(stats, lse, dots, 2.0 * rows.shape[1] ** (-0.5))
    for ref, rows_k, _ in tiles(moved):
        block = ref[rows_k, :]
        lhs, square = factor(block)
        edges = jnp.zeros((block.shape[0], 128), F32)
        for cols in cut(rows.shape[0]):
            expo = jnp.exp(dot_nt(lhs, rows[cols, :]) - square - lse[:, cols])
            expo_b[:, cols] = expo.astype(BF16)
            edge = expo * (dot_nt(lhs, cot[cols, :]) - dots[:, cols])
            edges = edges + lanes(edge)
            edge_b[:, cols] = edge.astype(BF16)
        total = dot(expo_b[...], cot[...]) + dot(edge_b[...], rows[...])
        total = total - jnp.sum(edges, axis=1, keepdims=True) * block.astype(F32)
        put_owners(outs[0] if ref is moved[0] else outs[1], rows_k.start, total)


def second_part(begin, stats, moved, rows, cot, out, lse, dots, edge_b):
    second_rows(stats, lse, dots, 2.0 * rows.shape[1] ** (-0.5))
    for ref, rows_k, whole in tiles(moved):
        lhs, square = factor(ref[rows_k, :])
        for local in cut(out.shape[1]):
            cols = slice(begin + local.start, begin + local.stop)
            expo = jnp.exp(dot_nt(lhs, rows[cols, :]) - square - lse[:, cols])
            edge = expo * (dot_nt(lhs, cot[cols, :]) - dots[:, cols])
            edge_b[whole, local] = edge.astype(BF16)
    for local in cut(out.shape[1]):
        out[:, local] = sum(
            dot(ref[...].T, edge_b[at : at + ref.shape[0], local])
            for ref, at in zip(moved, (0, moved[0].shape[0]))
        )


def put_chunks(index, total, outs):
    size = total.shape[0] // len(outs)
    for r, out in enumerate(outs):
        at = jnp.bitwise_xor(index, r) * size
        out[...] = total[pl.ds(pl.multiple_of(at, size), size), :].astype(out.dtype)


def first_rows(masks, ids, cent, rows, lse, outs, expo_b):
    cent_t = cent[...].T
    for mask, out in zip(masks, outs):
        size = out.shape[0]
        own = pl.ds(pl.multiple_of(jnp.bitwise_xor(ids[1], mask) * size, size), size)
        chunk, shift = rows[own, :], lse[:, own]
        for whole in cut(cent.shape[0]):
            lhs, square = factor(cent[whole, :])
            expo_b[whole, :] = jnp.exp(dot_nt(lhs, chunk) - square - shift).astype(BF16)
        out[...] = dot(cent_t, expo_b[...]).T.astype(out.dtype)


def third_terms(cent, moved, mean_cot, rows, lse, cols_all):
    scale = 2.0 * rows.shape[1] ** (-0.5)
    for (mean_ref, rows_k, whole), (moved_ref, _, _) in zip(tiles(mean_cot), tiles(moved)):
        lhs, square = factor(cent[whole, :])
        mean = mean_ref[rows_k, :].astype(F32) * scale
        count_cot = -jnp.sum(mean * moved_ref[rows_k, :].astype(F32), axis=1, keepdims=True)
        mean = mean.astype(BF16)
        for cols in cols_all:
            expo = jnp.exp(dot_nt(lhs, rows[cols, :]) - square - lse[:, cols])
            yield whole, cols, expo, dot_nt(mean, rows[cols, :]) + count_cot


def third_rows(ids, cent, moved, mean_cot, rows, lse, parts, stats, outs, expo_b, edge_b, expo_f, dfirst_f, sums, total):
    cent_t = cent[...].T
    halves = [(ref[...].T, at) for ref, at in zip(mean_cot, (0, mean_cot[0].shape[0]))]
    span = expo_f.shape[1]
    for begin, part in zip(range(0, rows.shape[0], span), parts):
        cols_all = [slice(begin + c.start, begin + c.stop) for c in cut(span)]
        sums[...] = jnp.zeros(sums.shape, F32)
        for whole, cols, expo, dfirst in third_terms(cent, moved, mean_cot, rows, lse, cols_all):
            local = slice(cols.start - begin, cols.stop - begin)
            expo_f[whole, local] = expo
            dfirst_f[whole, local] = dfirst
            expo_b[whole, local] = expo.astype(BF16)
            group = (expo.shape[0] // 8, 8, expo.shape[1])
            sums[0, :, local] = sums[0, :, local] + jnp.sum((expo * dfirst).reshape(group), axis=0)
            sums[1, :, local] = sums[1, :, local] + jnp.sum(expo.reshape(group), axis=0)
        dots = jnp.sum(sums[0], axis=0, keepdims=True)
        weight = jnp.sum(sums[1], axis=0, keepdims=True)
        mean = jnp.where(weight > 0.0, dots / jnp.where(weight > 0.0, weight, 1.0), 0.0)
        stats[0:1, begin : begin + span] = dots
        stats[1:2, begin : begin + span] = mean
        for local in cut(span):
            cols = slice(begin + local.start, begin + local.stop)
            for whole in cut(cent.shape[0]):
                edge = expo_f[whole, local] * (dfirst_f[whole, local] - mean[:, local])
                edge_b[whole, local] = edge.astype(BF16)
            value = part[:, local] + dot(cent_t, edge_b[:, local])
            for mean_t, at in halves:
                value = value + dot(mean_t, expo_b[at : at + mean_t.shape[1], local])
            total[cols, :] = value.T
    put_chunks(ids[1], total, outs)


def third_sums(stats, cent, moved, mean_cot, rows, lse, outs, dots, edge_b):
    dots[...] = sum(ref[0:1, :] for ref in stats)
    edges = jnp.zeros((edge_b.shape[0], 128), F32)
    for whole, cols, expo, dfirst in third_terms(cent, moved, mean_cot, rows, lse, cut(rows.shape[0])):
        edge = expo * (dfirst - dots[:, cols])
        edges = edges + lanes(edge)
        edge_b[:, cols] = edge.astype(BF16)
        if cols.stop == rows.shape[0]:
            value = dot(edge_b[...], rows[...])
            value = value - jnp.sum(edges, axis=1, keepdims=True) * cent[whole, :].astype(F32)
            which, start = divmod(whole.start, cent.shape[0] // 2)
            put_owners(outs[which], start, value)
            edges = jnp.zeros(edges.shape, F32)


def place_blocks(order, axis, ids, parts, out):
    at = 0
    for part in parts:
        block = out.shape[0] // len(order)
        for start in range(0, part.shape[0], block):
            owner = jnp.bitwise_xor(ids[axis], order[at])
            out[pl.ds(pl.multiple_of(owner * block, block), block), :] = part[start : start + block, :].astype(out.dtype)
            at += 1


def swap(x, axis, n, mask):
    return lax.ppermute(x, axis, [(i, i ^ mask) for i in range(n)])


def make_local(nv, nc):
    nq = nv // 2
    order = [2 * r + a for a in range(2) for r in range(nq)]

    def local(weights, centroids, cotangent):
        V, D = weights.shape
        K = centroids.shape[0]
        block, half = K // nv, K // 2
        step = min(STEP, half)
        ids = jnp.stack([lax.axis_index("vec"), lax.axis_index("cent")]).astype(jnp.int32)
        unit = 2 * K * V * D
        row = pltpu.VMEM((1, V), F32)
        strip = pltpu.VMEM((step, V), BF16)

        def spread(x):
            return [x] + [swap(x, "cent", nc, r) for r in range(1, nc)]

        def add_core(keep, send):
            return keep.astype(F32) + swap(send, "vec", nv, 1).astype(F32)

        def collect(chunks, beside):
            parts = [swap(chunks[r].astype(BF16), "vec", nv, 2 * r) for r in range(1, nq)]
            parts, beside = lax.optimization_barrier((parts, beside))
            return sum(part.astype(F32) for part in [chunks[0]] + parts), beside

        def share(x, beside):
            parts = [swap(x, "vec", nv, 2 * r) for r in range(1, nq)]
            parts, beside = lax.optimization_barrier((parts, beside))
            mine = jnp.concatenate([x] + parts)
            return [mine, swap(mine, "vec", nv, 1)], beside

        def split(fn, *counts):
            def kernel(*refs):
                groups, at = [], 0
                for count in counts:
                    groups.append(refs[at] if count == 0 else list(refs[at : at + count]))
                    at += max(count, 1)
                fn(*groups, *refs[at:])
            return kernel

        stats, cent = call(
            lambda *refs: first_stats(order, block, *refs),
            (shape(2, V), shape(K, D, dtype=BF16)),
            (ids, centroids, weights),
            [pltpu.VMEM((8, V), F32), pltpu.VMEM((1, 8, V), F32)],
            unit,
            [smem(), vmem(), vmem()],
        )
        stats = spread(stats)

        def sums(at):
            return call(
                split(lambda *refs: first_sums(at, block, nc, *refs), nc, 0, 0, 0, 0),
                (shape(nq, block + 16, D), shape(1, V)),
                (*stats, cent, weights),
                [strip],
                unit,
            )

        def rows_shape(kind):
            return [shape(V // nc, D, dtype=kind)] * nc

        def scatter(chunks):
            return [chunks[0]] + [swap(chunks[r], "cent", nc, r) for r in range(1, nc)]

        send, _ = sums(1)
        keep, lse = sums(0)

        def first_part(masks):
            return call(
                split(lambda *refs: first_rows(masks, *refs), 0, 0, 0, 0, len(masks)),
                [shape(V // nc, D, dtype=BF16)] * len(masks),
                (ids, cent, weights, lse),
                [pltpu.VMEM((K, V // nc), BF16)],
                unit,
                [smem()] + [vmem()] * 3,
            )

        first_cent = first_part(list(range(nc // 2)))
        chunks = add_core(keep, send)
        count = chunks[:, block]
        near = lax.reduce_precision(count, 8, 7)
        pair = jnp.stack([near, count - near], axis=1)
        chunks = jnp.concatenate([chunks[:, :block], pair, chunks[:, block + 2 :]], axis=1)
        chunk, first_cent = collect(chunks, first_cent)
        denom = chunk[block, :block] + chunk[block + 1, :block] + 1e-6
        moved, more = share(
            (chunk[:block] / denom[:, None]).astype(BF16), first_part(list(range(nc // 2, nc)))
        )
        first_cent = scatter([*first_cent, *more])

        stats = spread(call(
            split(second_stats, 2),
            shape(3, V),
            (*moved, weights, cotangent),
            [pltpu.VMEM((8, V), F32), pltpu.VMEM((2, 8, V), F32)],
        ))
        moved_cot = call(
            split(second_sums, nc, 2, 0, 0, 2),
            [shape(nq, block, D, dtype=BF16)] * 2,
            (*stats, *moved, weights, cotangent),
            [row, row, strip, strip],
            4 * unit,
        )
        span = V // 2

        def part(begin):
            return call(
                split(lambda *refs: second_part(begin, *refs), nc, 2),
                shape(D, span),
                (*stats, *moved, weights, cotangent),
                [row, row, pltpu.VMEM((K, span), BF16)],
                unit,
            )

        moved_cot, part_low = collect(add_core(*moved_cot), part(0))
        mean_cot, part_high = share((moved_cot / denom[:, None]).astype(BF16), part(span))

        stats, *grad_rows = call(
            split(third_rows, 0, 0, 2, 2, 0, 0, 2, 0, nc),
            [shape(2, V)] + rows_shape(BF16),
            (ids, cent, *moved, *mean_cot, weights, lse, part_low, part_high),
            [pltpu.VMEM((K, span), BF16)] * 2
            + [pltpu.VMEM((K, span), F32)] * 2
            + [pltpu.VMEM((2, 8, span), F32), pltpu.VMEM((V, D), F32)],
            4 * unit,
            [smem()] + [vmem()] * 9,
        )
        stats, first_cent = lax.optimization_barrier((stats, first_cent))
        stats = spread(stats)
        stats, grad_rows = lax.optimization_barrier((stats, grad_rows))
        grad_rows = scatter(grad_rows)
        start_cot = call(
            split(third_sums, nc, 0, 2, 2, 0, 0, 2),
            [shape(nq, block, D, dtype=BF16)] * 2,
            (*stats, cent, *moved, *mean_cot, weights, lse),
            [row, strip],
        )
        far = nc // 2
        start_cot, grad_rows[far] = lax.optimization_barrier((start_cot, grad_rows[far]))
        start_cot, grad_rows = collect(add_core(*start_cot), grad_rows)

        size = V // nc
        mine = lax.axis_index("cent") * size
        own = [lax.dynamic_slice(x, (0, mine), (2, size)) for x in stats]
        dots = sum(x[0] for x in own)
        rows = sum(x.astype(F32) for x in grad_rows)
        rows = rows - sum((dots - x[1])[:, None] * f.astype(F32) for x, f in zip(own, first_cent))
        rows = spread(rows.astype(BF16))
        start_cot, rows[far] = share(start_cot.astype(BF16), rows[far])
        start_cot = call(
            split(lambda *refs: place_blocks(order, 0, *refs), 0, 2),
            shape(K, D),
            (ids, *start_cot),
            specs=[smem()] + [vmem()] * 2,
        )
        grad_rows = jnp.zeros((V, D), BF16)
        for r in range(nc):
            at = jnp.bitwise_xor(lax.axis_index("cent"), r) * size
            grad_rows = lax.dynamic_update_slice(grad_rows, rows[r], (at, 0))
        return grad_rows, start_cot

    return local


def solution(mesh):
    return jax.shard_map(
        make_local(mesh.shape["vec"], mesh.shape["cent"]),
        mesh=mesh,
        in_specs=(P("vec", None), P("cent", None), P("vec", None)),
        out_specs=(P("vec", None), P("cent", None)),
        check_vma=False,
    )
```

```python
import jax
import jax.numpy as jnp
from jax import lax
from jax.experimental import pallas as pl
from jax.experimental.pallas import tpu as pltpu
from jax.sharding import PartitionSpec as P

F32 = jnp.float32
BF16 = jnp.bfloat16
STEP = 512


def vmem():
    return pl.BlockSpec(memory_space=pltpu.VMEM)


def smem():
    return pl.BlockSpec(memory_space=pltpu.SMEM)


def call(kernel, outs, args, scratch=(), flops=0, specs=None):
    return pl.pallas_call(
        kernel,
        in_specs=specs or [vmem()] * len(args),
        out_specs=jax.tree.map(lambda _: vmem(), outs),
        out_shape=outs,
        scratch_shapes=list(scratch),
        cost_estimate=pl.CostEstimate(flops=flops, bytes_accessed=2**22, transcendentals=0),
        compiler_params=pltpu.CompilerParams(vmem_limit_bytes=56 * 2**20),
    )(*args)


def shape(*dims, dtype=F32):
    return jax.ShapeDtypeStruct(dims, dtype)


def dot_nt(a, b):
    return lax.dot_general(a, b, (((1,), (1,)), ((), ())), preferred_element_type=F32)


def dot(a, b):
    return jnp.dot(a, b, preferred_element_type=F32)


def cut(total, step=STEP):
    step = min(step, total)
    return [slice(at, at + step) for at in range(0, total, step)]


def tiles(refs):
    start = 0
    for ref in refs:
        for rows in cut(ref.shape[0]):
            yield ref, rows, slice(start + rows.start, start + rows.stop)
        start += ref.shape[0]


def factor(block):
    scale = block.shape[1] ** (-0.5)
    block_f = block.astype(F32)
    square = jnp.sum(jnp.square(block_f), axis=1, keepdims=True) * scale
    return (block_f * (2.0 * scale)).astype(BF16), square


def lanes(x):
    total = x[:, 0:128]
    for at in range(128, x.shape[1], 128):
        total = total + x[:, at : at + 128]
    return total


def merge(stats):
    top = stats[0][0:1, :]
    for part in stats[1:]:
        top = jnp.maximum(top, part[0:1, :])
    weights = [jnp.exp(part[0:1, :] - top) for part in stats]
    total = sum(w * part[1:2, :] for w, part in zip(weights, stats))
    return top, total, weights


def online(out, top, sums, load):
    top[...] = jnp.full(top.shape, -jnp.inf, F32)
    sums[...] = jnp.zeros(sums.shape, F32)
    for score, cols, weight in load:
        score = score.reshape(score.shape[0] // 8, 8, score.shape[1])
        old = top[:, cols]
        new = jnp.maximum(old, jnp.max(score, axis=0))
        drop = jnp.exp(old - new)
        expo = jnp.exp(score - new[None])
        sums[0, :, cols] = sums[0, :, cols] * drop + jnp.sum(expo, axis=0)
        if weight is not None:
            expo = expo * weight.reshape(expo.shape)
            sums[1, :, cols] = sums[1, :, cols] * drop + jnp.sum(expo, axis=0)
        top[:, cols] = new
    peak = jnp.max(top[...], axis=0, keepdims=True)
    scale = jnp.exp(top[...] - peak)
    out[0:1, :] = peak
    for at in range(sums.shape[0]):
        out[at + 1 : at + 2, :] = jnp.sum(sums[at] * scale, axis=0, keepdims=True)


def first_stats(order, block, ids, cent, rows, out, cent_rel, top, sums):
    for at, mask in enumerate(order):
        owner = jnp.bitwise_xor(ids[0], mask)
        cent_rel[at * block : (at + 1) * block, :] = cent[pl.ds(pl.multiple_of(owner * block, block), block), :]

    def load():
        for rows_k in cut(cent_rel.shape[0]):
            lhs, square = factor(cent_rel[rows_k, :])
            for cols in cut(rows.shape[0]):
                yield dot_nt(lhs, rows[cols, :]) - square, cols, None

    online(out, top, sums, load())


def first_sums(half, block, parts, stats, cent, rows, out, lse, expo_b):
    peak, total, _ = merge(stats)
    lse[...] = peak + jnp.log(total)
    size = out.shape[0] * block
    per = max(1, min(STEP, size) // block)
    for at in range(0, out.shape[0], per):
        start = half * size + at * block
        lhs, square = factor(cent[start : start + per * block, :])
        count = jnp.zeros((per * block, 128), F32)
        for cols in cut(rows.shape[0]):
            expo = jnp.exp(dot_nt(lhs, rows[cols, :]) - square - lse[:, cols])
            count = count + lanes(expo)
            expo_b[:, cols] = expo.astype(BF16)
        mass = dot(expo_b[...], rows[...])
        for r in range(per):
            part = slice(r * block, (r + 1) * block)
            out[at + r, 0:block, :] = mass[part, :]
            out[at + r, block:, :] = jnp.zeros((out.shape[1] - block, out.shape[2]), F32)
            out[at + r, block : block + 1, 0:block] = jnp.sum(count[part, :].T, axis=0, keepdims=True)


def second_stats(moved, rows, cot, out, top, sums):
    def load():
        for ref, rows_k, _ in tiles(moved):
            block = ref[rows_k, :]
            lhs, square = factor(block)
            for cols in cut(rows.shape[0]):
                yield dot_nt(lhs, rows[cols, :]) - square, cols, dot_nt(block, cot[cols, :])

    online(out, top, sums, load())


def second_rows(stats, lse, dots, scale):
    peak, total, weights = merge(stats)
    lse[...] = peak + jnp.log(total)
    dots[...] = sum(w * part[2:3, :] for w, part in zip(weights, stats)) / total * scale


def put_owners(out, start, value):
    block = out.shape[1]
    per = value.shape[0] // block
    out[start // block : start // block + per] = value.reshape(per, block, value.shape[1]).astype(out.dtype)


def second_sums(stats, moved, rows, cot, outs, lse, dots, expo_b, edge_b):
    second_rows(stats, lse, dots, 2.0 * rows.shape[1] ** (-0.5))
    for ref, rows_k, _ in tiles(moved):
        block = ref[rows_k, :]
        lhs, square = factor(block)
        edges = jnp.zeros((block.shape[0], 128), F32)
        for cols in cut(rows.shape[0]):
            expo = jnp.exp(dot_nt(lhs, rows[cols, :]) - square - lse[:, cols])
            expo_b[:, cols] = expo.astype(BF16)
            edge = expo * (dot_nt(lhs, cot[cols, :]) - dots[:, cols])
            edges = edges + lanes(edge)
            edge_b[:, cols] = edge.astype(BF16)
        total = dot(expo_b[...], cot[...]) + dot(edge_b[...], rows[...])
        total = total - jnp.sum(edges, axis=1, keepdims=True) * block.astype(F32)
        put_owners(outs[0] if ref is moved[0] else outs[1], rows_k.start, total)


def second_part(begin, stats, moved, rows, cot, out, lse, dots, edge_b):
    second_rows(stats, lse, dots, 2.0 * rows.shape[1] ** (-0.5))
    for ref, rows_k, whole in tiles(moved):
        lhs, square = factor(ref[rows_k, :])
        for local in cut(out.shape[1]):
            cols = slice(begin + local.start, begin + local.stop)
            expo = jnp.exp(dot_nt(lhs, rows[cols, :]) - square - lse[:, cols])
            edge = expo * (dot_nt(lhs, cot[cols, :]) - dots[:, cols])
            edge_b[whole, local] = edge.astype(BF16)
    for local in cut(out.shape[1]):
        out[:, local] = sum(
            dot(ref[...].T, edge_b[at : at + ref.shape[0], local])
            for ref, at in zip(moved, (0, moved[0].shape[0]))
        )


def put_chunks(index, total, outs):
    size = total.shape[0] // len(outs)
    for r, out in enumerate(outs):
        at = jnp.bitwise_xor(index, r) * size
        out[...] = total[pl.ds(pl.multiple_of(at, size), size), :].astype(out.dtype)


def first_rows(masks, ids, cent, rows, lse, outs, expo_b):
    cent_t = cent[...].T
    for mask, out in zip(masks, outs):
        size = out.shape[0]
        own = pl.ds(pl.multiple_of(jnp.bitwise_xor(ids[1], mask) * size, size), size)
        chunk, shift = rows[own, :], lse[:, own]
        for whole in cut(cent.shape[0]):
            lhs, square = factor(cent[whole, :])
            expo_b[whole, :] = jnp.exp(dot_nt(lhs, chunk) - square - shift).astype(BF16)
        out[...] = dot(cent_t, expo_b[...]).T.astype(out.dtype)


def third_terms(cent, moved, mean_cot, rows, lse, cols_all):
    scale = 2.0 * rows.shape[1] ** (-0.5)
    for (mean_ref, rows_k, whole), (moved_ref, _, _) in zip(tiles(mean_cot), tiles(moved)):
        lhs, square = factor(cent[whole, :])
        mean = mean_ref[rows_k, :].astype(F32) * scale
        count_cot = -jnp.sum(mean * moved_ref[rows_k, :].astype(F32), axis=1, keepdims=True)
        mean = mean.astype(BF16)
        for cols in cols_all:
            expo = jnp.exp(dot_nt(lhs, rows[cols, :]) - square - lse[:, cols])
            yield whole, cols, expo, dot_nt(mean, rows[cols, :]) + count_cot


def third_rows(ids, cent, moved, mean_cot, rows, lse, parts, stats, outs, expo_b, edge_b, expo_f, dfirst_f, sums, total):
    cent_t = cent[...].T
    halves = [(ref[...].T, at) for ref, at in zip(mean_cot, (0, mean_cot[0].shape[0]))]
    span = expo_f.shape[1]
    for begin, part in zip(range(0, rows.shape[0], span), parts):
        cols_all = [slice(begin + c.start, begin + c.stop) for c in cut(span)]
        sums[...] = jnp.zeros(sums.shape, F32)
        for whole, cols, expo, dfirst in third_terms(cent, moved, mean_cot, rows, lse, cols_all):
            local = slice(cols.start - begin, cols.stop - begin)
            expo_f[whole, local] = expo
            dfirst_f[whole, local] = dfirst
            expo_b[whole, local] = expo.astype(BF16)
            group = (expo.shape[0] // 8, 8, expo.shape[1])
            sums[0, :, local] = sums[0, :, local] + jnp.sum((expo * dfirst).reshape(group), axis=0)
            sums[1, :, local] = sums[1, :, local] + jnp.sum(expo.reshape(group), axis=0)
        dots = jnp.sum(sums[0], axis=0, keepdims=True)
        weight = jnp.sum(sums[1], axis=0, keepdims=True)
        mean = jnp.where(weight > 0.0, dots / jnp.where(weight > 0.0, weight, 1.0), 0.0)
        stats[0:1, begin : begin + span] = dots
        stats[1:2, begin : begin + span] = mean
        for local in cut(span):
            cols = slice(begin + local.start, begin + local.stop)
            for whole in cut(cent.shape[0]):
                edge = expo_f[whole, local] * (dfirst_f[whole, local] - mean[:, local])
                edge_b[whole, local] = edge.astype(BF16)
            value = part[:, local] + dot(cent_t, edge_b[:, local])
            for mean_t, at in halves:
                value = value + dot(mean_t, expo_b[at : at + mean_t.shape[1], local])
            total[cols, :] = value.T
    put_chunks(ids[1], total, outs)


def third_sums(stats, cent, moved, mean_cot, rows, lse, outs, dots, edge_b):
    dots[...] = sum(ref[0:1, :] for ref in stats)
    edges = jnp.zeros((edge_b.shape[0], 128), F32)
    for whole, cols, expo, dfirst in third_terms(cent, moved, mean_cot, rows, lse, cut(rows.shape[0])):
        edge = expo * (dfirst - dots[:, cols])
        edges = edges + lanes(edge)
        edge_b[:, cols] = edge.astype(BF16)
        if cols.stop == rows.shape[0]:
            value = dot(edge_b[...], rows[...])
            value = value - jnp.sum(edges, axis=1, keepdims=True) * cent[whole, :].astype(F32)
            which, start = divmod(whole.start, cent.shape[0] // 2)
            put_owners(outs[which], start, value)
            edges = jnp.zeros(edges.shape, F32)


def place_blocks(order, axis, ids, parts, out):
    at = 0
    for part in parts:
        block = out.shape[0] // len(order)
        for start in range(0, part.shape[0], block):
            owner = jnp.bitwise_xor(ids[axis], order[at])
            out[pl.ds(pl.multiple_of(owner * block, block), block), :] = part[start : start + block, :].astype(out.dtype)
            at += 1


def swap(x, axis, n, mask):
    return lax.ppermute(x, axis, [(i, i ^ mask) for i in range(n)])


def make_local(nv, nc):
    nq = nv // 2
    order = [2 * r + a for a in range(2) for r in range(nq)]

    def local(weights, centroids, cotangent):
        V, D = weights.shape
        K = centroids.shape[0]
        block, half = K // nv, K // 2
        step = min(STEP, half)
        ids = jnp.stack([lax.axis_index("vec"), lax.axis_index("cent")]).astype(jnp.int32)
        unit = 2 * K * V * D
        row = pltpu.VMEM((1, V), F32)
        strip = pltpu.VMEM((step, V), BF16)

        def spread(x):
            return [x] + [swap(x, "cent", nc, r) for r in range(1, nc)]

        def add_core(keep, send):
            return keep.astype(F32) + swap(send, "vec", nv, 1).astype(F32)

        def collect(chunks, beside):
            parts = [swap(chunks[r].astype(BF16), "vec", nv, 2 * r) for r in range(1, nq)]
            parts, beside = lax.optimization_barrier((parts, beside))
            return sum(part.astype(F32) for part in [chunks[0]] + parts), beside

        def share(x, beside):
            parts = [swap(x, "vec", nv, 2 * r) for r in range(1, nq)]
            parts, beside = lax.optimization_barrier((parts, beside))
            mine = jnp.concatenate([x] + parts)
            return [mine, swap(mine, "vec", nv, 1)], beside

        def split(fn, *counts):
            def kernel(*refs):
                groups, at = [], 0
                for count in counts:
                    groups.append(refs[at] if count == 0 else list(refs[at : at + count]))
                    at += max(count, 1)
                fn(*groups, *refs[at:])
            return kernel

        stats, cent = call(
            lambda *refs: first_stats(order, block, *refs),
            (shape(2, V), shape(K, D, dtype=BF16)),
            (ids, centroids, weights),
            [pltpu.VMEM((8, V), F32), pltpu.VMEM((1, 8, V), F32)],
            unit,
            [smem(), vmem(), vmem()],
        )
        stats = spread(stats)

        def sums(at):
            return call(
                split(lambda *refs: first_sums(at, block, nc, *refs), nc, 0, 0, 0, 0),
                (shape(nq, block + 16, D), shape(1, V)),
                (*stats, cent, weights),
                [strip],
                unit,
            )

        def rows_shape(kind):
            return [shape(V // nc, D, dtype=kind)] * nc

        def scatter(chunks):
            return [chunks[0]] + [swap(chunks[r], "cent", nc, r) for r in range(1, nc)]

        send, _ = sums(1)
        keep, lse = sums(0)

        def first_part(masks):
            return call(
                split(lambda *refs: first_rows(masks, *refs), 0, 0, 0, 0, len(masks)),
                [shape(V // nc, D, dtype=BF16)] * len(masks),
                (ids, cent, weights, lse),
                [pltpu.VMEM((K, V // nc), BF16)],
                unit,
                [smem()] + [vmem()] * 3,
            )

        first_cent = first_part(list(range(nc // 2)))
        chunks = add_core(keep, send)
        count = chunks[:, block]
        near = lax.reduce_precision(count, 8, 7)
        pair = jnp.stack([near, count - near], axis=1)
        chunks = jnp.concatenate([chunks[:, :block], pair, chunks[:, block + 2 :]], axis=1)
        chunk, first_cent = collect(chunks, first_cent)
        denom = chunk[block, :block] + chunk[block + 1, :block] + 1e-6
        moved, more = share(
            (chunk[:block] / denom[:, None]).astype(BF16), first_part(list(range(nc // 2, nc)))
        )
        first_cent = scatter([*first_cent, *more])

        stats = spread(call(
            split(second_stats, 2),
            shape(3, V),
            (*moved, weights, cotangent),
            [pltpu.VMEM((8, V), F32), pltpu.VMEM((2, 8, V), F32)],
        ))
        moved_cot = call(
            split(second_sums, nc, 2, 0, 0, 2),
            [shape(nq, block, D, dtype=BF16)] * 2,
            (*stats, *moved, weights, cotangent),
            [row, row, strip, strip],
            4 * unit,
        )
        span = V // 2

        def part(begin):
            return call(
                split(lambda *refs: second_part(begin, *refs), nc, 2),
                shape(D, span),
                (*stats, *moved, weights, cotangent),
                [row, row, pltpu.VMEM((K, span), BF16)],
                unit,
            )

        moved_cot, part_low = collect(add_core(*moved_cot), part(0))
        mean_cot, part_high = share((moved_cot / denom[:, None]).astype(BF16), part(span))

        stats, *grad_rows = call(
            split(third_rows, 0, 0, 2, 2, 0, 0, 2, 0, nc),
            [shape(2, V)] + rows_shape(BF16),
            (ids, cent, *moved, *mean_cot, weights, lse, part_low, part_high),
            [pltpu.VMEM((K, span), BF16)] * 2
            + [pltpu.VMEM((K, span), F32)] * 2
            + [pltpu.VMEM((2, 8, span), F32), pltpu.VMEM((V, D), F32)],
            4 * unit,
            [smem()] + [vmem()] * 9,
        )
        stats, first_cent = lax.optimization_barrier((stats, first_cent))
        stats = spread(stats)
        grad_rows = scatter(grad_rows)
        start_cot = call(
            split(third_sums, nc, 0, 2, 2, 0, 0, 2),
            [shape(nq, block, D, dtype=BF16)] * 2,
            (*stats, cent, *moved, *mean_cot, weights, lse),
            [row, strip],
            2 * unit,
        )
        far = nc // 2
        start_cot, grad_rows = lax.optimization_barrier((start_cot, grad_rows))
        size = V // nc
        mine = lax.axis_index("cent") * size
        own = [lax.dynamic_slice(x, (0, mine), (2, size)) for x in stats]
        dots = sum(x[0] for x in own)
        rows = sum(x.astype(F32) for x in grad_rows)
        rows = rows - sum((dots - x[1])[:, None] * f.astype(F32) for x, f in zip(own, first_cent))
        rows = spread(rows.astype(BF16))
        start_cot, rows[far] = collect(add_core(*start_cot), rows[far])
        start_cot, rows[nc - 1] = share(start_cot.astype(BF16), rows[nc - 1])
        start_cot = call(
            split(lambda *refs: place_blocks(order, 0, *refs), 0, 2),
            shape(K, D),
            (ids, *start_cot),
            specs=[smem()] + [vmem()] * 2,
        )
        grad_rows = jnp.zeros((V, D), BF16)
        for r in range(nc):
            at = jnp.bitwise_xor(lax.axis_index("cent"), r) * size
            grad_rows = lax.dynamic_update_slice(grad_rows, rows[r], (at, 0))
        return grad_rows, start_cot

    return local


def solution(mesh):
    return jax.shard_map(
        make_local(mesh.shape["vec"], mesh.shape["cent"]),
        mesh=mesh,
        in_specs=(P("vec", None), P("cent", None), P("vec", None)),
        out_specs=(P("vec", None), P("cent", None)),
        check_vma=False,
    )
```

```python
import jax
import jax.numpy as jnp
from jax import lax
from jax.experimental import pallas as pl
from jax.experimental.pallas import tpu as pltpu
from jax.sharding import PartitionSpec as P

F32 = jnp.float32
BF16 = jnp.bfloat16
STEP = 512


def vmem():
    return pl.BlockSpec(memory_space=pltpu.VMEM)


def call(kernel, outs, args, scratch=(), flops=0, mib=24):
    return pl.pallas_call(
        kernel,
        in_specs=[vmem()] * len(args),
        out_specs=jax.tree.map(lambda _: vmem(), outs),
        out_shape=outs,
        scratch_shapes=list(scratch),
        cost_estimate=pl.CostEstimate(flops=flops, bytes_accessed=2**22, transcendentals=0),
        compiler_params=pltpu.CompilerParams(vmem_limit_bytes=mib * 2**20),
    )(*args)


def shape(*dims, dtype=F32):
    return jax.ShapeDtypeStruct(dims, dtype)


def dot_nt(a, b):
    return lax.dot_general(a, b, (((1,), (1,)), ((), ())), preferred_element_type=F32)


def dot(a, b):
    return jnp.dot(a, b, preferred_element_type=F32)


def cut(total, step=STEP):
    step = min(step, total)
    return [slice(at, at + step) for at in range(0, total, step)]


def tiles(refs):
    start = 0
    for ref in refs:
        for rows in cut(ref.shape[0]):
            yield ref, rows, slice(start + rows.start, start + rows.stop)
        start += ref.shape[0]


def factor(block):
    scale = block.shape[1] ** (-0.5)
    block_f = block.astype(F32)
    square = jnp.sum(jnp.square(block_f), axis=1, keepdims=True) * scale
    return (block_f * (2.0 * scale)).astype(BF16), square


def lanes(x):
    total = x[:, 0:128]
    for at in range(128, x.shape[1], 128):
        total = total + x[:, at : at + 128]
    return total


def merge(stats):
    top = stats[0][0:1, :]
    for part in stats[1:]:
        top = jnp.maximum(top, part[0:1, :])
    weights = [jnp.exp(part[0:1, :] - top) for part in stats]
    total = sum(w * part[1:2, :] for w, part in zip(weights, stats))
    return top, total, weights


def online(out, top, sums, load):
    top[...] = jnp.full(top.shape, -jnp.inf, F32)
    sums[...] = jnp.zeros(sums.shape, F32)
    for score, cols, weight in load:
        score = score.reshape(score.shape[0] // 8, 8, score.shape[1])
        old = top[:, cols]
        new = jnp.maximum(old, jnp.max(score, axis=0))
        drop = jnp.exp(old - new)
        expo = jnp.exp(score - new[None])
        sums[0, :, cols] = sums[0, :, cols] * drop + jnp.sum(expo, axis=0)
        if weight is not None:
            expo = expo * weight.reshape(expo.shape)
            sums[1, :, cols] = sums[1, :, cols] * drop + jnp.sum(expo, axis=0)
        top[:, cols] = new
    peak = jnp.max(top[...], axis=0, keepdims=True)
    scale = jnp.exp(top[...] - peak)
    out[0:1, :] = peak
    for at in range(sums.shape[0]):
        out[at + 1 : at + 2, :] = jnp.sum(sums[at] * scale, axis=0, keepdims=True)


def first_stats(order, block, cent, rows, out, cent_rel, top, sums):
    for at, mask in enumerate(order):
        owner = jnp.bitwise_xor(lax.axis_index("vec"), mask)
        cent_rel[at * block : (at + 1) * block, :] = cent[pl.ds(pl.multiple_of(owner * block, block), block), :]

    def load():
        for rows_k in cut(cent_rel.shape[0]):
            lhs, square = factor(cent_rel[rows_k, :])
            for cols in cut(rows.shape[0]):
                yield dot_nt(lhs, rows[cols, :]) - square, cols, None

    online(out, top, sums, load())


def first_sums(half, block, parts, stats, cent, rows, out, lse, expo_b):
    peak, total, _ = merge(stats)
    lse[...] = peak + jnp.log(total)
    size = out.shape[0] * block
    per = max(1, min(STEP, size) // block)
    for at in range(0, out.shape[0], per):
        start = half * size + at * block
        lhs, square = factor(cent[start : start + per * block, :])
        count = jnp.zeros((per * block, 128), F32)
        for cols in cut(rows.shape[0]):
            expo = jnp.exp(dot_nt(lhs, rows[cols, :]) - square - lse[:, cols])
            count = count + lanes(expo)
            expo_b[:, cols] = expo.astype(BF16)
        mass = dot(expo_b[...], rows[...])
        for r in range(per):
            part = slice(r * block, (r + 1) * block)
            out[at + r, 0:block, :] = mass[part, :]
            out[at + r, block:, :] = jnp.zeros((out.shape[1] - block, out.shape[2]), F32)
            out[at + r, block : block + 1, 0:block] = jnp.sum(count[part, :].T, axis=0, keepdims=True)


def second_stats(moved, rows, cot, out, top, sums):
    def load():
        for ref, rows_k, _ in tiles(moved):
            block = ref[rows_k, :]
            lhs, square = factor(block)
            for cols in cut(rows.shape[0]):
                yield dot_nt(lhs, rows[cols, :]) - square, cols, dot_nt(block, cot[cols, :])

    online(out, top, sums, load())


def second_rows(stats, lse, dots, scale):
    peak, total, weights = merge(stats)
    lse[...] = peak + jnp.log(total)
    dots[...] = sum(w * part[2:3, :] for w, part in zip(weights, stats)) / total * scale


def put_owners(out, start, value):
    block = out.shape[1]
    per = value.shape[0] // block
    out[start // block : start // block + per] = value.reshape(per, block, value.shape[1]).astype(out.dtype)


def second_sums(stats, moved, rows, cot, outs, lse, dots, expo_b, edge_b):
    second_rows(stats, lse, dots, 2.0 * rows.shape[1] ** (-0.5))
    for ref, rows_k, _ in tiles(moved):
        block = ref[rows_k, :]
        lhs, square = factor(block)
        edges = jnp.zeros((block.shape[0], 128), F32)
        for cols in cut(rows.shape[0]):
            expo = jnp.exp(dot_nt(lhs, rows[cols, :]) - square - lse[:, cols])
            expo_b[:, cols] = expo.astype(BF16)
            edge = expo * (dot_nt(lhs, cot[cols, :]) - dots[:, cols])
            edges = edges + lanes(edge)
            edge_b[:, cols] = edge.astype(BF16)
        total = dot(expo_b[...], cot[...]) + dot(edge_b[...], rows[...])
        total = total - jnp.sum(edges, axis=1, keepdims=True) * block.astype(F32)
        put_owners(outs[0] if ref is moved[0] else outs[1], rows_k.start, total)


def second_part(begin, stats, moved, rows, cot, out, lse, dots, edge_b):
    second_rows(stats, lse, dots, 2.0 * rows.shape[1] ** (-0.5))
    for ref, rows_k, whole in tiles(moved):
        lhs, square = factor(ref[rows_k, :])
        for local in cut(out.shape[1]):
            cols = slice(begin + local.start, begin + local.stop)
            expo = jnp.exp(dot_nt(lhs, rows[cols, :]) - square - lse[:, cols])
            edge = expo * (dot_nt(lhs, cot[cols, :]) - dots[:, cols])
            edge_b[whole, local] = edge.astype(BF16)
    for local in cut(out.shape[1]):
        out[:, local] = sum(
            dot(ref[...].T, edge_b[at : at + ref.shape[0], local])
            for ref, at in zip(moved, (0, moved[0].shape[0]))
        )


def put_chunks(index, total, outs):
    size = total.shape[0] // len(outs)
    for r, out in enumerate(outs):
        at = jnp.bitwise_xor(index, r) * size
        out[...] = total[pl.ds(pl.multiple_of(at, size), size), :].astype(out.dtype)


def first_rows(masks, cent, rows, lse, outs, expo_b):
    cent_t = cent[...].T
    for mask, out in zip(masks, outs):
        size = out.shape[0]
        own = pl.ds(pl.multiple_of(jnp.bitwise_xor(lax.axis_index("cent"), mask) * size, size), size)
        chunk, shift = rows[own, :], lse[:, own]
        for whole in cut(cent.shape[0]):
            lhs, square = factor(cent[whole, :])
            expo_b[whole, :] = jnp.exp(dot_nt(lhs, chunk) - square - shift).astype(BF16)
        out[...] = dot(cent_t, expo_b[...]).T.astype(out.dtype)


def third_terms(cent, moved, mean_cot, rows, lse, cols_all):
    scale = 2.0 * rows.shape[1] ** (-0.5)
    for (mean_ref, rows_k, whole), (moved_ref, _, _) in zip(tiles(mean_cot), tiles(moved)):
        lhs, square = factor(cent[whole, :])
        mean = mean_ref[rows_k, :].astype(F32) * scale
        count_cot = -jnp.sum(mean * moved_ref[rows_k, :].astype(F32), axis=1, keepdims=True)
        mean = mean.astype(BF16)
        for cols in cols_all:
            expo = jnp.exp(dot_nt(lhs, rows[cols, :]) - square - lse[:, cols])
            yield whole, cols, expo, dot_nt(mean, rows[cols, :]) + count_cot


def third_rows(cent, moved, mean_cot, rows, lse, parts, stats, outs, expo_b, edge_b, expo_f, dfirst_f, sums, total):
    cent_t = cent[...].T
    halves = [(ref[...].T, at) for ref, at in zip(mean_cot, (0, mean_cot[0].shape[0]))]
    span = expo_f.shape[1]
    for begin, part in zip(range(0, rows.shape[0], span), parts):
        cols_all = [slice(begin + c.start, begin + c.stop) for c in cut(span)]
        sums[...] = jnp.zeros(sums.shape, F32)
        for whole, cols, expo, dfirst in third_terms(cent, moved, mean_cot, rows, lse, cols_all):
            local = slice(cols.start - begin, cols.stop - begin)
            expo_f[whole, local] = expo
            dfirst_f[whole, local] = dfirst
            expo_b[whole, local] = expo.astype(BF16)
            group = (expo.shape[0] // 8, 8, expo.shape[1])
            sums[0, :, local] = sums[0, :, local] + jnp.sum((expo * dfirst).reshape(group), axis=0)
            sums[1, :, local] = sums[1, :, local] + jnp.sum(expo.reshape(group), axis=0)
        dots = jnp.sum(sums[0], axis=0, keepdims=True)
        weight = jnp.sum(sums[1], axis=0, keepdims=True)
        mean = jnp.where(weight > 0.0, dots / jnp.where(weight > 0.0, weight, 1.0), 0.0)
        stats[0:1, begin : begin + span] = dots
        stats[1:2, begin : begin + span] = mean
        for local in cut(span):
            cols = slice(begin + local.start, begin + local.stop)
            for whole in cut(cent.shape[0]):
                edge = expo_f[whole, local] * (dfirst_f[whole, local] - mean[:, local])
                edge_b[whole, local] = edge.astype(BF16)
            value = part[:, local] + dot(cent_t, edge_b[:, local])
            for mean_t, at in halves:
                value = value + dot(mean_t, expo_b[at : at + mean_t.shape[1], local])
            total[cols, :] = value.T
    put_chunks(lax.axis_index("cent"), total, outs)


def third_sums(stats, cent, moved, mean_cot, rows, lse, outs, dots, edge_b):
    dots[...] = sum(ref[0:1, :] for ref in stats)
    edges = jnp.zeros((edge_b.shape[0], 128), F32)
    for whole, cols, expo, dfirst in third_terms(cent, moved, mean_cot, rows, lse, cut(rows.shape[0])):
        edge = expo * (dfirst - dots[:, cols])
        edges = edges + lanes(edge)
        edge_b[:, cols] = edge.astype(BF16)
        if cols.stop == rows.shape[0]:
            value = dot(edge_b[...], rows[...])
            value = value - jnp.sum(edges, axis=1, keepdims=True) * cent[whole, :].astype(F32)
            which, start = divmod(whole.start, cent.shape[0] // 2)
            put_owners(outs[which], start, value)
            edges = jnp.zeros(edges.shape, F32)


def place_blocks(order, axis, parts, out):
    at = 0
    for part in parts:
        block = out.shape[0] // len(order)
        for start in range(0, part.shape[0], block):
            owner = jnp.bitwise_xor(lax.axis_index(axis), order[at])
            out[pl.ds(pl.multiple_of(owner * block, block), block), :] = part[start : start + block, :].astype(out.dtype)
            at += 1


def swap(x, axis, n, mask):
    return lax.ppermute(x, axis, [(i, i ^ mask) for i in range(n)])


def make_local(nv, nc):
    nq = nv // 2
    order = [2 * r + a for a in range(2) for r in range(nq)]

    def local(weights, centroids, cotangent):
        V, D = weights.shape
        K = centroids.shape[0]
        block, half = K // nv, K // 2
        step = min(STEP, half)
        unit = 2 * K * V * D
        row = pltpu.VMEM((1, V), F32)
        strip = pltpu.VMEM((step, V), BF16)

        def spread(x):
            return [x] + [swap(x, "cent", nc, r) for r in range(1, nc)]

        def add_core(keep, send):
            return keep.astype(F32) + swap(send, "vec", nv, 1).astype(F32)

        def collect(chunks, beside):
            parts = [swap(chunks[r].astype(BF16), "vec", nv, 2 * r) for r in range(1, nq)]
            parts, beside = lax.optimization_barrier((parts, beside))
            return sum(part.astype(F32) for part in [chunks[0]] + parts), beside

        def share(x, beside):
            parts = [swap(x, "vec", nv, 2 * r) for r in range(1, nq)]
            parts, beside = lax.optimization_barrier((parts, beside))
            mine = jnp.concatenate([x] + parts)
            return [mine, swap(mine, "vec", nv, 1)], beside

        def split(fn, *counts):
            def kernel(*refs):
                groups, at = [], 0
                for count in counts:
                    groups.append(refs[at] if count == 0 else list(refs[at : at + count]))
                    at += max(count, 1)
                fn(*groups, *refs[at:])
            return kernel

        stats, cent = call(
            lambda *refs: first_stats(order, block, *refs),
            (shape(2, V), shape(K, D, dtype=BF16)),
            (centroids, weights),
            [pltpu.VMEM((8, V), F32), pltpu.VMEM((1, 8, V), F32)],
            unit,
        )
        stats = spread(stats)

        def sums(at):
            return call(
                split(lambda *refs: first_sums(at, block, nc, *refs), nc, 0, 0, 0, 0),
                (shape(nq, block + 16, D), shape(1, V)),
                (*stats, cent, weights),
                [strip],
                unit,
            )

        def rows_shape(kind):
            return [shape(V // nc, D, dtype=kind)] * nc

        def scatter(chunks):
            return [chunks[0]] + [swap(chunks[r], "cent", nc, r) for r in range(1, nc)]

        send, _ = sums(1)
        keep, lse = sums(0)

        def first_part(masks):
            return call(
                split(lambda *refs: first_rows(masks, *refs), 0, 0, 0, len(masks)),
                [shape(V // nc, D, dtype=BF16)] * len(masks),
                (cent, weights, lse),
                [pltpu.VMEM((K, V // nc), BF16)],
                unit,
            )

        first_cent = first_part(list(range(nc // 2)))
        chunks = add_core(keep, send)
        count = chunks[:, block]
        near = lax.reduce_precision(count, 8, 7)
        pair = jnp.stack([near, count - near], axis=1)
        chunks = jnp.concatenate([chunks[:, :block], pair, chunks[:, block + 2 :]], axis=1)
        chunk, first_cent = collect(chunks, first_cent)
        denom = chunk[block, :block] + chunk[block + 1, :block] + 1e-6
        moved, more = share(
            (chunk[:block] / denom[:, None]).astype(BF16), first_part(list(range(nc // 2, nc)))
        )
        first_cent = scatter([*first_cent, *more])

        stats = spread(call(
            split(second_stats, 2),
            shape(3, V),
            (*moved, weights, cotangent),
            [pltpu.VMEM((8, V), F32), pltpu.VMEM((2, 8, V), F32)],
        ))
        moved_cot = call(
            split(second_sums, nc, 2, 0, 0, 2),
            [shape(nq, block, D, dtype=BF16)] * 2,
            (*stats, *moved, weights, cotangent),
            [row, row, strip, strip],
            4 * unit,
        )
        span = V // 2

        def part(begin):
            return call(
                split(lambda *refs: second_part(begin, *refs), nc, 2),
                shape(D, span),
                (*stats, *moved, weights, cotangent),
                [row, row, pltpu.VMEM((K, span), BF16)],
                unit,
            )

        moved_cot, part_low = collect(add_core(*moved_cot), part(0))
        mean_cot, part_high = share((moved_cot / denom[:, None]).astype(BF16), part(span))

        stats, *grad_rows = call(
            split(third_rows, 0, 2, 2, 0, 0, 2, 0, nc),
            [shape(2, V)] + rows_shape(BF16),
            (cent, *moved, *mean_cot, weights, lse, part_low, part_high),
            [pltpu.VMEM((K, span), BF16)] * 2
            + [pltpu.VMEM((K, span), F32)] * 2
            + [pltpu.VMEM((2, 8, span), F32), pltpu.VMEM((V, D), F32)],
            4 * unit,
            44,
        )
        stats, first_cent = lax.optimization_barrier((stats, first_cent))
        stats = spread(stats)
        grad_rows = scatter(grad_rows)
        start_cot = call(
            split(third_sums, nc, 0, 2, 2, 0, 0, 2),
            [shape(nq, block, D, dtype=BF16)] * 2,
            (*stats, cent, *moved, *mean_cot, weights, lse),
            [row, strip],
            2 * unit,
        )
        far = nc // 2
        start_cot, grad_rows = lax.optimization_barrier((start_cot, grad_rows))
        size = V // nc
        mine = lax.axis_index("cent") * size
        own = [lax.dynamic_slice(x, (0, mine), (2, size)) for x in stats]
        dots = sum(x[0] for x in own)
        rows = sum(x.astype(F32) for x in grad_rows)
        rows = rows - sum((dots - x[1])[:, None] * f.astype(F32) for x, f in zip(own, first_cent))
        rows = spread(rows.astype(BF16))
        start_cot, _ = collect(add_core(*start_cot), ())
        start_cot, rows[far:] = share(start_cot.astype(BF16), rows[far:])
        start_cot = call(
            split(lambda *refs: place_blocks(order, "vec", *refs), 2),
            shape(K, D),
            start_cot,
        )
        grad_rows = jnp.zeros((V, D), BF16)
        for r in range(nc):
            at = jnp.bitwise_xor(lax.axis_index("cent"), r) * size
            grad_rows = lax.dynamic_update_slice(grad_rows, rows[r], (at, 0))
        return grad_rows, start_cot

    return local


def solution(mesh):
    return jax.shard_map(
        make_local(mesh.shape["vec"], mesh.shape["cent"]),
        mesh=mesh,
        in_specs=(P("vec", None), P("cent", None), P("vec", None)),
        out_specs=(P("vec", None), P("cent", None)),
        check_vma=False,
    )
```

```python
import jax
import jax.numpy as jnp
from jax import lax
from jax.experimental import pallas as pl
from jax.experimental.pallas import tpu as pltpu
from jax.sharding import PartitionSpec as P

F32 = jnp.float32
BF16 = jnp.bfloat16
STEP = 512


def vmem():
    return pl.BlockSpec(memory_space=pltpu.VMEM)


def call(kernel, outs, args, scratch=(), flops=0, mib=24):
    return pl.pallas_call(
        kernel,
        in_specs=[vmem()] * len(args),
        out_specs=jax.tree.map(lambda _: vmem(), outs),
        out_shape=outs,
        scratch_shapes=list(scratch),
        cost_estimate=pl.CostEstimate(flops=flops, bytes_accessed=2**22, transcendentals=0),
        compiler_params=pltpu.CompilerParams(vmem_limit_bytes=mib * 2**20),
    )(*args)


def shape(*dims, dtype=F32):
    return jax.ShapeDtypeStruct(dims, dtype)


def dot_nt(a, b):
    return lax.dot_general(a, b, (((1,), (1,)), ((), ())), preferred_element_type=F32)


def dot(a, b):
    return jnp.dot(a, b, preferred_element_type=F32)


def cut(total, step=STEP):
    step = min(step, total)
    return [slice(at, at + step) for at in range(0, total, step)]


def tiles(refs):
    start = 0
    for ref in refs:
        for rows in cut(ref.shape[0]):
            yield ref, rows, slice(start + rows.start, start + rows.stop)
        start += ref.shape[0]


def factor(block):
    scale = block.shape[1] ** (-0.5)
    block_f = block.astype(F32)
    square = jnp.sum(jnp.square(block_f), axis=1, keepdims=True) * scale
    return (block_f * (2.0 * scale)).astype(BF16), square


def lanes(x):
    total = x[:, 0:128]
    for at in range(128, x.shape[1], 128):
        total = total + x[:, at : at + 128]
    return total


def merge(stats):
    top = stats[0][0:1, :]
    for part in stats[1:]:
        top = jnp.maximum(top, part[0:1, :])
    weights = [jnp.exp(part[0:1, :] - top) for part in stats]
    total = sum(w * part[1:2, :] for w, part in zip(weights, stats))
    return top, total, weights


def online(out, top, sums, load):
    top[...] = jnp.full(top.shape, -jnp.inf, F32)
    sums[...] = jnp.zeros(sums.shape, F32)
    for score, cols, weight in load:
        score = score.reshape(score.shape[0] // 8, 8, score.shape[1])
        old = top[:, cols]
        new = jnp.maximum(old, jnp.max(score, axis=0))
        drop = jnp.exp(old - new)
        expo = jnp.exp(score - new[None])
        sums[0, :, cols] = sums[0, :, cols] * drop + jnp.sum(expo, axis=0)
        if weight is not None:
            expo = expo * weight.reshape(expo.shape)
            sums[1, :, cols] = sums[1, :, cols] * drop + jnp.sum(expo, axis=0)
        top[:, cols] = new
    peak = jnp.max(top[...], axis=0, keepdims=True)
    scale = jnp.exp(top[...] - peak)
    out[0:1, :] = peak
    for at in range(sums.shape[0]):
        out[at + 1 : at + 2, :] = jnp.sum(sums[at] * scale, axis=0, keepdims=True)


def first_stats(order, block, cent, rows, out, cent_rel, top, sums):
    for at, mask in enumerate(order):
        owner = jnp.bitwise_xor(lax.axis_index("vec"), mask)
        cent_rel[at * block : (at + 1) * block, :] = cent[pl.ds(pl.multiple_of(owner * block, block), block), :]

    def load():
        for rows_k in cut(cent_rel.shape[0]):
            lhs, square = factor(cent_rel[rows_k, :])
            for cols in cut(rows.shape[0]):
                yield dot_nt(lhs, rows[cols, :]) - square, cols, None

    online(out, top, sums, load())


def first_sums(half, block, parts, stats, cent, rows, out, lse, expo_b):
    peak, total, _ = merge(stats)
    lse[...] = peak + jnp.log(total)
    size = out.shape[0] * block
    per = max(1, min(STEP, size) // block)
    for at in range(0, out.shape[0], per):
        start = half * size + at * block
        lhs, square = factor(cent[start : start + per * block, :])
        count = jnp.zeros((per * block, 128), F32)
        for cols in cut(rows.shape[0]):
            expo = jnp.exp(dot_nt(lhs, rows[cols, :]) - square - lse[:, cols])
            count = count + lanes(expo)
            expo_b[:, cols] = expo.astype(BF16)
        mass = dot(expo_b[...], rows[...])
        for r in range(per):
            part = slice(r * block, (r + 1) * block)
            out[at + r, 0:block, :] = mass[part, :]
            out[at + r, block:, :] = jnp.zeros((out.shape[1] - block, out.shape[2]), F32)
            out[at + r, block : block + 1, 0:block] = jnp.sum(count[part, :].T, axis=0, keepdims=True)


def second_stats(moved, rows, cot, out, top, sums):
    def load():
        for ref, rows_k, _ in tiles(moved):
            block = ref[rows_k, :]
            lhs, square = factor(block)
            for cols in cut(rows.shape[0]):
                yield dot_nt(lhs, rows[cols, :]) - square, cols, dot_nt(block, cot[cols, :])

    online(out, top, sums, load())


def second_rows(stats, lse, dots, scale):
    peak, total, weights = merge(stats)
    lse[...] = peak + jnp.log(total)
    dots[...] = sum(w * part[2:3, :] for w, part in zip(weights, stats)) / total * scale


def put_owners(out, start, value):
    block = out.shape[1]
    per = value.shape[0] // block
    out[start // block : start // block + per] = value.reshape(per, block, value.shape[1]).astype(out.dtype)


def second_sums(stats, moved, rows, cot, outs, lse, dots, expo_b, edge_b):
    second_rows(stats, lse, dots, 2.0 * rows.shape[1] ** (-0.5))
    for ref, rows_k, _ in tiles(moved):
        block = ref[rows_k, :]
        lhs, square = factor(block)
        edges = jnp.zeros((block.shape[0], 128), F32)
        for cols in cut(rows.shape[0]):
            expo = jnp.exp(dot_nt(lhs, rows[cols, :]) - square - lse[:, cols])
            expo_b[:, cols] = expo.astype(BF16)
            edge = expo * (dot_nt(lhs, cot[cols, :]) - dots[:, cols])
            edges = edges + lanes(edge)
            edge_b[:, cols] = edge.astype(BF16)
        total = dot(expo_b[...], cot[...]) + dot(edge_b[...], rows[...])
        total = total - jnp.sum(edges, axis=1, keepdims=True) * block.astype(F32)
        put_owners(outs[0] if ref is moved[0] else outs[1], rows_k.start, total)


def second_part(begin, stats, moved, rows, cot, out, lse, dots, edge_b):
    second_rows(stats, lse, dots, 2.0 * rows.shape[1] ** (-0.5))
    for ref, rows_k, whole in tiles(moved):
        lhs, square = factor(ref[rows_k, :])
        for local in cut(out.shape[1]):
            cols = slice(begin + local.start, begin + local.stop)
            expo = jnp.exp(dot_nt(lhs, rows[cols, :]) - square - lse[:, cols])
            edge = expo * (dot_nt(lhs, cot[cols, :]) - dots[:, cols])
            edge_b[whole, local] = edge.astype(BF16)
    for local in cut(out.shape[1]):
        out[:, local] = sum(
            dot(ref[...].T, edge_b[at : at + ref.shape[0], local])
            for ref, at in zip(moved, (0, moved[0].shape[0]))
        )


def put_chunks(index, total, outs):
    size = total.shape[0] // len(outs)
    for r, out in enumerate(outs):
        at = jnp.bitwise_xor(index, r) * size
        out[...] = total[pl.ds(pl.multiple_of(at, size), size), :].astype(out.dtype)


def first_rows(masks, cent, rows, lse, outs, expo_b):
    cent_t = cent[...].T
    for mask, out in zip(masks, outs):
        size = out.shape[0]
        own = pl.ds(pl.multiple_of(jnp.bitwise_xor(lax.axis_index("cent"), mask) * size, size), size)
        chunk, shift = rows[own, :], lse[:, own]
        for whole in cut(cent.shape[0]):
            lhs, square = factor(cent[whole, :])
            expo_b[whole, :] = jnp.exp(dot_nt(lhs, chunk) - square - shift).astype(BF16)
        out[...] = dot(cent_t, expo_b[...]).T.astype(out.dtype)


def third_terms(cent, moved, mean_cot, rows, lse, cols_all):
    scale = 2.0 * rows.shape[1] ** (-0.5)
    for (mean_ref, rows_k, whole), (moved_ref, _, _) in zip(tiles(mean_cot), tiles(moved)):
        lhs, square = factor(cent[whole, :])
        mean = mean_ref[rows_k, :].astype(F32) * scale
        count_cot = -jnp.sum(mean * moved_ref[rows_k, :].astype(F32), axis=1, keepdims=True)
        mean = mean.astype(BF16)
        for cols in cols_all:
            expo = jnp.exp(dot_nt(lhs, rows[cols, :]) - square - lse[:, cols])
            yield whole, cols, expo, dot_nt(mean, rows[cols, :]) + count_cot


def third_rows(cent, moved, mean_cot, rows, lse, parts, stats, outs, expo_b, edge_b, expo_f, dfirst_f, sums, total):
    cent_t = cent[...].T
    halves = [(ref[...].T, at) for ref, at in zip(mean_cot, (0, mean_cot[0].shape[0]))]
    span = expo_f.shape[1]
    for begin, part in zip(range(0, rows.shape[0], span), parts):
        cols_all = [slice(begin + c.start, begin + c.stop) for c in cut(span)]
        sums[...] = jnp.zeros(sums.shape, F32)
        for whole, cols, expo, dfirst in third_terms(cent, moved, mean_cot, rows, lse, cols_all):
            local = slice(cols.start - begin, cols.stop - begin)
            expo_f[whole, local] = expo
            dfirst_f[whole, local] = dfirst
            expo_b[whole, local] = expo.astype(BF16)
            group = (expo.shape[0] // 8, 8, expo.shape[1])
            sums[0, :, local] = sums[0, :, local] + jnp.sum((expo * dfirst).reshape(group), axis=0)
            sums[1, :, local] = sums[1, :, local] + jnp.sum(expo.reshape(group), axis=0)
        dots = jnp.sum(sums[0], axis=0, keepdims=True)
        weight = jnp.sum(sums[1], axis=0, keepdims=True)
        mean = jnp.where(weight > 0.0, dots / jnp.where(weight > 0.0, weight, 1.0), 0.0)
        stats[0:1, begin : begin + span] = dots
        stats[1:2, begin : begin + span] = mean
        for local in cut(span):
            cols = slice(begin + local.start, begin + local.stop)
            for whole in cut(cent.shape[0]):
                edge = expo_f[whole, local] * (dfirst_f[whole, local] - mean[:, local])
                edge_b[whole, local] = edge.astype(BF16)
            value = part[:, local] + dot(cent_t, edge_b[:, local])
            for mean_t, at in halves:
                value = value + dot(mean_t, expo_b[at : at + mean_t.shape[1], local])
            total[cols, :] = value.T
    put_chunks(lax.axis_index("cent"), total, outs)


def third_sums(stats, cent, moved, mean_cot, rows, lse, outs, dots, edge_b):
    dots[...] = sum(ref[0:1, :] for ref in stats)
    edges = jnp.zeros((edge_b.shape[0], 128), F32)
    for whole, cols, expo, dfirst in third_terms(cent, moved, mean_cot, rows, lse, cut(rows.shape[0])):
        edge = expo * (dfirst - dots[:, cols])
        edges = edges + lanes(edge)
        edge_b[:, cols] = edge.astype(BF16)
        if cols.stop == rows.shape[0]:
            value = dot(edge_b[...], rows[...])
            value = value - jnp.sum(edges, axis=1, keepdims=True) * cent[whole, :].astype(F32)
            which, start = divmod(whole.start, cent.shape[0] // 2)
            put_owners(outs[which], start, value)
            edges = jnp.zeros(edges.shape, F32)


def place_blocks(order, axis, parts, out):
    at = 0
    for part in parts:
        block = out.shape[0] // len(order)
        for start in range(0, part.shape[0], block):
            owner = jnp.bitwise_xor(lax.axis_index(axis), order[at])
            out[pl.ds(pl.multiple_of(owner * block, block), block), :] = part[start : start + block, :].astype(out.dtype)
            at += 1


def swap(x, axis, n, mask):
    return lax.ppermute(x, axis, [(i, i ^ mask) for i in range(n)])


def make_local(nv, nc):
    nq = nv // 2
    order = [2 * r + a for a in range(2) for r in range(nq)]

    def local(weights, centroids, cotangent):
        V, D = weights.shape
        K = centroids.shape[0]
        block, half = K // nv, K // 2
        step = min(STEP, half)
        unit = 2 * K * V * D
        row = pltpu.VMEM((1, V), F32)
        strip = pltpu.VMEM((step, V), BF16)

        def spread(x):
            return [x] + [swap(x, "cent", nc, r) for r in range(1, nc)]

        def add_core(keep, send):
            return keep.astype(F32) + swap(send, "vec", nv, 1).astype(F32)

        def collect(chunks, beside):
            parts = [swap(chunks[r].astype(BF16), "vec", nv, 2 * r) for r in range(1, nq)]
            parts, beside = lax.optimization_barrier((parts, beside))
            return sum(part.astype(F32) for part in [chunks[0]] + parts), beside

        def share(x, beside):
            parts = [swap(x, "vec", nv, 2 * r) for r in range(1, nq)]
            parts, beside = lax.optimization_barrier((parts, beside))
            mine = jnp.concatenate([x] + parts)
            return [mine, swap(mine, "vec", nv, 1)], beside

        def split(fn, *counts):
            def kernel(*refs):
                groups, at = [], 0
                for count in counts:
                    groups.append(refs[at] if count == 0 else list(refs[at : at + count]))
                    at += max(count, 1)
                fn(*groups, *refs[at:])
            return kernel

        stats, cent = call(
            lambda *refs: first_stats(order, block, *refs),
            (shape(2, V), shape(K, D, dtype=BF16)),
            (centroids, weights),
            [pltpu.VMEM((8, V), F32), pltpu.VMEM((1, 8, V), F32)],
            unit,
        )
        stats = spread(stats)

        def sums(at):
            return call(
                split(lambda *refs: first_sums(at, block, nc, *refs), nc, 0, 0, 0, 0),
                (shape(nq, block + 16, D), shape(1, V)),
                (*stats, cent, weights),
                [strip],
                unit,
            )

        def rows_shape(kind):
            return [shape(V // nc, D, dtype=kind)] * nc

        def scatter(chunks):
            return [chunks[0]] + [swap(chunks[r], "cent", nc, r) for r in range(1, nc)]

        send, _ = sums(1)
        keep, lse = sums(0)

        def first_part(masks):
            return call(
                split(lambda *refs: first_rows(masks, *refs), 0, 0, 0, len(masks)),
                [shape(V // nc, D, dtype=BF16)] * len(masks),
                (cent, weights, lse),
                [pltpu.VMEM((K, V // nc), BF16)],
                unit,
            )

        first_cent = first_part(list(range(nc // 2)))
        chunks = add_core(keep, send)
        count = chunks[:, block]
        near = lax.reduce_precision(count, 8, 7)
        pair = jnp.stack([near, count - near], axis=1)
        chunks = jnp.concatenate([chunks[:, :block], pair, chunks[:, block + 2 :]], axis=1)
        chunk, first_cent = collect(chunks, first_cent)
        denom = chunk[block, :block] + chunk[block + 1, :block] + 1e-6
        moved, more = share(
            (chunk[:block] / denom[:, None]).astype(BF16), first_part(list(range(nc // 2, nc)))
        )
        first_cent = scatter([*first_cent, *more])

        stats = spread(call(
            split(second_stats, 2),
            shape(3, V),
            (*moved, weights, cotangent),
            [pltpu.VMEM((8, V), F32), pltpu.VMEM((2, 8, V), F32)],
        ))
        moved_cot = call(
            split(second_sums, nc, 2, 0, 0, 2),
            [shape(nq, block, D, dtype=BF16)] * 2,
            (*stats, *moved, weights, cotangent),
            [row, row, strip, strip],
            4 * unit,
        )
        span = V // 2

        def part(begin):
            return call(
                split(lambda *refs: second_part(begin, *refs), nc, 2),
                shape(D, span),
                (*stats, *moved, weights, cotangent),
                [row, row, pltpu.VMEM((K, span), BF16)],
                unit,
            )

        far = nc // 2
        moved_cot, (part_low, first_cent[1:far]) = collect(add_core(*moved_cot), (part(0), first_cent[1:far]))
        mean_cot, (part_high, first_cent[far:-1]) = share(
            (moved_cot / denom[:, None]).astype(BF16), (part(span), first_cent[far:-1])
        )

        stats, *grad_rows = call(
            split(third_rows, 0, 2, 2, 0, 0, 2, 0, nc),
            [shape(2, V)] + rows_shape(BF16),
            (cent, *moved, *mean_cot, weights, lse, part_low, part_high),
            [pltpu.VMEM((K, span), BF16)] * 2
            + [pltpu.VMEM((K, span), F32)] * 2
            + [pltpu.VMEM((2, 8, span), F32), pltpu.VMEM((V, D), F32)],
            4 * unit,
            44,
        )
        stats, first_cent[-1] = lax.optimization_barrier((stats, first_cent[-1]))
        stats = spread(stats)
        grad_rows = scatter(grad_rows)
        start_cot = call(
            split(third_sums, nc, 0, 2, 2, 0, 0, 2),
            [shape(nq, block, D, dtype=BF16)] * 2,
            (*stats, cent, *moved, *mean_cot, weights, lse),
            [row, strip],
            2 * unit,
        )
        start_cot, grad_rows = lax.optimization_barrier((start_cot, grad_rows))
        size = V // nc
        mine = lax.axis_index("cent") * size
        own = [lax.dynamic_slice(x, (0, mine), (2, size)) for x in stats]
        dots = sum(x[0] for x in own)
        rows = sum(x.astype(F32) for x in grad_rows)
        rows = rows - sum((dots - x[1])[:, None] * f.astype(F32) for x, f in zip(own, first_cent))
        rows = spread(rows.astype(BF16))
        start_cot, _ = collect(add_core(*start_cot), ())
        start_cot, rows = share(start_cot.astype(BF16), rows)
        start_cot = call(
            split(lambda *refs: place_blocks(order, "vec", *refs), 2),
            shape(K, D),
            start_cot,
        )
        grad_rows = jnp.zeros((V, D), BF16)
        for r in range(nc):
            at = jnp.bitwise_xor(lax.axis_index("cent"), r) * size
            grad_rows = lax.dynamic_update_slice(grad_rows, rows[r], (at, 0))
        return grad_rows, start_cot

    return local


def solution(mesh):
    return jax.shard_map(
        make_local(mesh.shape["vec"], mesh.shape["cent"]),
        mesh=mesh,
        in_specs=(P("vec", None), P("cent", None), P("vec", None)),
        out_specs=(P("vec", None), P("cent", None)),
        check_vma=False,
    )
```

```python
import jax
import jax.numpy as jnp
from jax import lax
from jax.experimental import pallas as pl
from jax.experimental.pallas import tpu as pltpu
from jax.sharding import PartitionSpec as P

F32 = jnp.float32
BF16 = jnp.bfloat16
STEP = 512


def vmem():
    return pl.BlockSpec(memory_space=pltpu.VMEM)


def call(kernel, outs, args, scratch=(), flops=0, mib=24):
    return pl.pallas_call(
        kernel,
        in_specs=[vmem()] * len(args),
        out_specs=jax.tree.map(lambda _: vmem(), outs),
        out_shape=outs,
        scratch_shapes=list(scratch),
        cost_estimate=pl.CostEstimate(flops=flops, bytes_accessed=2**22, transcendentals=0),
        compiler_params=pltpu.CompilerParams(vmem_limit_bytes=mib * 2**20),
    )(*args)


def shape(*dims, dtype=F32):
    return jax.ShapeDtypeStruct(dims, dtype)


def dot_nt(a, b):
    return lax.dot_general(a, b, (((1,), (1,)), ((), ())), preferred_element_type=F32)


def dot(a, b):
    return jnp.dot(a, b, preferred_element_type=F32)


def cut(total, step=STEP):
    step = min(step, total)
    return [slice(at, at + step) for at in range(0, total, step)]


def tiles(refs):
    start = 0
    for ref in refs:
        for rows in cut(ref.shape[0]):
            yield ref, rows, slice(start + rows.start, start + rows.stop)
        start += ref.shape[0]


def factor(block):
    scale = block.shape[1] ** (-0.5)
    block_f = block.astype(F32)
    square = jnp.sum(jnp.square(block_f), axis=1, keepdims=True) * scale
    return (block_f * (2.0 * scale)).astype(BF16), square


def lanes(x):
    total = x[:, 0:128]
    for at in range(128, x.shape[1], 128):
        total = total + x[:, at : at + 128]
    return total


def merge(stats):
    top = stats[0][0:1, :]
    for part in stats[1:]:
        top = jnp.maximum(top, part[0:1, :])
    weights = [jnp.exp(part[0:1, :] - top) for part in stats]
    total = sum(w * part[1:2, :] for w, part in zip(weights, stats))
    return top, total, weights


def online(out, top, sums, load):
    top[...] = jnp.full(top.shape, -jnp.inf, F32)
    sums[...] = jnp.zeros(sums.shape, F32)
    for score, cols, weight in load:
        score = score.reshape(score.shape[0] // 8, 8, score.shape[1])
        old = top[:, cols]
        new = jnp.maximum(old, jnp.max(score, axis=0))
        drop = jnp.exp(old - new)
        expo = jnp.exp(score - new[None])
        sums[0, :, cols] = sums[0, :, cols] * drop + jnp.sum(expo, axis=0)
        if weight is not None:
            expo = expo * weight.reshape(expo.shape)
            sums[1, :, cols] = sums[1, :, cols] * drop + jnp.sum(expo, axis=0)
        top[:, cols] = new
    peak = jnp.max(top[...], axis=0, keepdims=True)
    scale = jnp.exp(top[...] - peak)
    out[0:1, :] = peak
    for at in range(sums.shape[0]):
        out[at + 1 : at + 2, :] = jnp.sum(sums[at] * scale, axis=0, keepdims=True)


def first_stats(order, block, cent, rows, out, cent_rel, top, sums):
    for at, mask in enumerate(order):
        owner = jnp.bitwise_xor(lax.axis_index("vec"), mask)
        cent_rel[at * block : (at + 1) * block, :] = cent[pl.ds(pl.multiple_of(owner * block, block), block), :]

    def load():
        for rows_k in cut(cent_rel.shape[0]):
            lhs, square = factor(cent_rel[rows_k, :])
            for cols in cut(rows.shape[0]):
                yield dot_nt(lhs, rows[cols, :]) - square, cols, None

    online(out, top, sums, load())


def first_sums(half, block, parts, stats, cent, rows, out, lse, expo_b):
    peak, total, _ = merge(stats)
    lse[...] = peak + jnp.log(total)
    size = out.shape[0] * block
    per = max(1, min(STEP, size) // block)
    for at in range(0, out.shape[0], per):
        start = half * size + at * block
        lhs, square = factor(cent[start : start + per * block, :])
        count = jnp.zeros((per * block, 128), F32)
        for cols in cut(rows.shape[0]):
            expo = jnp.exp(dot_nt(lhs, rows[cols, :]) - square - lse[:, cols])
            count = count + lanes(expo)
            expo_b[:, cols] = expo.astype(BF16)
        mass = dot(expo_b[...], rows[...])
        for r in range(per):
            part = slice(r * block, (r + 1) * block)
            out[at + r, 0:block, :] = mass[part, :]
            out[at + r, block:, :] = jnp.zeros((out.shape[1] - block, out.shape[2]), F32)
            out[at + r, block : block + 1, 0:block] = jnp.sum(count[part, :].T, axis=0, keepdims=True)


def second_stats(moved, rows, cot, out, top, sums):
    def load():
        for ref, rows_k, _ in tiles(moved):
            block = ref[rows_k, :]
            lhs, square = factor(block)
            for cols in cut(rows.shape[0]):
                yield dot_nt(lhs, rows[cols, :]) - square, cols, dot_nt(block, cot[cols, :])

    online(out, top, sums, load())


def second_rows(stats, lse, dots, scale):
    peak, total, weights = merge(stats)
    lse[...] = peak + jnp.log(total)
    dots[...] = sum(w * part[2:3, :] for w, part in zip(weights, stats)) / total * scale


def put_owners(out, start, value):
    block = out.shape[1]
    per = value.shape[0] // block
    out[start // block : start // block + per] = value.reshape(per, block, value.shape[1]).astype(out.dtype)


def second_sums(stats, moved, rows, cot, out, lse, dots, expo_b, edge_b):
    second_rows(stats, lse, dots, 2.0 * rows.shape[1] ** (-0.5))
    for rows_k in cut(moved.shape[0]):
        block = moved[rows_k, :]
        lhs, square = factor(block)
        edges = jnp.zeros((block.shape[0], 128), F32)
        for cols in cut(rows.shape[0]):
            expo = jnp.exp(dot_nt(lhs, rows[cols, :]) - square - lse[:, cols])
            expo_b[:, cols] = expo.astype(BF16)
            edge = expo * (dot_nt(lhs, cot[cols, :]) - dots[:, cols])
            edges = edges + lanes(edge)
            edge_b[:, cols] = edge.astype(BF16)
        total = dot(expo_b[...], cot[...]) + dot(edge_b[...], rows[...])
        total = total - jnp.sum(edges, axis=1, keepdims=True) * block.astype(F32)
        put_owners(out, rows_k.start, total)


def second_part(begin, stats, moved, rows, cot, out, lse, dots, edge_b):
    second_rows(stats, lse, dots, 2.0 * rows.shape[1] ** (-0.5))
    for ref, rows_k, whole in tiles(moved):
        lhs, square = factor(ref[rows_k, :])
        for local in cut(out.shape[1]):
            cols = slice(begin + local.start, begin + local.stop)
            expo = jnp.exp(dot_nt(lhs, rows[cols, :]) - square - lse[:, cols])
            edge = expo * (dot_nt(lhs, cot[cols, :]) - dots[:, cols])
            edge_b[whole, local] = edge.astype(BF16)
    for local in cut(out.shape[1]):
        out[:, local] = sum(
            dot(ref[...].T, edge_b[at : at + ref.shape[0], local])
            for ref, at in zip(moved, (0, moved[0].shape[0]))
        )


def put_chunks(index, total, outs):
    size = total.shape[0] // len(outs)
    for r, out in enumerate(outs):
        at = jnp.bitwise_xor(index, r) * size
        out[...] = total[pl.ds(pl.multiple_of(at, size), size), :].astype(out.dtype)


def first_rows(masks, cent, rows, lse, outs, expo_b):
    cent_t = cent[...].T
    for mask, out in zip(masks, outs):
        size = out.shape[0]
        own = pl.ds(pl.multiple_of(jnp.bitwise_xor(lax.axis_index("cent"), mask) * size, size), size)
        chunk, shift = rows[own, :], lse[:, own]
        for whole in cut(cent.shape[0]):
            lhs, square = factor(cent[whole, :])
            expo_b[whole, :] = jnp.exp(dot_nt(lhs, chunk) - square - shift).astype(BF16)
        out[...] = dot(cent_t, expo_b[...]).T.astype(out.dtype)


def third_terms(cent, moved, mean_cot, rows, lse, cols_all):
    scale = 2.0 * rows.shape[1] ** (-0.5)
    for (mean_ref, rows_k, whole), (moved_ref, _, _) in zip(tiles(mean_cot), tiles(moved)):
        lhs, square = factor(cent[whole, :])
        mean = mean_ref[rows_k, :].astype(F32) * scale
        count_cot = -jnp.sum(mean * moved_ref[rows_k, :].astype(F32), axis=1, keepdims=True)
        mean = mean.astype(BF16)
        for cols in cols_all:
            expo = jnp.exp(dot_nt(lhs, rows[cols, :]) - square - lse[:, cols])
            yield whole, cols, expo, dot_nt(mean, rows[cols, :]) + count_cot


def third_rows(cent, moved, mean_cot, rows, lse, parts, stats, outs, expo_b, edge_b, expo_f, dfirst_f, sums, total):
    cent_t = cent[...].T
    halves = [(ref[...].T, at) for ref, at in zip(mean_cot, (0, mean_cot[0].shape[0]))]
    span = expo_f.shape[1]
    for begin, part in zip(range(0, rows.shape[0], span), parts):
        cols_all = [slice(begin + c.start, begin + c.stop) for c in cut(span)]
        sums[...] = jnp.zeros(sums.shape, F32)
        for whole, cols, expo, dfirst in third_terms(cent, moved, mean_cot, rows, lse, cols_all):
            local = slice(cols.start - begin, cols.stop - begin)
            expo_f[whole, local] = expo
            dfirst_f[whole, local] = dfirst
            expo_b[whole, local] = expo.astype(BF16)
            group = (expo.shape[0] // 8, 8, expo.shape[1])
            sums[0, :, local] = sums[0, :, local] + jnp.sum((expo * dfirst).reshape(group), axis=0)
            sums[1, :, local] = sums[1, :, local] + jnp.sum(expo.reshape(group), axis=0)
        dots = jnp.sum(sums[0], axis=0, keepdims=True)
        weight = jnp.sum(sums[1], axis=0, keepdims=True)
        mean = jnp.where(weight > 0.0, dots / jnp.where(weight > 0.0, weight, 1.0), 0.0)
        stats[0:1, begin : begin + span] = dots
        stats[1:2, begin : begin + span] = mean
        for local in cut(span):
            cols = slice(begin + local.start, begin + local.stop)
            for whole in cut(cent.shape[0]):
                edge = expo_f[whole, local] * (dfirst_f[whole, local] - mean[:, local])
                edge_b[whole, local] = edge.astype(BF16)
            value = part[:, local] + dot(cent_t, edge_b[:, local])
            for mean_t, at in halves:
                value = value + dot(mean_t, expo_b[at : at + mean_t.shape[1], local])
            total[cols, :] = value.T
    put_chunks(lax.axis_index("cent"), total, outs)


def third_sums(stats, cent, moved, mean_cot, rows, lse, outs, dots, edge_b):
    dots[...] = sum(ref[0:1, :] for ref in stats)
    edges = jnp.zeros((edge_b.shape[0], 128), F32)
    for whole, cols, expo, dfirst in third_terms(cent, moved, mean_cot, rows, lse, cut(rows.shape[0])):
        edge = expo * (dfirst - dots[:, cols])
        edges = edges + lanes(edge)
        edge_b[:, cols] = edge.astype(BF16)
        if cols.stop == rows.shape[0]:
            value = dot(edge_b[...], rows[...])
            value = value - jnp.sum(edges, axis=1, keepdims=True) * cent[whole, :].astype(F32)
            which, start = divmod(whole.start, cent.shape[0] // 2)
            put_owners(outs[which], start, value)
            edges = jnp.zeros(edges.shape, F32)


def place_blocks(order, axis, parts, out):
    at = 0
    for part in parts:
        block = out.shape[0] // len(order)
        for start in range(0, part.shape[0], block):
            owner = jnp.bitwise_xor(lax.axis_index(axis), order[at])
            out[pl.ds(pl.multiple_of(owner * block, block), block), :] = part[start : start + block, :].astype(out.dtype)
            at += 1


def swap(x, axis, n, mask):
    return lax.ppermute(x, axis, [(i, i ^ mask) for i in range(n)])


def make_local(nv, nc):
    nq = nv // 2
    order = [2 * r + a for a in range(2) for r in range(nq)]

    def local(weights, centroids, cotangent):
        V, D = weights.shape
        K = centroids.shape[0]
        block, half = K // nv, K // 2
        step = min(STEP, half)
        unit = 2 * K * V * D
        row = pltpu.VMEM((1, V), F32)
        strip = pltpu.VMEM((step, V), BF16)

        def spread(x):
            return [x] + [swap(x, "cent", nc, r) for r in range(1, nc)]

        def add_core(keep, send):
            return keep.astype(F32) + swap(send, "vec", nv, 1).astype(F32)

        def collect(chunks, beside):
            parts = [swap(chunks[r].astype(BF16), "vec", nv, 2 * r) for r in range(1, nq)]
            parts, beside = lax.optimization_barrier((parts, beside))
            return sum(part.astype(F32) for part in [chunks[0]] + parts), beside

        def share(x, beside):
            parts = [swap(x, "vec", nv, 2 * r) for r in range(1, nq)]
            parts, beside = lax.optimization_barrier((parts, beside))
            mine = jnp.concatenate([x] + parts)
            return [mine, swap(mine, "vec", nv, 1)], beside

        def split(fn, *counts):
            def kernel(*refs):
                groups, at = [], 0
                for count in counts:
                    groups.append(refs[at] if count == 0 else list(refs[at : at + count]))
                    at += max(count, 1)
                fn(*groups, *refs[at:])
            return kernel

        stats, cent = call(
            lambda *refs: first_stats(order, block, *refs),
            (shape(2, V), shape(K, D, dtype=BF16)),
            (centroids, weights),
            [pltpu.VMEM((8, V), F32), pltpu.VMEM((1, 8, V), F32)],
            unit,
        )
        stats = spread(stats)

        def sums(at):
            return call(
                split(lambda *refs: first_sums(at, block, nc, *refs), nc, 0, 0, 0, 0),
                (shape(nq, block + 16, D), shape(1, V)),
                (*stats, cent, weights),
                [strip],
                unit,
            )

        def rows_shape(kind):
            return [shape(V // nc, D, dtype=kind)] * nc

        def scatter(chunks):
            return [chunks[0]] + [swap(chunks[r], "cent", nc, r) for r in range(1, nc)]

        far = nc // 2
        send, _ = sums(1)
        keep, lse = sums(0)

        def first_part(masks):
            return call(
                split(lambda *refs: first_rows(masks, *refs), 0, 0, 0, len(masks)),
                [shape(V // nc, D, dtype=BF16)] * len(masks),
                (cent, weights, lse),
                [pltpu.VMEM((K, V // nc), BF16)],
                unit,
            )

        first_cent = first_part(list(range(nc // 2)))
        chunks = add_core(keep, send)
        count = chunks[:, block]
        near = lax.reduce_precision(count, 8, 7)
        pair = jnp.stack([near, count - near], axis=1)
        chunks = jnp.concatenate([chunks[:, :block], pair, chunks[:, block + 2 :]], axis=1)
        chunk, first_cent = collect(chunks, first_cent)
        denom = chunk[block, :block] + chunk[block + 1, :block] + 1e-6
        moved, more = share(
            (chunk[:block] / denom[:, None]).astype(BF16), first_part(list(range(nc // 2, nc)))
        )
        first_cent = scatter([*first_cent, *more])

        stats = call(
            split(second_stats, 2),
            shape(3, V),
            (*moved, weights, cotangent),
            [pltpu.VMEM((8, V), F32), pltpu.VMEM((2, 8, V), F32)],
        )
        stats, first_cent[1:far] = lax.optimization_barrier((stats, first_cent[1:far]))
        stats = spread(stats)

        def moved_cot(at, flops):
            return call(
                split(second_sums, nc),
                shape(nq, block, D, dtype=BF16),
                (*stats, moved[at], weights, cotangent),
                [row, row, strip, strip],
                flops,
            )

        span = V // 2

        def part(begin):
            return call(
                split(lambda *refs: second_part(begin, *refs), nc, 2),
                shape(D, span),
                (*stats, *moved, weights, cotangent),
                [row, row, pltpu.VMEM((K, span), BF16)],
                2 * unit,
            )

        send = moved_cot(1, 2 * unit)
        keep, first_cent[far:-1] = lax.optimization_barrier((moved_cot(0, 0), first_cent[far:-1]))
        moved_cot, part_low = collect(add_core(keep, send), part(0))
        mean_cot, part_high = share((moved_cot / denom[:, None]).astype(BF16), part(span))

        stats, *grad_rows = call(
            split(third_rows, 0, 2, 2, 0, 0, 2, 0, nc),
            [shape(2, V)] + rows_shape(BF16),
            (cent, *moved, *mean_cot, weights, lse, part_low, part_high),
            [pltpu.VMEM((K, span), BF16)] * 2
            + [pltpu.VMEM((K, span), F32)] * 2
            + [pltpu.VMEM((2, 8, span), F32), pltpu.VMEM((V, D), F32)],
            4 * unit,
            44,
        )
        stats, first_cent[-1] = lax.optimization_barrier((stats, first_cent[-1]))
        stats = spread(stats)
        grad_rows = scatter(grad_rows)
        start_cot = call(
            split(third_sums, nc, 0, 2, 2, 0, 0, 2),
            [shape(nq, block, D, dtype=BF16)] * 2,
            (*stats, cent, *moved, *mean_cot, weights, lse),
            [row, strip],
            2 * unit,
        )
        start_cot, grad_rows = lax.optimization_barrier((start_cot, grad_rows))
        size = V // nc
        mine = lax.axis_index("cent") * size
        own = [lax.dynamic_slice(x, (0, mine), (2, size)) for x in stats]
        dots = sum(x[0] for x in own)
        rows = sum(x.astype(F32) for x in grad_rows)
        rows = rows - sum((dots - x[1])[:, None] * f.astype(F32) for x, f in zip(own, first_cent))
        rows = spread(rows.astype(BF16))
        start_cot, _ = collect(add_core(*start_cot), ())
        start_cot = start_cot.astype(BF16)
        pair = jnp.concatenate([start_cot, swap(start_cot, "vec", nv, 1)])
        pairs, rows = lax.optimization_barrier(([swap(pair, "vec", nv, 2 * r) for r in range(1, nq)], rows))
        start_cot = call(
            split(lambda *refs: place_blocks(list(range(nv)), "vec", *refs), nq),
            shape(K, D),
            [pair] + pairs,
        )
        grad_rows = jnp.zeros((V, D), BF16)
        for r in range(nc):
            at = jnp.bitwise_xor(lax.axis_index("cent"), r) * size
            grad_rows = lax.dynamic_update_slice(grad_rows, rows[r], (at, 0))
        return grad_rows, start_cot

    return local


def solution(mesh):
    return jax.shard_map(
        make_local(mesh.shape["vec"], mesh.shape["cent"]),
        mesh=mesh,
        in_specs=(P("vec", None), P("cent", None), P("vec", None)),
        out_specs=(P("vec", None), P("cent", None)),
        check_vma=False,
    )
```

```python
import jax
import jax.numpy as jnp
from jax import lax
from jax.experimental import pallas as pl
from jax.experimental.pallas import tpu as pltpu
from jax.sharding import PartitionSpec as P

F32 = jnp.float32
BF16 = jnp.bfloat16
STEP = 512


def vmem():
    return pl.BlockSpec(memory_space=pltpu.VMEM)


def call(kernel, outs, args, scratch=(), flops=0, mib=24):
    return pl.pallas_call(
        kernel,
        in_specs=[vmem()] * len(args),
        out_specs=jax.tree.map(lambda _: vmem(), outs),
        out_shape=outs,
        scratch_shapes=list(scratch),
        cost_estimate=pl.CostEstimate(flops=flops, bytes_accessed=2**22, transcendentals=0),
        compiler_params=pltpu.CompilerParams(vmem_limit_bytes=mib * 2**20),
    )(*args)


def shape(*dims, dtype=F32):
    return jax.ShapeDtypeStruct(dims, dtype)


def dot_nt(a, b):
    return lax.dot_general(a, b, (((1,), (1,)), ((), ())), preferred_element_type=F32)


def dot(a, b):
    return jnp.dot(a, b, preferred_element_type=F32)


def cut(total, step=STEP):
    step = min(step, total)
    return [slice(at, at + step) for at in range(0, total, step)]


def tiles(refs):
    start = 0
    for ref in refs:
        for rows in cut(ref.shape[0]):
            yield ref, rows, slice(start + rows.start, start + rows.stop)
        start += ref.shape[0]


def factor(block):
    scale = block.shape[1] ** (-0.5)
    block_f = block.astype(F32)
    square = jnp.sum(jnp.square(block_f), axis=1, keepdims=True) * scale
    return (block_f * (2.0 * scale)).astype(BF16), square


def lanes(x):
    total = x[:, 0:128]
    for at in range(128, x.shape[1], 128):
        total = total + x[:, at : at + 128]
    return total


def merge(stats):
    top = stats[0][0:1, :]
    for part in stats[1:]:
        top = jnp.maximum(top, part[0:1, :])
    weights = [jnp.exp(part[0:1, :] - top) for part in stats]
    total = sum(w * part[1:2, :] for w, part in zip(weights, stats))
    return top, total, weights


def online(out, top, sums, load):
    top[...] = jnp.full(top.shape, -jnp.inf, F32)
    sums[...] = jnp.zeros(sums.shape, F32)
    for score, cols, weight in load:
        score = score.reshape(score.shape[0] // 8, 8, score.shape[1])
        old = top[:, cols]
        new = jnp.maximum(old, jnp.max(score, axis=0))
        drop = jnp.exp(old - new)
        expo = jnp.exp(score - new[None])
        sums[0, :, cols] = sums[0, :, cols] * drop + jnp.sum(expo, axis=0)
        if weight is not None:
            expo = expo * weight.reshape(expo.shape)
            sums[1, :, cols] = sums[1, :, cols] * drop + jnp.sum(expo, axis=0)
        top[:, cols] = new
    peak = jnp.max(top[...], axis=0, keepdims=True)
    scale = jnp.exp(top[...] - peak)
    out[0:1, :] = peak
    for at in range(sums.shape[0]):
        out[at + 1 : at + 2, :] = jnp.sum(sums[at] * scale, axis=0, keepdims=True)


def first_stats(order, block, cent, rows, out, cent_rel, top, sums):
    for at, mask in enumerate(order):
        owner = jnp.bitwise_xor(lax.axis_index("vec"), mask)
        cent_rel[at * block : (at + 1) * block, :] = cent[pl.ds(pl.multiple_of(owner * block, block), block), :]

    def load():
        for rows_k in cut(cent_rel.shape[0]):
            lhs, square = factor(cent_rel[rows_k, :])
            for cols in cut(rows.shape[0]):
                yield dot_nt(lhs, rows[cols, :]) - square, cols, None

    online(out, top, sums, load())


def first_sums(half, block, parts, stats, cent, rows, out, lse, expo_b):
    peak, total, _ = merge(stats)
    lse[...] = peak + jnp.log(total)
    size = out.shape[0] * block
    per = max(1, min(STEP, size) // block)
    for at in range(0, out.shape[0], per):
        start = half * size + at * block
        lhs, square = factor(cent[start : start + per * block, :])
        count = jnp.zeros((per * block, 128), F32)
        for cols in cut(rows.shape[0]):
            expo = jnp.exp(dot_nt(lhs, rows[cols, :]) - square - lse[:, cols])
            count = count + lanes(expo)
            expo_b[:, cols] = expo.astype(BF16)
        mass = dot(expo_b[...], rows[...])
        for r in range(per):
            part = slice(r * block, (r + 1) * block)
            out[at + r, 0:block, :] = mass[part, :]
            out[at + r, block:, :] = jnp.zeros((out.shape[1] - block, out.shape[2]), F32)
            out[at + r, block : block + 1, 0:block] = jnp.sum(count[part, :].T, axis=0, keepdims=True)


def second_stats(moved, rows, cot, out, top, sums):
    def load():
        for ref, rows_k, _ in tiles(moved):
            block = ref[rows_k, :]
            lhs, square = factor(block)
            for cols in cut(rows.shape[0]):
                yield dot_nt(lhs, rows[cols, :]) - square, cols, dot_nt(block, cot[cols, :])

    online(out, top, sums, load())


def second_rows(stats, lse, dots, scale):
    peak, total, weights = merge(stats)
    lse[...] = peak + jnp.log(total)
    dots[...] = sum(w * part[2:3, :] for w, part in zip(weights, stats)) / total * scale


def put_owners(out, start, value):
    block = out.shape[1]
    per = value.shape[0] // block
    out[start // block : start // block + per] = value.reshape(per, block, value.shape[1]).astype(out.dtype)


def second_sums(stats, moved, rows, cot, outs, lse, dots, expo_b, edge_b):
    second_rows(stats, lse, dots, 2.0 * rows.shape[1] ** (-0.5))
    cols_all = cut(rows.shape[0])
    ready = None
    for at, (ref, rows_k, _) in enumerate([*tiles(moved), (None, None, None)]):
        slot, last = at % 2, 1 - at % 2
        if ref is not None:
            block = ref[rows_k, :]
            lhs, square = factor(block)
            edges = jnp.zeros((block.shape[0], 128), F32)
        for step, cols in enumerate(cols_all):
            if ref is not None:
                expo = jnp.exp(dot_nt(lhs, rows[cols, :]) - square - lse[:, cols])
                expo_b[slot, :, cols] = expo.astype(BF16)
                edge = expo * (dot_nt(lhs, cot[cols, :]) - dots[:, cols])
                edges = edges + lanes(edge)
                edge_b[slot, :, cols] = edge.astype(BF16)
            if ready is not None and step == 0:
                total = dot(expo_b[last], cot[...])
            if ready is not None and step == len(cols_all) // 2:
                total = total + dot(edge_b[last], rows[...])
        if ready is not None:
            out, start, old, old_edges = ready
            put_owners(out, start, total - jnp.sum(old_edges, axis=1, keepdims=True) * old.astype(F32))
        if ref is not None:
            ready = outs[0] if ref is moved[0] else outs[1], rows_k.start, block, edges


def second_part(begin, stats, moved, rows, cot, out, lse, dots, edge_b):
    second_rows(stats, lse, dots, 2.0 * rows.shape[1] ** (-0.5))
    for ref, rows_k, whole in tiles(moved):
        lhs, square = factor(ref[rows_k, :])
        for local in cut(out.shape[1]):
            cols = slice(begin + local.start, begin + local.stop)
            expo = jnp.exp(dot_nt(lhs, rows[cols, :]) - square - lse[:, cols])
            edge = expo * (dot_nt(lhs, cot[cols, :]) - dots[:, cols])
            edge_b[whole, local] = edge.astype(BF16)
    for local in cut(out.shape[1]):
        out[:, local] = sum(
            dot(ref[...].T, edge_b[at : at + ref.shape[0], local])
            for ref, at in zip(moved, (0, moved[0].shape[0]))
        )


def put_chunks(index, total, outs):
    size = total.shape[0] // len(outs)
    for r, out in enumerate(outs):
        at = jnp.bitwise_xor(index, r) * size
        out[...] = total[pl.ds(pl.multiple_of(at, size), size), :].astype(out.dtype)


def first_rows(masks, cent, rows, lse, outs, expo_b):
    cent_t = cent[...].T
    for mask, out in zip(masks, outs):
        size = out.shape[0]
        own = pl.ds(pl.multiple_of(jnp.bitwise_xor(lax.axis_index("cent"), mask) * size, size), size)
        chunk, shift = rows[own, :], lse[:, own]
        for whole in cut(cent.shape[0]):
            lhs, square = factor(cent[whole, :])
            expo_b[whole, :] = jnp.exp(dot_nt(lhs, chunk) - square - shift).astype(BF16)
        out[...] = dot(cent_t, expo_b[...]).T.astype(out.dtype)


def third_terms(cent, moved, mean_cot, rows, lse, cols_all):
    scale = 2.0 * rows.shape[1] ** (-0.5)
    for (mean_ref, rows_k, whole), (moved_ref, _, _) in zip(tiles(mean_cot), tiles(moved)):
        lhs, square = factor(cent[whole, :])
        mean = mean_ref[rows_k, :].astype(F32) * scale
        count_cot = -jnp.sum(mean * moved_ref[rows_k, :].astype(F32), axis=1, keepdims=True)
        mean = mean.astype(BF16)
        for cols in cols_all:
            expo = jnp.exp(dot_nt(lhs, rows[cols, :]) - square - lse[:, cols])
            yield whole, cols, expo, dot_nt(mean, rows[cols, :]) + count_cot


def third_rows(own, cent, moved, mean_cot, rows, lse, parts, stats, outs, lhs_s, mean_s, expo_b, edge_b, expo_f, dfirst_f, total):
    scale = 2.0 * rows.shape[1] ** (-0.5)
    cent_t = cent[...].T
    halves = [ref[...].T for ref in mean_cot]
    size = halves[0].shape[1]
    terms = []
    for (mean_ref, rows_k, whole), (moved_ref, _, _) in zip(tiles(mean_cot), tiles(moved)):
        lhs, square = factor(cent[whole, :])
        mean = mean_ref[rows_k, :].astype(F32) * scale
        lhs_s[whole, :] = lhs
        mean_s[whole, :] = mean.astype(BF16)
        terms.append((whole, square, -jnp.sum(mean * moved_ref[rows_k, :].astype(F32), axis=1, keepdims=True)))
    cols_all = cut(rows.shape[0])
    ready = None
    for at, cols in enumerate([*cols_all, None]):
        slot, last = at % 2, 1 - at % 2
        if cols is not None:
            dots = jnp.zeros((8, cols.stop - cols.start), F32)
        if ready is not None:
            done, mean = ready
            part = parts[done.start // parts[0].shape[1]]
            begin = done.start % parts[0].shape[1]
            value = part[:, begin : begin + done.stop - done.start]
        for whole, square, count_cot in terms:
            if cols is not None:
                expo = jnp.exp(dot_nt(lhs_s[whole, :], rows[cols, :]) - square - lse[:, cols])
                dfirst = dot_nt(mean_s[whole, :], rows[cols, :]) + count_cot
                expo_f[slot, whole, :] = expo
                dfirst_f[slot, whole, :] = dfirst
                expo_b[slot, whole, :] = expo.astype(BF16)
                dots = dots + jnp.sum((expo * dfirst).reshape(expo.shape[0] // 8, 8, expo.shape[1]), axis=0)
            if ready is not None:
                edge = expo_f[last, whole, :] * (dfirst_f[last, whole, :] - mean)
                edge_b[whole, :] = edge.astype(BF16)
                if whole.stop % size == 0:
                    half = slice(whole.stop - size, whole.stop)
                    value = value + dot(cent_t[:, half], edge_b[half, :])
                    value = value + dot(halves[half.start // size], expo_b[last, half, :])
        if ready is not None:
            total[done, :] = value.T
        if cols is not None:
            dots = jnp.sum(dots, axis=0, keepdims=True)
            weight = own[1:2, cols] * jnp.exp(own[0:1, cols] - lse[:, cols])
            mean = jnp.where(weight > 0.0, dots / jnp.where(weight > 0.0, weight, 1.0), 0.0)
            stats[0:1, cols] = dots
            stats[1:2, cols] = mean
            ready = cols, mean
    put_chunks(lax.axis_index("cent"), total, outs)


def third_sums(stats, cent, moved, mean_cot, rows, lse, outs, dots, edge_b):
    dots[...] = sum(ref[0:1, :] for ref in stats)
    edges = jnp.zeros((edge_b.shape[0], 128), F32)
    for whole, cols, expo, dfirst in third_terms(cent, moved, mean_cot, rows, lse, cut(rows.shape[0])):
        edge = expo * (dfirst - dots[:, cols])
        edges = edges + lanes(edge)
        edge_b[:, cols] = edge.astype(BF16)
        if cols.stop == rows.shape[0]:
            value = dot(edge_b[...], rows[...])
            value = value - jnp.sum(edges, axis=1, keepdims=True) * cent[whole, :].astype(F32)
            which, start = divmod(whole.start, cent.shape[0] // 2)
            put_owners(outs[which], start, value)
            edges = jnp.zeros(edges.shape, F32)


def place_blocks(order, axis, parts, out):
    at = 0
    for part in parts:
        block = out.shape[0] // len(order)
        for start in range(0, part.shape[0], block):
            owner = jnp.bitwise_xor(lax.axis_index(axis), order[at])
            out[pl.ds(pl.multiple_of(owner * block, block), block), :] = part[start : start + block, :].astype(out.dtype)
            at += 1


def swap(x, axis, n, mask):
    return lax.ppermute(x, axis, [(i, i ^ mask) for i in range(n)])


def make_local(nv, nc):
    nq = nv // 2
    order = [2 * r + a for a in range(2) for r in range(nq)]

    def local(weights, centroids, cotangent):
        V, D = weights.shape
        K = centroids.shape[0]
        block, half = K // nv, K // 2
        step, wide = min(STEP, half), min(STEP, V)
        unit = 2 * K * V * D
        row = pltpu.VMEM((1, V), F32)
        strip = pltpu.VMEM((step, V), BF16)

        def spread(x):
            return [x] + [swap(x, "cent", nc, r) for r in range(1, nc)]

        def add_core(keep, send):
            return keep.astype(F32) + swap(send, "vec", nv, 1).astype(F32)

        def collect(chunks, beside):
            parts = [swap(chunks[r].astype(BF16), "vec", nv, 2 * r) for r in range(1, nq)]
            parts, beside = lax.optimization_barrier((parts, beside))
            return sum(part.astype(F32) for part in [chunks[0]] + parts), beside

        def share(x, beside):
            parts = [swap(x, "vec", nv, 2 * r) for r in range(1, nq)]
            parts, beside = lax.optimization_barrier((parts, beside))
            mine = jnp.concatenate([x] + parts)
            return [mine, swap(mine, "vec", nv, 1)], beside

        def split(fn, *counts):
            def kernel(*refs):
                groups, at = [], 0
                for count in counts:
                    groups.append(refs[at] if count == 0 else list(refs[at : at + count]))
                    at += max(count, 1)
                fn(*groups, *refs[at:])
            return kernel

        stats, cent = call(
            lambda *refs: first_stats(order, block, *refs),
            (shape(2, V), shape(K, D, dtype=BF16)),
            (centroids, weights),
            [pltpu.VMEM((8, V), F32), pltpu.VMEM((1, 8, V), F32)],
            unit,
        )
        first_own = stats
        stats = spread(stats)

        def sums(at):
            return call(
                split(lambda *refs: first_sums(at, block, nc, *refs), nc, 0, 0, 0, 0),
                (shape(nq, block + 16, D), shape(1, V)),
                (*stats, cent, weights),
                [strip],
                unit,
            )

        def rows_shape(kind):
            return [shape(V // nc, D, dtype=kind)] * nc

        def scatter(chunks):
            return [chunks[0]] + [swap(chunks[r], "cent", nc, r) for r in range(1, nc)]

        send, _ = sums(1)
        keep, lse = sums(0)

        def first_part(masks):
            return call(
                split(lambda *refs: first_rows(masks, *refs), 0, 0, 0, len(masks)),
                [shape(V // nc, D, dtype=BF16)] * len(masks),
                (cent, weights, lse),
                [pltpu.VMEM((K, V // nc), BF16)],
                unit,
            )

        first_cent = first_part(list(range(nc // 2)))
        chunks = add_core(keep, send)
        count = chunks[:, block]
        near = lax.reduce_precision(count, 8, 7)
        pair = jnp.stack([near, count - near], axis=1)
        chunks = jnp.concatenate([chunks[:, :block], pair, chunks[:, block + 2 :]], axis=1)
        chunk, first_cent = collect(chunks, first_cent)
        denom = chunk[block, :block] + chunk[block + 1, :block] + 1e-6
        moved, more = share(
            (chunk[:block] / denom[:, None]).astype(BF16), first_part(list(range(nc // 2, nc)))
        )
        first_cent = scatter([*first_cent, *more])

        stats = spread(call(
            split(second_stats, 2),
            shape(3, V),
            (*moved, weights, cotangent),
            [pltpu.VMEM((8, V), F32), pltpu.VMEM((2, 8, V), F32)],
        ))
        moved_cot = call(
            split(second_sums, nc, 2, 0, 0, 2),
            [shape(nq, block, D, dtype=BF16)] * 2,
            (*stats, *moved, weights, cotangent),
            [row, row] + [pltpu.VMEM((2, step, V), BF16)] * 2,
            4 * unit,
        )
        span = V // 2

        def part(begin):
            return call(
                split(lambda *refs: second_part(begin, *refs), nc, 2),
                shape(D, span),
                (*stats, *moved, weights, cotangent),
                [row, row, pltpu.VMEM((K, span), BF16)],
                unit,
            )

        far = nc // 2
        moved_cot, (part_low, first_cent[1:far]) = collect(add_core(*moved_cot), (part(0), first_cent[1:far]))
        mean_cot, (part_high, first_cent[far:-1]) = share(
            (moved_cot / denom[:, None]).astype(BF16), (part(span), first_cent[far:-1])
        )

        stats, *grad_rows = call(
            split(third_rows, 0, 0, 2, 2, 0, 0, 2, 0, nc),
            [shape(2, V)] + rows_shape(BF16),
            (first_own, cent, *moved, *mean_cot, weights, lse, part_low, part_high),
            [pltpu.VMEM((K, D), BF16)] * 2
            + [pltpu.VMEM((2, K, wide), BF16), pltpu.VMEM((K, wide), BF16)]
            + [pltpu.VMEM((2, K, wide), F32)] * 2
            + [pltpu.VMEM((V, D), F32)],
            4 * unit,
            44,
        )
        stats, first_cent[-1] = lax.optimization_barrier((stats, first_cent[-1]))
        stats = spread(stats)
        grad_rows = scatter(grad_rows)
        start_cot = call(
            split(third_sums, nc, 0, 2, 2, 0, 0, 2),
            [shape(nq, block, D, dtype=BF16)] * 2,
            (*stats, cent, *moved, *mean_cot, weights, lse),
            [row, strip],
            2 * unit,
        )
        start_cot, grad_rows = lax.optimization_barrier((start_cot, grad_rows))
        size = V // nc
        mine = lax.axis_index("cent") * size
        own = [lax.dynamic_slice(x, (0, mine), (2, size)) for x in stats]
        dots = sum(x[0] for x in own)
        rows = sum(x.astype(F32) for x in grad_rows)
        rows = rows - sum((dots - x[1])[:, None] * f.astype(F32) for x, f in zip(own, first_cent))
        rows = spread(rows.astype(BF16))
        start_cot, _ = collect(add_core(*start_cot), ())
        start_cot, rows = share(start_cot.astype(BF16), rows)
        start_cot = call(
            split(lambda *refs: place_blocks(order, "vec", *refs), 2),
            shape(K, D),
            start_cot,
        )
        grad_rows = jnp.zeros((V, D), BF16)
        for r in range(nc):
            at = jnp.bitwise_xor(lax.axis_index("cent"), r) * size
            grad_rows = lax.dynamic_update_slice(grad_rows, rows[r], (at, 0))
        return grad_rows, start_cot

    return local


def solution(mesh):
    return jax.shard_map(
        make_local(mesh.shape["vec"], mesh.shape["cent"]),
        mesh=mesh,
        in_specs=(P("vec", None), P("cent", None), P("vec", None)),
        out_specs=(P("vec", None), P("cent", None)),
        check_vma=False,
    )
```

```python
import jax
import jax.numpy as jnp
from jax import lax
from jax.experimental import pallas as pl
from jax.experimental.pallas import tpu as pltpu
from jax.sharding import PartitionSpec as P

F32 = jnp.float32
BF16 = jnp.bfloat16
STEP = 512


def vmem():
    return pl.BlockSpec(memory_space=pltpu.VMEM)


def call(kernel, outs, args, scratch=(), flops=0, mib=24):
    return pl.pallas_call(
        kernel,
        in_specs=[vmem()] * len(args),
        out_specs=jax.tree.map(lambda _: vmem(), outs),
        out_shape=outs,
        scratch_shapes=list(scratch),
        cost_estimate=pl.CostEstimate(flops=flops, bytes_accessed=2**22, transcendentals=0),
        compiler_params=pltpu.CompilerParams(vmem_limit_bytes=mib * 2**20),
    )(*args)


def shape(*dims, dtype=F32):
    return jax.ShapeDtypeStruct(dims, dtype)


def dot_nt(a, b):
    return lax.dot_general(a, b, (((1,), (1,)), ((), ())), preferred_element_type=F32)


def dot(a, b):
    return jnp.dot(a, b, preferred_element_type=F32)


def cut(total, step=STEP):
    step = min(step, total)
    return [slice(at, at + step) for at in range(0, total, step)]


def tiles(refs):
    start = 0
    for ref in refs:
        for rows in cut(ref.shape[0]):
            yield ref, rows, slice(start + rows.start, start + rows.stop)
        start += ref.shape[0]


def factor(block):
    scale = block.shape[1] ** (-0.5)
    block_f = block.astype(F32)
    square = jnp.sum(jnp.square(block_f), axis=1, keepdims=True) * scale
    return (block_f * (2.0 * scale)).astype(BF16), square


def lanes(x):
    total = x[:, 0:128]
    for at in range(128, x.shape[1], 128):
        total = total + x[:, at : at + 128]
    return total


def merge(stats):
    top = stats[0][0:1, :]
    for part in stats[1:]:
        top = jnp.maximum(top, part[0:1, :])
    weights = [jnp.exp(part[0:1, :] - top) for part in stats]
    total = sum(w * part[1:2, :] for w, part in zip(weights, stats))
    return top, total, weights


def online(out, top, sums, load):
    top[...] = jnp.full(top.shape, -jnp.inf, F32)
    sums[...] = jnp.zeros(sums.shape, F32)
    for score, cols, weight in load:
        score = score.reshape(score.shape[0] // 8, 8, score.shape[1])
        old = top[:, cols]
        new = jnp.maximum(old, jnp.max(score, axis=0))
        drop = jnp.exp(old - new)
        expo = jnp.exp(score - new[None])
        sums[0, :, cols] = sums[0, :, cols] * drop + jnp.sum(expo, axis=0)
        if weight is not None:
            expo = expo * weight.reshape(expo.shape)
            sums[1, :, cols] = sums[1, :, cols] * drop + jnp.sum(expo, axis=0)
        top[:, cols] = new
    peak = jnp.max(top[...], axis=0, keepdims=True)
    scale = jnp.exp(top[...] - peak)
    out[0:1, :] = peak
    for at in range(sums.shape[0]):
        out[at + 1 : at + 2, :] = jnp.sum(sums[at] * scale, axis=0, keepdims=True)


def first_stats(order, block, cent, rows, out, cent_rel, top, sums):
    for at, mask in enumerate(order):
        owner = jnp.bitwise_xor(lax.axis_index("vec"), mask)
        cent_rel[at * block : (at + 1) * block, :] = cent[pl.ds(pl.multiple_of(owner * block, block), block), :]

    def load():
        for rows_k in cut(cent_rel.shape[0]):
            lhs, square = factor(cent_rel[rows_k, :])
            for cols in cut(rows.shape[0]):
                yield dot_nt(lhs, rows[cols, :]) - square, cols, None

    online(out, top, sums, load())


def first_sums(half, block, parts, stats, cent, rows, out, lse, expo_b):
    peak, total, _ = merge(stats)
    lse[...] = peak + jnp.log(total)
    size = out.shape[0] * block
    per = max(1, min(STEP, size) // block)
    for at in range(0, out.shape[0], per):
        start = half * size + at * block
        lhs, square = factor(cent[start : start + per * block, :])
        count = jnp.zeros((per * block, 128), F32)
        for cols in cut(rows.shape[0]):
            expo = jnp.exp(dot_nt(lhs, rows[cols, :]) - square - lse[:, cols])
            count = count + lanes(expo)
            expo_b[:, cols] = expo.astype(BF16)
        mass = dot(expo_b[...], rows[...])
        for r in range(per):
            part = slice(r * block, (r + 1) * block)
            out[at + r, 0:block, :] = mass[part, :]
            out[at + r, block:, :] = jnp.zeros((out.shape[1] - block, out.shape[2]), F32)
            out[at + r, block : block + 1, 0:block] = jnp.sum(count[part, :].T, axis=0, keepdims=True)


def second_stats(moved, rows, cot, out, top, sums):
    def load():
        for ref, rows_k, _ in tiles(moved):
            block = ref[rows_k, :]
            lhs, square = factor(block)
            for cols in cut(rows.shape[0]):
                yield dot_nt(lhs, rows[cols, :]) - square, cols, dot_nt(block, cot[cols, :])

    online(out, top, sums, load())


def second_rows(stats, lse, dots, scale):
    peak, total, weights = merge(stats)
    lse[...] = peak + jnp.log(total)
    dots[...] = sum(w * part[2:3, :] for w, part in zip(weights, stats)) / total * scale


def put_owners(out, start, value):
    block = out.shape[1]
    per = value.shape[0] // block
    out[start // block : start // block + per] = value.reshape(per, block, value.shape[1]).astype(out.dtype)


def second_sums(stats, moved, rows, cot, outs, lse, dots, expo_b, edge_b):
    second_rows(stats, lse, dots, 2.0 * rows.shape[1] ** (-0.5))
    cols_all = cut(rows.shape[0])
    ready = None
    for at, (ref, rows_k, _) in enumerate([*tiles(moved), (None, None, None)]):
        slot, last = at % 2, 1 - at % 2
        if ref is not None:
            block = ref[rows_k, :]
            lhs, square = factor(block)
            edges = jnp.zeros((block.shape[0], 128), F32)
        for step, cols in enumerate(cols_all):
            if ref is not None:
                expo = jnp.exp(dot_nt(lhs, rows[cols, :]) - square - lse[:, cols])
                expo_b[slot, :, cols] = expo.astype(BF16)
                edge = expo * (dot_nt(lhs, cot[cols, :]) - dots[:, cols])
                edges = edges + lanes(edge)
                edge_b[slot, :, cols] = edge.astype(BF16)
            if ready is not None and step == 0:
                total = dot(expo_b[last], cot[...])
            if ready is not None and step == len(cols_all) // 2:
                total = total + dot(edge_b[last], rows[...])
        if ready is not None:
            out, start, old, old_edges = ready
            put_owners(out, start, total - jnp.sum(old_edges, axis=1, keepdims=True) * old.astype(F32))
        if ref is not None:
            ready = outs[0] if ref is moved[0] else outs[1], rows_k.start, block, edges


def second_part(begin, stats, moved, rows, cot, out, lse, dots, edge_b):
    second_rows(stats, lse, dots, 2.0 * rows.shape[1] ** (-0.5))
    for ref, rows_k, whole in tiles(moved):
        lhs, square = factor(ref[rows_k, :])
        for local in cut(out.shape[1]):
            cols = slice(begin + local.start, begin + local.stop)
            expo = jnp.exp(dot_nt(lhs, rows[cols, :]) - square - lse[:, cols])
            edge = expo * (dot_nt(lhs, cot[cols, :]) - dots[:, cols])
            edge_b[whole, local] = edge.astype(BF16)
    for local in cut(out.shape[1]):
        out[:, local] = sum(
            dot(ref[...].T, edge_b[at : at + ref.shape[0], local])
            for ref, at in zip(moved, (0, moved[0].shape[0]))
        )


def put_chunks(index, total, outs):
    size = total.shape[0] // len(outs)
    for r, out in enumerate(outs):
        at = jnp.bitwise_xor(index, r) * size
        out[...] = total[pl.ds(pl.multiple_of(at, size), size), :].astype(out.dtype)


def first_rows(masks, cent, rows, lse, outs, expo_b):
    cent_t = cent[...].T
    for mask, out in zip(masks, outs):
        size = out.shape[0]
        own = pl.ds(pl.multiple_of(jnp.bitwise_xor(lax.axis_index("cent"), mask) * size, size), size)
        chunk, shift = rows[own, :], lse[:, own]
        for whole in cut(cent.shape[0]):
            lhs, square = factor(cent[whole, :])
            expo_b[whole, :] = jnp.exp(dot_nt(lhs, chunk) - square - shift).astype(BF16)
        out[...] = dot(cent_t, expo_b[...]).T.astype(out.dtype)


def third_terms(cent, moved, mean_cot, rows, lse, cols_all):
    scale = 2.0 * rows.shape[1] ** (-0.5)
    for (mean_ref, rows_k, whole), (moved_ref, _, _) in zip(tiles(mean_cot), tiles(moved)):
        lhs, square = factor(cent[whole, :])
        mean = mean_ref[rows_k, :].astype(F32) * scale
        count_cot = -jnp.sum(mean * moved_ref[rows_k, :].astype(F32), axis=1, keepdims=True)
        mean = mean.astype(BF16)
        for cols in cols_all:
            expo = jnp.exp(dot_nt(lhs, rows[cols, :]) - square - lse[:, cols])
            yield whole, cols, expo, dot_nt(mean, rows[cols, :]) + count_cot


def third_rows(own, cent, moved, mean_cot, rows, lse, parts, stats, outs, lhs_s, mean_s, expo_b, edge_b, expo_f, dfirst_f, total):
    scale = 2.0 * rows.shape[1] ** (-0.5)
    cent_t = cent[...].T
    halves = [ref[...].T for ref in mean_cot]
    size = halves[0].shape[1]
    terms = []
    for (mean_ref, rows_k, whole), (moved_ref, _, _) in zip(tiles(mean_cot), tiles(moved)):
        lhs, square = factor(cent[whole, :])
        mean = mean_ref[rows_k, :].astype(F32) * scale
        lhs_s[whole, :] = lhs
        mean_s[whole, :] = mean.astype(BF16)
        terms.append((whole, square, -jnp.sum(mean * moved_ref[rows_k, :].astype(F32), axis=1, keepdims=True)))
    cols_all = cut(rows.shape[0])
    ready = None
    for at, cols in enumerate([*cols_all, None]):
        slot, last = at % 2, 1 - at % 2
        if cols is not None:
            dots = jnp.zeros((8, cols.stop - cols.start), F32)
        if ready is not None:
            done, mean = ready
            part = parts[done.start // parts[0].shape[1]]
            begin = done.start % parts[0].shape[1]
            value = part[:, begin : begin + done.stop - done.start]
        for whole, square, count_cot in terms:
            if cols is not None:
                expo = jnp.exp(dot_nt(lhs_s[whole, :], rows[cols, :]) - square - lse[:, cols])
                dfirst = dot_nt(mean_s[whole, :], rows[cols, :]) + count_cot
                expo_f[slot, whole, :] = expo
                dfirst_f[slot, whole, :] = dfirst
                expo_b[slot, whole, :] = expo.astype(BF16)
                dots = dots + jnp.sum((expo * dfirst).reshape(expo.shape[0] // 8, 8, expo.shape[1]), axis=0)
            if ready is not None:
                edge = expo_f[last, whole, :] * (dfirst_f[last, whole, :] - mean)
                edge_b[whole, :] = edge.astype(BF16)
                if whole.stop % size == 0:
                    half = slice(whole.stop - size, whole.stop)
                    value = value + dot(cent_t[:, half], edge_b[half, :])
                    value = value + dot(halves[half.start // size], expo_b[last, half, :])
        if ready is not None:
            total[done, :] = value.T
        if cols is not None:
            dots = jnp.sum(dots, axis=0, keepdims=True)
            weight = own[1:2, cols] * jnp.exp(own[0:1, cols] - lse[:, cols])
            mean = jnp.where(weight > 0.0, dots / jnp.where(weight > 0.0, weight, 1.0), 0.0)
            stats[0:1, cols] = dots
            stats[1:2, cols] = mean
            ready = cols, mean
    put_chunks(lax.axis_index("cent"), total, outs)


def third_sums(stats, cent, moved, mean_cot, rows, lse, outs, dots, edge_b):
    dots[...] = sum(ref[0:1, :] for ref in stats)
    edges = jnp.zeros((edge_b.shape[0], 128), F32)
    for whole, cols, expo, dfirst in third_terms(cent, moved, mean_cot, rows, lse, cut(rows.shape[0])):
        edge = expo * (dfirst - dots[:, cols])
        edges = edges + lanes(edge)
        edge_b[:, cols] = edge.astype(BF16)
        if cols.stop == rows.shape[0]:
            value = dot(edge_b[...], rows[...])
            value = value - jnp.sum(edges, axis=1, keepdims=True) * cent[whole, :].astype(F32)
            which, start = divmod(whole.start, cent.shape[0] // 2)
            put_owners(outs[which], start, value)
            edges = jnp.zeros(edges.shape, F32)


def place_blocks(order, axis, parts, out):
    at = 0
    for part in parts:
        block = out.shape[0] // len(order)
        for start in range(0, part.shape[0], block):
            owner = jnp.bitwise_xor(lax.axis_index(axis), order[at])
            out[pl.ds(pl.multiple_of(owner * block, block), block), :] = part[start : start + block, :].astype(out.dtype)
            at += 1


def swap(x, axis, n, mask):
    return lax.ppermute(x, axis, [(i, i ^ mask) for i in range(n)])


def make_local(nv, nc):
    nq = nv // 2
    order = [2 * r + a for a in range(2) for r in range(nq)]

    def local(weights, centroids, cotangent):
        V, D = weights.shape
        K = centroids.shape[0]
        block, half = K // nv, K // 2
        step, wide = min(STEP, half), min(STEP, V)
        unit = 2 * K * V * D
        row = pltpu.VMEM((1, V), F32)
        strip = pltpu.VMEM((step, V), BF16)

        def spread(x):
            return [x] + [swap(x, "cent", nc, r) for r in range(1, nc)]

        def add_core(keep, send):
            return keep.astype(F32) + swap(send, "vec", nv, 1).astype(F32)

        def collect(chunks, beside):
            parts = [swap(chunks[r].astype(BF16), "vec", nv, 2 * r) for r in range(1, nq)]
            parts, beside = lax.optimization_barrier((parts, beside))
            return sum(part.astype(F32) for part in [chunks[0]] + parts), beside

        def share(x, beside):
            parts = [swap(x, "vec", nv, 2 * r) for r in range(1, nq)]
            parts, beside = lax.optimization_barrier((parts, beside))
            mine = jnp.concatenate([x] + parts)
            return [mine, swap(mine, "vec", nv, 1)], beside

        def split(fn, *counts):
            def kernel(*refs):
                groups, at = [], 0
                for count in counts:
                    groups.append(refs[at] if count == 0 else list(refs[at : at + count]))
                    at += max(count, 1)
                fn(*groups, *refs[at:])
            return kernel

        stats, cent = call(
            lambda *refs: first_stats(order, block, *refs),
            (shape(2, V), shape(K, D, dtype=BF16)),
            (centroids, weights),
            [pltpu.VMEM((8, V), F32), pltpu.VMEM((1, 8, V), F32)],
            unit,
        )
        first_own = stats
        stats = spread(stats)

        def sums(at):
            return call(
                split(lambda *refs: first_sums(at, block, nc, *refs), nc, 0, 0, 0, 0),
                (shape(nq, block + 16, D), shape(1, V)),
                (*stats, cent, weights),
                [strip],
                unit,
            )

        def rows_shape(kind):
            return [shape(V // nc, D, dtype=kind)] * nc

        def scatter(chunks):
            return [chunks[0]] + [swap(chunks[r], "cent", nc, r) for r in range(1, nc)]

        send, _ = sums(1)
        keep, lse = sums(0)

        def first_part(masks):
            return call(
                split(lambda *refs: first_rows(masks, *refs), 0, 0, 0, len(masks)),
                [shape(V // nc, D, dtype=BF16)] * len(masks),
                (cent, weights, lse),
                [pltpu.VMEM((K, V // nc), BF16)],
                unit,
            )

        first_cent = first_part(list(range(nc // 2)))
        chunks = add_core(keep, send)
        count = chunks[:, block]
        near = lax.reduce_precision(count, 8, 7)
        pair = jnp.stack([near, count - near], axis=1)
        chunks = jnp.concatenate([chunks[:, :block], pair, chunks[:, block + 2 :]], axis=1)
        chunk, first_cent = collect(chunks, first_cent)
        denom = chunk[block, :block] + chunk[block + 1, :block] + 1e-6
        moved, more = share(
            (chunk[:block] / denom[:, None]).astype(BF16), first_part(list(range(nc // 2, nc)))
        )
        first_cent = scatter([*first_cent, *more])

        far = nc // 2
        stats = call(
            split(second_stats, 2),
            shape(3, V),
            (*moved, weights, cotangent),
            [pltpu.VMEM((8, V), F32), pltpu.VMEM((2, 8, V), F32)],
        )
        stats, first_cent[1:far] = lax.optimization_barrier((stats, first_cent[1:far]))
        stats = spread(stats)
        moved_cot = call(
            split(second_sums, nc, 2, 0, 0, 2),
            [shape(nq, block, D, dtype=BF16)] * 2,
            (*stats, *moved, weights, cotangent),
            [row, row] + [pltpu.VMEM((2, step, V), BF16)] * 2,
            3 * unit,
        )
        moved_cot, first_cent[far:-1] = lax.optimization_barrier((moved_cot, first_cent[far:-1]))
        span = V // 2

        def part(begin):
            return call(
                split(lambda *refs: second_part(begin, *refs), nc, 2),
                shape(D, span),
                (*stats, *moved, weights, cotangent),
                [row, row, pltpu.VMEM((K, span), BF16)],
                unit,
            )

        moved_cot, part_low = collect(add_core(*moved_cot), part(0))
        mean_cot, part_high = share((moved_cot / denom[:, None]).astype(BF16), part(span))

        stats, *grad_rows = call(
            split(third_rows, 0, 0, 2, 2, 0, 0, 2, 0, nc),
            [shape(2, V)] + rows_shape(BF16),
            (first_own, cent, *moved, *mean_cot, weights, lse, part_low, part_high),
            [pltpu.VMEM((K, D), BF16)] * 2
            + [pltpu.VMEM((2, K, wide), BF16), pltpu.VMEM((K, wide), BF16)]
            + [pltpu.VMEM((2, K, wide), F32)] * 2
            + [pltpu.VMEM((V, D), F32)],
            4 * unit,
            44,
        )
        stats, first_cent[-1] = lax.optimization_barrier((stats, first_cent[-1]))
        stats = spread(stats)
        grad_rows = scatter(grad_rows)
        start_cot = call(
            split(third_sums, nc, 0, 2, 2, 0, 0, 2),
            [shape(nq, block, D, dtype=BF16)] * 2,
            (*stats, cent, *moved, *mean_cot, weights, lse),
            [row, strip],
            2 * unit,
        )
        start_cot, grad_rows = lax.optimization_barrier((start_cot, grad_rows))
        size = V // nc
        mine = lax.axis_index("cent") * size
        own = [lax.dynamic_slice(x, (0, mine), (2, size)) for x in stats]
        dots = sum(x[0] for x in own)
        rows = sum(x.astype(F32) for x in grad_rows)
        rows = rows - sum((dots - x[1])[:, None] * f.astype(F32) for x, f in zip(own, first_cent))
        rows = spread(rows.astype(BF16))
        start_cot, _ = collect(add_core(*start_cot), ())
        start_cot, rows = share(start_cot.astype(BF16), rows)
        start_cot = call(
            split(lambda *refs: place_blocks(order, "vec", *refs), 2),
            shape(K, D),
            start_cot,
        )
        grad_rows = jnp.zeros((V, D), BF16)
        for r in range(nc):
            at = jnp.bitwise_xor(lax.axis_index("cent"), r) * size
            grad_rows = lax.dynamic_update_slice(grad_rows, rows[r], (at, 0))
        return grad_rows, start_cot

    return local


def solution(mesh):
    return jax.shard_map(
        make_local(mesh.shape["vec"], mesh.shape["cent"]),
        mesh=mesh,
        in_specs=(P("vec", None), P("cent", None), P("vec", None)),
        out_specs=(P("vec", None), P("cent", None)),
        check_vma=False,
    )
```

```python
import jax
import jax.numpy as jnp
from jax import lax
from jax.experimental import pallas as pl
from jax.experimental.pallas import tpu as pltpu
from jax.sharding import PartitionSpec as P

F32 = jnp.float32
BF16 = jnp.bfloat16
STEP = 512


def vmem():
    return pl.BlockSpec(memory_space=pltpu.VMEM)


def call(kernel, outs, args, scratch=(), flops=0, mib=24):
    return pl.pallas_call(
        kernel,
        in_specs=[vmem()] * len(args),
        out_specs=jax.tree.map(lambda _: vmem(), outs),
        out_shape=outs,
        scratch_shapes=list(scratch),
        cost_estimate=pl.CostEstimate(flops=flops, bytes_accessed=2**22, transcendentals=0),
        compiler_params=pltpu.CompilerParams(vmem_limit_bytes=mib * 2**20),
    )(*args)


def shape(*dims, dtype=F32):
    return jax.ShapeDtypeStruct(dims, dtype)


def dot_nt(a, b):
    return lax.dot_general(a, b, (((1,), (1,)), ((), ())), preferred_element_type=F32)


def dot(a, b):
    return jnp.dot(a, b, preferred_element_type=F32)


def cut(total, step=STEP):
    step = min(step, total)
    return [slice(at, at + step) for at in range(0, total, step)]


def tiles(refs):
    start = 0
    for ref in refs:
        for rows in cut(ref.shape[0]):
            yield ref, rows, slice(start + rows.start, start + rows.stop)
        start += ref.shape[0]


def factor(block):
    scale = block.shape[1] ** (-0.5)
    block_f = block.astype(F32)
    square = jnp.sum(jnp.square(block_f), axis=1, keepdims=True) * scale
    return (block_f * (2.0 * scale)).astype(BF16), square


def lanes(x):
    total = x[:, 0:128]
    for at in range(128, x.shape[1], 128):
        total = total + x[:, at : at + 128]
    return total


def merge(stats):
    top = stats[0][0:1, :]
    for part in stats[1:]:
        top = jnp.maximum(top, part[0:1, :])
    weights = [jnp.exp(part[0:1, :] - top) for part in stats]
    total = sum(w * part[1:2, :] for w, part in zip(weights, stats))
    return top, total, weights


def online(out, top, sums, load):
    top[...] = jnp.full(top.shape, -jnp.inf, F32)
    sums[...] = jnp.zeros(sums.shape, F32)
    for score, cols, weight in load:
        score = score.reshape(score.shape[0] // 8, 8, score.shape[1])
        old = top[:, cols]
        new = jnp.maximum(old, jnp.max(score, axis=0))
        drop = jnp.exp(old - new)
        expo = jnp.exp(score - new[None])
        sums[0, :, cols] = sums[0, :, cols] * drop + jnp.sum(expo, axis=0)
        if weight is not None:
            expo = expo * weight.reshape(expo.shape)
            sums[1, :, cols] = sums[1, :, cols] * drop + jnp.sum(expo, axis=0)
        top[:, cols] = new
    peak = jnp.max(top[...], axis=0, keepdims=True)
    scale = jnp.exp(top[...] - peak)
    out[0:1, :] = peak
    for at in range(sums.shape[0]):
        out[at + 1 : at + 2, :] = jnp.sum(sums[at] * scale, axis=0, keepdims=True)


def first_stats(order, block, cent, rows, out, cent_rel, top, sums):
    for at, mask in enumerate(order):
        owner = jnp.bitwise_xor(lax.axis_index("vec"), mask)
        cent_rel[at * block : (at + 1) * block, :] = cent[pl.ds(pl.multiple_of(owner * block, block), block), :]

    def load():
        for rows_k in cut(cent_rel.shape[0]):
            lhs, square = factor(cent_rel[rows_k, :])
            for cols in cut(rows.shape[0]):
                yield dot_nt(lhs, rows[cols, :]) - square, cols, None

    online(out, top, sums, load())


def first_sums(half, block, parts, stats, cent, rows, out, lse, expo_b):
    peak, total, _ = merge(stats)
    lse[...] = peak + jnp.log(total)
    size = out.shape[0] * block
    per = max(1, min(STEP, size) // block)
    for at in range(0, out.shape[0], per):
        start = half * size + at * block
        lhs, square = factor(cent[start : start + per * block, :])
        count = jnp.zeros((per * block, 128), F32)
        for cols in cut(rows.shape[0]):
            expo = jnp.exp(dot_nt(lhs, rows[cols, :]) - square - lse[:, cols])
            count = count + lanes(expo)
            expo_b[:, cols] = expo.astype(BF16)
        mass = dot(expo_b[...], rows[...])
        for r in range(per):
            part = slice(r * block, (r + 1) * block)
            out[at + r, 0:block, :] = mass[part, :]
            out[at + r, block:, :] = jnp.zeros((out.shape[1] - block, out.shape[2]), F32)
            out[at + r, block : block + 1, 0:block] = jnp.sum(count[part, :].T, axis=0, keepdims=True)


def second_stats(moved, rows, cot, out, top, sums):
    def load():
        for ref, rows_k, _ in tiles(moved):
            block = ref[rows_k, :]
            lhs, square = factor(block)
            for cols in cut(rows.shape[0]):
                yield dot_nt(lhs, rows[cols, :]) - square, cols, dot_nt(block, cot[cols, :])

    online(out, top, sums, load())


def second_rows(stats, lse, dots, scale):
    peak, total, weights = merge(stats)
    lse[...] = peak + jnp.log(total)
    dots[...] = sum(w * part[2:3, :] for w, part in zip(weights, stats)) / total * scale


def put_owners(out, start, value):
    block = out.shape[1]
    per = value.shape[0] // block
    out[start // block : start // block + per] = value.reshape(per, block, value.shape[1]).astype(out.dtype)


def second_sums(stats, moved, rows, cot, outs, lse, dots, expo_b, edge_b):
    second_rows(stats, lse, dots, 2.0 * rows.shape[1] ** (-0.5))
    cols_all = cut(rows.shape[0])
    ready = None
    for at, (ref, rows_k, _) in enumerate([*tiles(moved), (None, None, None)]):
        slot, last = at % 2, 1 - at % 2
        if ref is not None:
            block = ref[rows_k, :]
            lhs, square = factor(block)
            edges = jnp.zeros((block.shape[0], 128), F32)
        for step, cols in enumerate(cols_all):
            if ref is not None:
                expo = jnp.exp(dot_nt(lhs, rows[cols, :]) - square - lse[:, cols])
                expo_b[slot, :, cols] = expo.astype(BF16)
                edge = expo * (dot_nt(lhs, cot[cols, :]) - dots[:, cols])
                edges = edges + lanes(edge)
                edge_b[slot, :, cols] = edge.astype(BF16)
            if ready is not None and step == 0:
                total = dot(expo_b[last], cot[...])
            if ready is not None and step == len(cols_all) // 2:
                total = total + dot(edge_b[last], rows[...])
        if ready is not None:
            out, start, old, old_edges = ready
            put_owners(out, start, total - jnp.sum(old_edges, axis=1, keepdims=True) * old.astype(F32))
        if ref is not None:
            ready = outs[0] if ref is moved[0] else outs[1], rows_k.start, block, edges


def second_part(begin, stats, moved, rows, cot, out, lse, dots, edge_b):
    second_rows(stats, lse, dots, 2.0 * rows.shape[1] ** (-0.5))
    for ref, rows_k, whole in tiles(moved):
        lhs, square = factor(ref[rows_k, :])
        for local in cut(out.shape[1]):
            cols = slice(begin + local.start, begin + local.stop)
            expo = jnp.exp(dot_nt(lhs, rows[cols, :]) - square - lse[:, cols])
            edge = expo * (dot_nt(lhs, cot[cols, :]) - dots[:, cols])
            edge_b[whole, local] = edge.astype(BF16)
    for local in cut(out.shape[1]):
        out[:, local] = sum(
            dot(ref[...].T, edge_b[at : at + ref.shape[0], local])
            for ref, at in zip(moved, (0, moved[0].shape[0]))
        )


def put_chunks(index, total, outs):
    size = total.shape[0] // len(outs)
    for r, out in enumerate(outs):
        at = jnp.bitwise_xor(index, r) * size
        out[...] = total[pl.ds(pl.multiple_of(at, size), size), :].astype(out.dtype)


def first_rows(masks, cent, rows, lse, outs, expo_b):
    cent_t = cent[...].T
    for mask, out in zip(masks, outs):
        size = out.shape[0]
        own = pl.ds(pl.multiple_of(jnp.bitwise_xor(lax.axis_index("cent"), mask) * size, size), size)
        chunk, shift = rows[own, :], lse[:, own]
        for whole in cut(cent.shape[0]):
            lhs, square = factor(cent[whole, :])
            expo_b[whole, :] = jnp.exp(dot_nt(lhs, chunk) - square - shift).astype(BF16)
        out[...] = dot(cent_t, expo_b[...]).T.astype(out.dtype)


def third_terms(cent, moved, mean_cot, rows, lse, cols_all):
    scale = 2.0 * rows.shape[1] ** (-0.5)
    for (mean_ref, rows_k, whole), (moved_ref, _, _) in zip(tiles(mean_cot), tiles(moved)):
        lhs, square = factor(cent[whole, :])
        mean = mean_ref[rows_k, :].astype(F32) * scale
        count_cot = -jnp.sum(mean * moved_ref[rows_k, :].astype(F32), axis=1, keepdims=True)
        mean = mean.astype(BF16)
        for cols in cols_all:
            expo = jnp.exp(dot_nt(lhs, rows[cols, :]) - square - lse[:, cols])
            yield whole, cols, expo, dot_nt(mean, rows[cols, :]) + count_cot


def third_rows(own, cent, moved, mean_cot, rows, lse, parts, stats, outs, lhs_s, mean_s, expo_b, edge_b, expo_f, dfirst_f, total):
    scale = 2.0 * rows.shape[1] ** (-0.5)
    cent_t = cent[...].T
    halves = [ref[...].T for ref in mean_cot]
    size = halves[0].shape[1]
    terms = []
    for (mean_ref, rows_k, whole), (moved_ref, _, _) in zip(tiles(mean_cot), tiles(moved)):
        lhs, square = factor(cent[whole, :])
        mean = mean_ref[rows_k, :].astype(F32) * scale
        lhs_s[whole, :] = lhs
        mean_s[whole, :] = mean.astype(BF16)
        terms.append((whole, square, -jnp.sum(mean * moved_ref[rows_k, :].astype(F32), axis=1, keepdims=True)))
    cols_all = cut(rows.shape[0])
    ready = None
    for at, cols in enumerate([*cols_all, None]):
        slot, last = at % 2, 1 - at % 2
        if cols is not None:
            dots = jnp.zeros((8, cols.stop - cols.start), F32)
        if ready is not None:
            done, mean = ready
            part = parts[done.start // parts[0].shape[1]]
            begin = done.start % parts[0].shape[1]
            value = part[:, begin : begin + done.stop - done.start]
        for whole, square, count_cot in terms:
            if cols is not None:
                expo = jnp.exp(dot_nt(lhs_s[whole, :], rows[cols, :]) - square - lse[:, cols])
                dfirst = dot_nt(mean_s[whole, :], rows[cols, :]) + count_cot
                expo_f[slot, whole, :] = expo
                dfirst_f[slot, whole, :] = dfirst
                expo_b[slot, whole, :] = expo.astype(BF16)
                dots = dots + jnp.sum((expo * dfirst).reshape(expo.shape[0] // 8, 8, expo.shape[1]), axis=0)
            if ready is not None:
                edge = expo_f[last, whole, :] * (dfirst_f[last, whole, :] - mean)
                edge_b[whole, :] = edge.astype(BF16)
                if whole.stop % size == 0:
                    half = slice(whole.stop - size, whole.stop)
                    value = value + dot(cent_t[:, half], edge_b[half, :])
                    value = value + dot(halves[half.start // size], expo_b[last, half, :])
        if ready is not None:
            total[done, :] = value.T
        if cols is not None:
            dots = jnp.sum(dots, axis=0, keepdims=True)
            weight = own[1:2, cols] * jnp.exp(own[0:1, cols] - lse[:, cols])
            mean = jnp.where(weight > 0.0, dots / jnp.where(weight > 0.0, weight, 1.0), 0.0)
            stats[0:1, cols] = dots
            stats[1:2, cols] = mean
            ready = cols, mean
    put_chunks(lax.axis_index("cent"), total, outs)


def third_sums(stats, cent, moved, mean_cot, rows, lse, outs, dots, edge_b):
    dots[...] = sum(ref[0:1, :] for ref in stats)
    edges = jnp.zeros((edge_b.shape[0], 128), F32)
    for whole, cols, expo, dfirst in third_terms(cent, moved, mean_cot, rows, lse, cut(rows.shape[0])):
        edge = expo * (dfirst - dots[:, cols])
        edges = edges + lanes(edge)
        edge_b[:, cols] = edge.astype(BF16)
        if cols.stop == rows.shape[0]:
            value = dot(edge_b[...], rows[...])
            value = value - jnp.sum(edges, axis=1, keepdims=True) * cent[whole, :].astype(F32)
            which, start = divmod(whole.start, cent.shape[0] // 2)
            put_owners(outs[which], start, value)
            edges = jnp.zeros(edges.shape, F32)


def place_blocks(order, axis, parts, out):
    at = 0
    for part in parts:
        block = out.shape[0] // len(order)
        for start in range(0, part.shape[0], block):
            owner = jnp.bitwise_xor(lax.axis_index(axis), order[at])
            out[pl.ds(pl.multiple_of(owner * block, block), block), :] = part[start : start + block, :].astype(out.dtype)
            at += 1


def swap(x, axis, n, mask):
    return lax.ppermute(x, axis, [(i, i ^ mask) for i in range(n)])


def make_local(nv, nc):
    nq = nv // 2
    order = [2 * r + a for a in range(2) for r in range(nq)]

    def local(weights, centroids, cotangent):
        V, D = weights.shape
        K = centroids.shape[0]
        block, half = K // nv, K // 2
        step, wide = min(STEP, half), min(STEP, V)
        unit = 2 * K * V * D
        row = pltpu.VMEM((1, V), F32)
        strip = pltpu.VMEM((step, V), BF16)

        def spread(x):
            return [x] + [swap(x, "cent", nc, r) for r in range(1, nc)]

        def add_core(keep, send):
            return keep.astype(F32) + swap(send, "vec", nv, 1).astype(F32)

        def collect(chunks, beside):
            parts = [swap(chunks[r].astype(BF16), "vec", nv, 2 * r) for r in range(1, nq)]
            parts, beside = lax.optimization_barrier((parts, beside))
            return sum(part.astype(F32) for part in [chunks[0]] + parts), beside

        def share(x, beside):
            parts = [swap(x, "vec", nv, 2 * r) for r in range(1, nq)]
            parts, beside = lax.optimization_barrier((parts, beside))
            mine = jnp.concatenate([x] + parts)
            return [mine, swap(mine, "vec", nv, 1)], beside

        def split(fn, *counts):
            def kernel(*refs):
                groups, at = [], 0
                for count in counts:
                    groups.append(refs[at] if count == 0 else list(refs[at : at + count]))
                    at += max(count, 1)
                fn(*groups, *refs[at:])
            return kernel

        stats, cent = call(
            lambda *refs: first_stats(order, block, *refs),
            (shape(2, V), shape(K, D, dtype=BF16)),
            (centroids, weights),
            [pltpu.VMEM((8, V), F32), pltpu.VMEM((1, 8, V), F32)],
            unit,
        )
        first_own = stats
        stats = spread(stats)

        def sums(at):
            return call(
                split(lambda *refs: first_sums(at, block, nc, *refs), nc, 0, 0, 0, 0),
                (shape(nq, block + 16, D), shape(1, V)),
                (*stats, cent, weights),
                [strip],
                unit,
            )

        def rows_shape(kind):
            return [shape(V // nc, D, dtype=kind)] * nc

        def scatter(chunks):
            return [chunks[0]] + [swap(chunks[r], "cent", nc, r) for r in range(1, nc)]

        send, _ = sums(1)
        keep, lse = sums(0)

        def first_part(masks):
            return call(
                split(lambda *refs: first_rows(masks, *refs), 0, 0, 0, len(masks)),
                [shape(V // nc, D, dtype=BF16)] * len(masks),
                (cent, weights, lse),
                [pltpu.VMEM((K, V // nc), BF16)],
                unit,
            )

        first_cent = first_part(list(range(nc // 2)))
        chunks = add_core(keep, send)
        count = chunks[:, block]
        near = lax.reduce_precision(count, 8, 7)
        pair = jnp.stack([near, count - near], axis=1)
        chunks = jnp.concatenate([chunks[:, :block], pair, chunks[:, block + 2 :]], axis=1)
        chunk, first_cent = collect(chunks, first_cent)
        denom = chunk[block, :block] + chunk[block + 1, :block] + 1e-6
        moved, more = share(
            (chunk[:block] / denom[:, None]).astype(BF16), first_part(list(range(nc // 2, nc)))
        )
        first_cent = scatter([*first_cent, *more])

        far = nc // 2
        stats = call(
            split(second_stats, 2),
            shape(3, V),
            (*moved, weights, cotangent),
            [pltpu.VMEM((8, V), F32), pltpu.VMEM((2, 8, V), F32)],
        )
        stats, first_cent[1:far] = lax.optimization_barrier((stats, first_cent[1:far]))
        stats = spread(stats)
        moved_cot = call(
            split(second_sums, nc, 2, 0, 0, 2),
            [shape(nq, block, D, dtype=BF16)] * 2,
            (*stats, *moved, weights, cotangent),
            [row, row] + [pltpu.VMEM((2, step, V), BF16)] * 2,
            4 * unit,
        )
        span = V // 2

        def part(begin):
            return call(
                split(lambda *refs: second_part(begin, *refs), nc, 2),
                shape(D, span),
                (*stats, *moved, weights, cotangent),
                [row, row, pltpu.VMEM((K, span), BF16)],
                unit,
            )

        moved_cot, part_low = collect(add_core(*moved_cot), part(0))
        mean_cot, (part_high, first_cent[far:-1]) = share(
            (moved_cot / denom[:, None]).astype(BF16), (part(span), first_cent[far:-1])
        )

        stats, *grad_rows = call(
            split(third_rows, 0, 0, 2, 2, 0, 0, 2, 0, nc),
            [shape(2, V)] + rows_shape(BF16),
            (first_own, cent, *moved, *mean_cot, weights, lse, part_low, part_high),
            [pltpu.VMEM((K, D), BF16)] * 2
            + [pltpu.VMEM((2, K, wide), BF16), pltpu.VMEM((K, wide), BF16)]
            + [pltpu.VMEM((2, K, wide), F32)] * 2
            + [pltpu.VMEM((V, D), F32)],
            4 * unit,
            44,
        )
        stats, first_cent[-1] = lax.optimization_barrier((stats, first_cent[-1]))
        stats = spread(stats)
        grad_rows = scatter(grad_rows)
        start_cot = call(
            split(third_sums, nc, 0, 2, 2, 0, 0, 2),
            [shape(nq, block, D, dtype=BF16)] * 2,
            (*stats, cent, *moved, *mean_cot, weights, lse),
            [row, strip],
            2 * unit,
        )
        start_cot, grad_rows = lax.optimization_barrier((start_cot, grad_rows))
        size = V // nc
        mine = lax.axis_index("cent") * size
        own = [lax.dynamic_slice(x, (0, mine), (2, size)) for x in stats]
        dots = sum(x[0] for x in own)
        rows = sum(x.astype(F32) for x in grad_rows)
        rows = rows - sum((dots - x[1])[:, None] * f.astype(F32) for x, f in zip(own, first_cent))
        rows = spread(rows.astype(BF16))
        start_cot, _ = collect(add_core(*start_cot), ())
        start_cot, rows = share(start_cot.astype(BF16), rows)
        start_cot = call(
            split(lambda *refs: place_blocks(order, "vec", *refs), 2),
            shape(K, D),
            start_cot,
        )
        grad_rows = jnp.zeros((V, D), BF16)
        for r in range(nc):
            at = jnp.bitwise_xor(lax.axis_index("cent"), r) * size
            grad_rows = lax.dynamic_update_slice(grad_rows, rows[r], (at, 0))
        return grad_rows, start_cot

    return local


def solution(mesh):
    return jax.shard_map(
        make_local(mesh.shape["vec"], mesh.shape["cent"]),
        mesh=mesh,
        in_specs=(P("vec", None), P("cent", None), P("vec", None)),
        out_specs=(P("vec", None), P("cent", None)),
        check_vma=False,
    )
```

```python
import jax
import jax.numpy as jnp
from jax import lax
from jax.experimental import pallas as pl
from jax.experimental.pallas import tpu as pltpu
from jax.sharding import PartitionSpec as P

F32 = jnp.float32
BF16 = jnp.bfloat16
STEP = 512


def vmem():
    return pl.BlockSpec(memory_space=pltpu.VMEM)


def call(kernel, outs, args, scratch=(), flops=0, mib=24):
    return pl.pallas_call(
        kernel,
        in_specs=[vmem()] * len(args),
        out_specs=jax.tree.map(lambda _: vmem(), outs),
        out_shape=outs,
        scratch_shapes=list(scratch),
        cost_estimate=pl.CostEstimate(flops=flops, bytes_accessed=2**22, transcendentals=0),
        compiler_params=pltpu.CompilerParams(vmem_limit_bytes=mib * 2**20),
    )(*args)


def shape(*dims, dtype=F32):
    return jax.ShapeDtypeStruct(dims, dtype)


def dot_nt(a, b):
    return lax.dot_general(a, b, (((1,), (1,)), ((), ())), preferred_element_type=F32)


def dot(a, b):
    return jnp.dot(a, b, preferred_element_type=F32)


def cut(total, step=STEP):
    step = min(step, total)
    return [slice(at, at + step) for at in range(0, total, step)]


def tiles(refs):
    start = 0
    for ref in refs:
        for rows in cut(ref.shape[0]):
            yield ref, rows, slice(start + rows.start, start + rows.stop)
        start += ref.shape[0]


def factor(block):
    scale = block.shape[1] ** (-0.5)
    block_f = block.astype(F32)
    square = jnp.sum(jnp.square(block_f), axis=1, keepdims=True) * scale
    return (block_f * (2.0 * scale)).astype(BF16), square


def lanes(x):
    total = x[:, 0:128]
    for at in range(128, x.shape[1], 128):
        total = total + x[:, at : at + 128]
    return total


def merge(stats):
    top = stats[0][0:1, :]
    for part in stats[1:]:
        top = jnp.maximum(top, part[0:1, :])
    weights = [jnp.exp(part[0:1, :] - top) for part in stats]
    total = sum(w * part[1:2, :] for w, part in zip(weights, stats))
    return top, total, weights


def online(out, top, sums, load):
    top[...] = jnp.full(top.shape, -jnp.inf, F32)
    sums[...] = jnp.zeros(sums.shape, F32)
    for score, cols, weight in load:
        score = score.reshape(score.shape[0] // 8, 8, score.shape[1])
        old = top[:, cols]
        new = jnp.maximum(old, jnp.max(score, axis=0))
        drop = jnp.exp(old - new)
        expo = jnp.exp(score - new[None])
        sums[0, :, cols] = sums[0, :, cols] * drop + jnp.sum(expo, axis=0)
        if weight is not None:
            expo = expo * weight.reshape(expo.shape)
            sums[1, :, cols] = sums[1, :, cols] * drop + jnp.sum(expo, axis=0)
        top[:, cols] = new
    peak = jnp.max(top[...], axis=0, keepdims=True)
    scale = jnp.exp(top[...] - peak)
    out[0:1, :] = peak
    for at in range(sums.shape[0]):
        out[at + 1 : at + 2, :] = jnp.sum(sums[at] * scale, axis=0, keepdims=True)


def first_stats(order, block, cent, rows, out, cent_rel, top, sums):
    for at, mask in enumerate(order):
        owner = jnp.bitwise_xor(lax.axis_index("vec"), mask)
        cent_rel[at * block : (at + 1) * block, :] = cent[pl.ds(pl.multiple_of(owner * block, block), block), :]

    def load():
        for rows_k in cut(cent_rel.shape[0]):
            lhs, square = factor(cent_rel[rows_k, :])
            for cols in cut(rows.shape[0]):
                yield dot_nt(lhs, rows[cols, :]) - square, cols, None

    online(out, top, sums, load())


def first_sums(half, block, parts, stats, cent, rows, out, lse, expo_b):
    peak, total, _ = merge(stats)
    lse[...] = peak + jnp.log(total)
    size = out.shape[0] * block
    per = max(1, min(STEP, size) // block)
    for at in range(0, out.shape[0], per):
        start = half * size + at * block
        lhs, square = factor(cent[start : start + per * block, :])
        count = jnp.zeros((per * block, 128), F32)
        for cols in cut(rows.shape[0]):
            expo = jnp.exp(dot_nt(lhs, rows[cols, :]) - square - lse[:, cols])
            count = count + lanes(expo)
            expo_b[:, cols] = expo.astype(BF16)
        mass = dot(expo_b[...], rows[...])
        for r in range(per):
            part = slice(r * block, (r + 1) * block)
            out[at + r, 0:block, :] = mass[part, :]
            out[at + r, block:, :] = jnp.zeros((out.shape[1] - block, out.shape[2]), F32)
            out[at + r, block : block + 1, 0:block] = jnp.sum(count[part, :].T, axis=0, keepdims=True)


def second_stats(moved, rows, cot, out, top, sums):
    def load():
        for ref, rows_k, _ in tiles(moved):
            block = ref[rows_k, :]
            lhs, square = factor(block)
            for cols in cut(rows.shape[0]):
                yield dot_nt(lhs, rows[cols, :]) - square, cols, dot_nt(block, cot[cols, :])

    online(out, top, sums, load())


def second_rows(stats, lse, dots, scale):
    peak, total, weights = merge(stats)
    lse[...] = peak + jnp.log(total)
    dots[...] = sum(w * part[2:3, :] for w, part in zip(weights, stats)) / total * scale


def put_owners(out, start, value):
    block = out.shape[1]
    per = value.shape[0] // block
    out[start // block : start // block + per] = value.reshape(per, block, value.shape[1]).astype(out.dtype)


def second_sums(stats, moved, rows, cot, outs, lse, dots, expo_b, edge_b):
    second_rows(stats, lse, dots, 2.0 * rows.shape[1] ** (-0.5))
    cols_all = cut(rows.shape[0])
    ready = None
    for at, (ref, rows_k, _) in enumerate([*tiles(moved), (None, None, None)]):
        slot, last = at % 2, 1 - at % 2
        if ref is not None:
            block = ref[rows_k, :]
            lhs, square = factor(block)
            edges = jnp.zeros((block.shape[0], 128), F32)
        for step, cols in enumerate(cols_all):
            if ref is not None:
                expo = jnp.exp(dot_nt(lhs, rows[cols, :]) - square - lse[:, cols])
                expo_b[slot, :, cols] = expo.astype(BF16)
                edge = expo * (dot_nt(lhs, cot[cols, :]) - dots[:, cols])
                edges = edges + lanes(edge)
                edge_b[slot, :, cols] = edge.astype(BF16)
            if ready is not None and step == 0:
                total = dot(expo_b[last], cot[...])
            if ready is not None and step == len(cols_all) // 2:
                total = total + dot(edge_b[last], rows[...])
        if ready is not None:
            out, start, old, old_edges = ready
            put_owners(out, start, total - jnp.sum(old_edges, axis=1, keepdims=True) * old.astype(F32))
        if ref is not None:
            ready = outs[0] if ref is moved[0] else outs[1], rows_k.start, block, edges


def second_part(begin, stats, moved, rows, cot, out, lse, dots, edge_b):
    second_rows(stats, lse, dots, 2.0 * rows.shape[1] ** (-0.5))
    for ref, rows_k, whole in tiles(moved):
        lhs, square = factor(ref[rows_k, :])
        for local in cut(out.shape[1]):
            cols = slice(begin + local.start, begin + local.stop)
            expo = jnp.exp(dot_nt(lhs, rows[cols, :]) - square - lse[:, cols])
            edge = expo * (dot_nt(lhs, cot[cols, :]) - dots[:, cols])
            edge_b[whole, local] = edge.astype(BF16)
    for local in cut(out.shape[1]):
        out[:, local] = sum(
            dot(ref[...].T, edge_b[at : at + ref.shape[0], local])
            for ref, at in zip(moved, (0, moved[0].shape[0]))
        )


def put_chunks(index, total, outs):
    size = total.shape[0] // len(outs)
    for r, out in enumerate(outs):
        at = jnp.bitwise_xor(index, r) * size
        out[...] = total[pl.ds(pl.multiple_of(at, size), size), :].astype(out.dtype)


def first_rows(masks, cent, rows, lse, outs, expo_b):
    cent_t = cent[...].T
    for mask, out in zip(masks, outs):
        size = out.shape[0]
        own = pl.ds(pl.multiple_of(jnp.bitwise_xor(lax.axis_index("cent"), mask) * size, size), size)
        chunk, shift = rows[own, :], lse[:, own]
        for whole in cut(cent.shape[0]):
            lhs, square = factor(cent[whole, :])
            expo_b[whole, :] = jnp.exp(dot_nt(lhs, chunk) - square - shift).astype(BF16)
        out[...] = dot(cent_t, expo_b[...]).T.astype(out.dtype)


def third_terms(cent, moved, mean_cot, rows, lse, cols_all):
    scale = 2.0 * rows.shape[1] ** (-0.5)
    for (mean_ref, rows_k, whole), (moved_ref, _, _) in zip(tiles(mean_cot), tiles(moved)):
        lhs, square = factor(cent[whole, :])
        mean = mean_ref[rows_k, :].astype(F32) * scale
        count_cot = -jnp.sum(mean * moved_ref[rows_k, :].astype(F32), axis=1, keepdims=True)
        mean = mean.astype(BF16)
        for cols in cols_all:
            expo = jnp.exp(dot_nt(lhs, rows[cols, :]) - square - lse[:, cols])
            yield whole, cols, expo, dot_nt(mean, rows[cols, :]) + count_cot


def third_rows(own, cent, moved, mean_cot, rows, lse, parts, stats, outs, lhs_s, mean_s, expo_b, edge_b, expo_f, dfirst_f, total):
    scale = 2.0 * rows.shape[1] ** (-0.5)
    cent_t = cent[...].T
    halves = [ref[...].T for ref in mean_cot]
    size = halves[0].shape[1]
    terms = []
    for (mean_ref, rows_k, whole), (moved_ref, _, _) in zip(tiles(mean_cot), tiles(moved)):
        lhs, square = factor(cent[whole, :])
        mean = mean_ref[rows_k, :].astype(F32) * scale
        lhs_s[whole, :] = lhs
        mean_s[whole, :] = mean.astype(BF16)
        terms.append((whole, square, -jnp.sum(mean * moved_ref[rows_k, :].astype(F32), axis=1, keepdims=True)))
    cols_all = cut(rows.shape[0])
    ready = None
    for at, cols in enumerate([*cols_all, None]):
        slot, last = at % 2, 1 - at % 2
        if cols is not None:
            dots = jnp.zeros((8, cols.stop - cols.start), F32)
        if ready is not None:
            done, mean = ready
            part = parts[done.start // parts[0].shape[1]]
            begin = done.start % parts[0].shape[1]
            value = part[:, begin : begin + done.stop - done.start]
        for whole, square, count_cot in terms:
            if cols is not None:
                expo = jnp.exp(dot_nt(lhs_s[whole, :], rows[cols, :]) - square - lse[:, cols])
                dfirst = dot_nt(mean_s[whole, :], rows[cols, :]) + count_cot
                expo_f[slot, whole, :] = expo
                dfirst_f[slot, whole, :] = dfirst
                expo_b[slot, whole, :] = expo.astype(BF16)
                dots = dots + jnp.sum((expo * dfirst).reshape(expo.shape[0] // 8, 8, expo.shape[1]), axis=0)
            if ready is not None:
                edge = expo_f[last, whole, :] * (dfirst_f[last, whole, :] - mean)
                edge_b[whole, :] = edge.astype(BF16)
                if whole.stop % size == 0:
                    half = slice(whole.stop - size, whole.stop)
                    value = value + dot(cent_t[:, half], edge_b[half, :])
                    value = value + dot(halves[half.start // size], expo_b[last, half, :])
        if ready is not None:
            total[done, :] = value.T
        if cols is not None:
            dots = jnp.sum(dots, axis=0, keepdims=True)
            weight = own[1:2, cols] * jnp.exp(own[0:1, cols] - lse[:, cols])
            mean = jnp.where(weight > 0.0, dots / jnp.where(weight > 0.0, weight, 1.0), 0.0)
            stats[0:1, cols] = dots
            stats[1:2, cols] = mean
            ready = cols, mean
    put_chunks(lax.axis_index("cent"), total, outs)


def third_sums(stats, cent, moved, mean_cot, rows, lse, outs, dots, edge_b):
    dots[...] = sum(ref[0:1, :] for ref in stats)
    edges = jnp.zeros((edge_b.shape[0], 128), F32)
    for whole, cols, expo, dfirst in third_terms(cent, moved, mean_cot, rows, lse, cut(rows.shape[0])):
        edge = expo * (dfirst - dots[:, cols])
        edges = edges + lanes(edge)
        edge_b[:, cols] = edge.astype(BF16)
        if cols.stop == rows.shape[0]:
            value = dot(edge_b[...], rows[...])
            value = value - jnp.sum(edges, axis=1, keepdims=True) * cent[whole, :].astype(F32)
            which, start = divmod(whole.start, cent.shape[0] // 2)
            put_owners(outs[which], start, value)
            edges = jnp.zeros(edges.shape, F32)


def place_blocks(order, axis, parts, out):
    at = 0
    for part in parts:
        block = out.shape[0] // len(order)
        for start in range(0, part.shape[0], block):
            owner = jnp.bitwise_xor(lax.axis_index(axis), order[at])
            out[pl.ds(pl.multiple_of(owner * block, block), block), :] = part[start : start + block, :].astype(out.dtype)
            at += 1


def swap(x, axis, n, mask):
    return lax.ppermute(x, axis, [(i, i ^ mask) for i in range(n)])


def make_local(nv, nc):
    nq = nv // 2
    order = [2 * r + a for a in range(2) for r in range(nq)]

    def local(weights, centroids, cotangent):
        V, D = weights.shape
        K = centroids.shape[0]
        block, half = K // nv, K // 2
        step, wide = min(STEP, half), min(STEP, V)
        unit = 2 * K * V * D
        row = pltpu.VMEM((1, V), F32)
        strip = pltpu.VMEM((step, V), BF16)

        def spread(x):
            return [x] + [swap(x, "cent", nc, r) for r in range(1, nc)]

        def add_core(keep, send):
            return keep.astype(F32) + swap(send, "vec", nv, 1).astype(F32)

        def collect(chunks, beside):
            parts = [swap(chunks[r].astype(BF16), "vec", nv, 2 * r) for r in range(1, nq)]
            parts, beside = lax.optimization_barrier((parts, beside))
            return sum(part.astype(F32) for part in [chunks[0]] + parts), beside

        def share(x, beside):
            parts = [swap(x, "vec", nv, 2 * r) for r in range(1, nq)]
            parts, beside = lax.optimization_barrier((parts, beside))
            mine = jnp.concatenate([x] + parts)
            return [mine, swap(mine, "vec", nv, 1)], beside

        def split(fn, *counts):
            def kernel(*refs):
                groups, at = [], 0
                for count in counts:
                    groups.append(refs[at] if count == 0 else list(refs[at : at + count]))
                    at += max(count, 1)
                fn(*groups, *refs[at:])
            return kernel

        stats, cent = call(
            lambda *refs: first_stats(order, block, *refs),
            (shape(2, V), shape(K, D, dtype=BF16)),
            (centroids, weights),
            [pltpu.VMEM((8, V), F32), pltpu.VMEM((1, 8, V), F32)],
            unit,
        )
        first_own = stats
        stats = spread(stats)

        def sums(at):
            return call(
                split(lambda *refs: first_sums(at, block, nc, *refs), nc, 0, 0, 0, 0),
                (shape(nq, block + 16, D), shape(1, V)),
                (*stats, cent, weights),
                [strip],
                unit,
            )

        def rows_shape(kind):
            return [shape(V // nc, D, dtype=kind)] * nc

        def scatter(chunks):
            return [chunks[0]] + [swap(chunks[r], "cent", nc, r) for r in range(1, nc)]

        send, _ = sums(1)
        keep, lse = sums(0)

        def first_part(masks):
            return call(
                split(lambda *refs: first_rows(masks, *refs), 0, 0, 0, len(masks)),
                [shape(V // nc, D, dtype=BF16)] * len(masks),
                (cent, weights, lse),
                [pltpu.VMEM((K, V // nc), BF16)],
                unit,
            )

        first_cent = first_part(list(range(nc // 2)))
        chunks = add_core(keep, send)
        count = chunks[:, block]
        near = lax.reduce_precision(count, 8, 7)
        pair = jnp.stack([near, count - near], axis=1)
        chunks = jnp.concatenate([chunks[:, :block], pair, chunks[:, block + 2 :]], axis=1)
        chunk, first_cent = collect(chunks, first_cent)
        denom = chunk[block, :block] + chunk[block + 1, :block] + 1e-6
        moved, more = share(
            (chunk[:block] / denom[:, None]).astype(BF16), first_part(list(range(nc // 2, nc)))
        )
        first_cent = scatter([*first_cent, *more])

        far = nc // 2
        stats = call(
            split(second_stats, 2),
            shape(3, V),
            (*moved, weights, cotangent),
            [pltpu.VMEM((8, V), F32), pltpu.VMEM((2, 8, V), F32)],
        )
        stats, first_cent[1:far] = lax.optimization_barrier((stats, first_cent[1:far]))
        stats = spread(stats)
        moved_cot = call(
            split(second_sums, nc, 2, 0, 0, 2),
            [shape(nq, block, D, dtype=BF16)] * 2,
            (*stats, *moved, weights, cotangent),
            [row, row] + [pltpu.VMEM((2, step, V), BF16)] * 2,
            4 * unit,
        )
        span = V // 2

        def part(begin):
            return call(
                split(lambda *refs: second_part(begin, *refs), nc, 2),
                shape(D, span),
                (*stats, *moved, weights, cotangent),
                [row, row, pltpu.VMEM((K, span), BF16)],
                unit,
            )

        moved_cot, part_low = collect(add_core(*moved_cot), part(0))
        mean_cot, (part_high, first_cent[far:-1]) = share(
            (moved_cot / denom[:, None]).astype(BF16), (part(span), first_cent[far:-1])
        )

        stats, *grad_rows = call(
            split(third_rows, 0, 0, 2, 2, 0, 0, 2, 0, nc),
            [shape(2, V)] + rows_shape(BF16),
            (first_own, cent, *moved, *mean_cot, weights, lse, part_low, part_high),
            [pltpu.VMEM((K, D), BF16)] * 2
            + [pltpu.VMEM((2, K, wide), BF16), pltpu.VMEM((K, wide), BF16)]
            + [pltpu.VMEM((2, K, wide), F32)] * 2
            + [pltpu.VMEM((V, D), F32)],
            4 * unit,
            36,
        )
        stats, first_cent[-1] = lax.optimization_barrier((stats, first_cent[-1]))
        stats = spread(stats)
        grad_rows = scatter(grad_rows)
        start_cot = call(
            split(third_sums, nc, 0, 2, 2, 0, 0, 2),
            [shape(nq, block, D, dtype=BF16)] * 2,
            (*stats, cent, *moved, *mean_cot, weights, lse),
            [row, strip],
            2 * unit,
        )
        start_cot, grad_rows = lax.optimization_barrier((start_cot, grad_rows))
        size = V // nc
        mine = lax.axis_index("cent") * size
        own = [lax.dynamic_slice(x, (0, mine), (2, size)) for x in stats]
        dots = sum(x[0] for x in own)
        rows = sum(x.astype(F32) for x in grad_rows)
        rows = rows - sum((dots - x[1])[:, None] * f.astype(F32) for x, f in zip(own, first_cent))
        rows = spread(rows.astype(BF16))
        start_cot, _ = collect(add_core(*start_cot), ())
        start_cot, rows = share(start_cot.astype(BF16), rows)
        start_cot = call(
            split(lambda *refs: place_blocks(order, "vec", *refs), 2),
            shape(K, D),
            start_cot,
        )
        grad_rows = jnp.zeros((V, D), BF16)
        for r in range(nc):
            at = jnp.bitwise_xor(lax.axis_index("cent"), r) * size
            grad_rows = lax.dynamic_update_slice(grad_rows, rows[r], (at, 0))
        return grad_rows, start_cot

    return local


def solution(mesh):
    return jax.shard_map(
        make_local(mesh.shape["vec"], mesh.shape["cent"]),
        mesh=mesh,
        in_specs=(P("vec", None), P("cent", None), P("vec", None)),
        out_specs=(P("vec", None), P("cent", None)),
        check_vma=False,
    )
```
